32 devices in a mesh: batch: 4 (over y, x), tm: 8 (over z, core).
Axes of the slice: x: 2, y: 2, z: 4, core: 2. Of those that a mesh axis runs over, the one named last changes fastest.
Arguments:
- tokens: bfloat16 [16, 2048, 512], P('batch', 'tm'), may hold values from -80 to 80
- starts: int32 [16, 16], P('batch'), may hold values from 0 to 2047, as said below
- lengths: int32 [16], P('batch'), may hold values from 1024 to 2048
- cotangent: bfloat16 [16, 2048, 512], P('batch', 'tm'), may hold values from -6 to 6
- norm_gain: float32 [2, 512], replicated, may hold values from 0.5 to 1.5
- norm_shift: float32 [2, 512], replicated, may hold values from -1.75 to 1.75
- b_proj: bfloat16 [2, 512, 768], replicated, may hold values from -0.25 to 0.25
- log_rate: float32 [2, 384], replicated, may hold values from -20 to -3
- rotation: float32 [2, 384], replicated, may hold values from -3.140625 to 3.140625
- c_proj: bfloat16 [2, 768, 512], replicated, may hold values from -0.21875 to 0.21875
- skip_gain: float32 [2, 512], replicated, may hold values from -3 to 3
- w_gate: bfloat16 [2, 512, 512], replicated, may hold values from -0.25 to 0.25
- gate_bias: float32 [2, 512], replicated, may hold values from -3 to 3
- run_mean: float32 [2, 512], replicated, may hold values from -3 to 3
- run_var: float32 [2, 512], replicated, may hold values from 0.5 to 4
Outputs:
- output: bfloat16 [16, 2048, 512], P('batch', 'tm')
- tokens_grad: float32 [16, 2048, 512], P('batch', 'tm')
- grad_norm_gain: float32 [2, 512], replicated
- grad_norm_shift: float32 [2, 512], replicated
- grad_b_proj: float32 [2, 512, 768], replicated
- grad_log_rate: float32 [2, 384], replicated
- grad_rotation: float32 [2, 384], replicated
- grad_c_proj: float32 [2, 768, 512], replicated
- grad_skip_gain: float32 [2, 512], replicated
- grad_w_gate: float32 [2, 512, 512], replicated
- grad_gate_bias: float32 [2, 512], replicated
- new_mean: float32 [2, 512], replicated
- new_var: float32 [2, 512], replicated
The draws below stay inside these ranges and needn't reach their ends.
Inputs may be any that keep to these rules, and one draw needn't show every extreme that they name: starts[i,0] is 0 and starts may repeat; among the 4 rows of each index of batch one row has all its starts below 128 and length 2048.
All inputs are finite; a program needn't handle non-finite values.
Results may differ from the reference program's by a relative error of at most 0.009.
Values sent between devices are 32-bit elements; how exact they have to be, the bound alone decides.
No kernel may reach another device: no remote copies, remote signals or barrier semaphores. Data moves between devices by JAX's collectives and lax.ppermute only.
A program may use at most 192 MiB of HBM per device.

```python
import math
import jax
import jax.numpy as jnp
from jax import lax

H = 512
P_SIZE = 384
TCH = 256
ROWS_DEV = 2
MICRO = 2
NSEG = 16
LEN = 2048
ROWS = 16


def spanning_rows(key):
    group_rows = MICRO * ROWS_DEV
    groups = ROWS // group_rows
    chosen = jax.random.randint(key, (groups,), 0, group_rows)
    row_ids = jnp.arange(ROWS, dtype=jnp.int32)
    return row_ids % group_rows == chosen[row_ids // group_rows]


def draw_starts(key, part):
    spanning = spanning_rows(key)
    key = jax.random.fold_in(key, 11)
    near_key, far_key = jax.random.split(key)
    near = jax.random.randint(near_key, (ROWS, NSEG), 0, TCH // 2)
    far = jax.random.randint(far_key, (ROWS, NSEG), 1, LEN)
    chosen = jnp.where(spanning[:, None], near, far)
    return jnp.concatenate((jnp.zeros((ROWS, 1), jnp.int32), chosen[:, 1:]), axis=1)


def draw_lengths(key, part):
    spanning = spanning_rows(key)
    key = jax.random.fold_in(key, 12)
    drawn = jax.random.randint(key, (ROWS,), LEN // 2, LEN + 1)
    return jnp.where(spanning, LEN, drawn)


def draw_tokens(key, part):
    key = jax.random.fold_in(key, 21)
    noise_key, scale_key, shift_key = jax.random.split(key, 3)
    ramp = 0.5 + 1.5 * jnp.arange(LEN, dtype=jnp.float32) / LEN
    noise = jnp.clip(jax.random.normal(noise_key, (ROWS, LEN, H), jnp.float32), -6.0, 6.0)
    scales = jnp.exp(jax.random.uniform(scale_key, (H,), jnp.float32, math.log(0.5), math.log(5.0)))
    shifts = 0.5 * jnp.clip(jax.random.normal(shift_key, (H,), jnp.float32), -3.0, 3.0)
    return (noise * scales[None, None, :] * ramp[None, :, None] + shifts[None, None, :]).astype(jnp.bfloat16)


def draw_log_rate(key, part):
    key = jax.random.fold_in(key, 31)
    pick_key, slow_key, fast_key = jax.random.split(key, 3)
    picked = jax.random.uniform(pick_key, (2, P_SIZE), jnp.float32)
    slow = jax.random.uniform(slow_key, (2, P_SIZE), jnp.float32, math.log(0.05), math.log(2.0)) - jnp.log(jnp.float32(LEN))
    fast = -jax.random.uniform(fast_key, (2, P_SIZE), jnp.float32, math.log(30.0), math.log(50.0))
    share = 0.5
    return jnp.where(picked < share, slow, fast)


def levels(stream_key, dims, pieces, smallest, top_value):
    loudness = 1.0
    for axis_at, shards_of in pieces:
        draws = jax.random.uniform(jax.random.fold_in(jax.random.fold_in(stream_key, 6), axis_at), (shards_of,), jnp.float32, smallest / len(pieces), top_value / len(pieces))
        loudness = loudness * jnp.repeat(jnp.exp(draws), dims[axis_at] // shards_of).reshape((-1,) + (1,) * (len(dims) - 1 - axis_at))
    return loudness


def bell_draw(stream_key, extent, deviation, reach, cuts=(), held_as=jnp.bfloat16):
    values = jax.random.normal(stream_key, extent, jnp.float32) * deviation
    if len(cuts) > 0:
        values = levels(stream_key, extent, cuts, -0.22, 0.18) * values
    return jnp.clip(values, min=-reach, max=reach).astype(held_as)


def setup_inputs(seed: int = 0) -> dict:
    splits = jax.random.split(jax.random.key(seed), 16)
    tokens = draw_tokens(jax.random.fold_in(splits[15], 71), 0)
    starts = draw_starts(jax.random.fold_in(splits[15], 71), 0)
    lengths = draw_lengths(jax.random.fold_in(splits[15], 71), 0)
    cotangent = bell_draw(splits[3], (ROWS, LEN, H), 1.0, 6.0, ((0, 4), (1, 8)))
    norm_gain = jnp.clip(1.0 + 0.1 * jax.random.normal(splits[4], (2, H), jnp.float32), 0.5, 1.5)
    norm_shift = bell_draw(splits[5], (2, H), 0.3, 1.75, (), jnp.float32)
    b_proj = bell_draw(splits[6], (2, H, 2 * P_SIZE), H ** -0.5, 0.25)
    log_rate = draw_log_rate(jax.random.fold_in(splits[15], 71), 0)
    rotation = jnp.clip(jax.random.uniform(splits[8], (2, P_SIZE), jnp.float32, -3.140625, 3.140625), -3.140625, 3.140625)
    c_proj = bell_draw(splits[9], (2, 2 * P_SIZE, H), (2 * P_SIZE) ** -0.5, 0.21875)
    skip_gain = bell_draw(splits[10], (2, H), 0.5, 3.0, (), jnp.float32)
    w_gate = bell_draw(splits[11], (2, H, H), H ** -0.5, 0.25)
    gate_bias = bell_draw(splits[12], (2, H), 0.5, 3.0, (), jnp.float32)
    run_mean = bell_draw(splits[13], (2, H), 0.5, 3.0, (), jnp.float32)
    run_var = jnp.clip(jnp.exp(jax.random.uniform(splits[14], (2, H), jnp.float32, math.log(0.5), math.log(4.0))), 0.5, 4.0)
    return {"tokens": tokens, "starts": starts, "lengths": lengths, "cotangent": cotangent, "norm_gain": norm_gain, "norm_shift": norm_shift, "b_proj": b_proj, "log_rate": log_rate, "rotation": rotation, "c_proj": c_proj, "skip_gain": skip_gain, "w_gate": w_gate, "gate_bias": gate_bias, "run_mean": run_mean, "run_var": run_var}


epsilon = 1e-05
momentum = 0.1
highest = lax.Precision.HIGHEST

@jax.custom_vjp
def low(v):
    return lax.optimization_barrier(v.astype(jnp.bfloat16)).astype(jnp.float32)

@jax.custom_vjp
def low_back(v):
    return v

def low_keep(v):
    return (low(v), None)

def low_pass(kept, grad):
    return (grad,)

def back_keep(v):
    return (v, None)

def back_low(kept, grad):
    return (low(grad),)
low.defvjp(low_keep, low_pass)
low_back.defvjp(back_keep, back_low)

def complex_times(ar, ai, br, bi):
    return (ar * br - ai * bi, ar * bi + ai * br)

def combine(earlier, later):
    coef_re, coef_im = complex_times(later[0], later[1], earlier[0], earlier[1])
    state_re, state_im = complex_times(later[0], later[1], earlier[2], earlier[3])
    return (coef_re, coef_im, state_re + later[2], state_im + later[3])

def apply_layer(current, valid_mask, keep_mask, params, reverse):
    norm_gain, norm_shift, b_proj, log_rate, rotation, c_proj, skip_gain, w_gate, gate_bias = params
    counted = jnp.sum(valid_mask)
    center = lax.optimization_barrier(jnp.sum(valid_mask * current, axis=(0, 1))) / counted
    spread = lax.optimization_barrier(jnp.sum(valid_mask * (current - center) ** 2, axis=(0, 1))) / counted
    normed = (current - center) * lax.rsqrt(spread + epsilon)
    masked = valid_mask * (normed * norm_gain + norm_shift)
    driven = low_back(jnp.einsum('rth,hs->rts', low(masked), b_proj, precision=highest))
    decay_rate = jnp.exp(log_rate)
    magnitude = jnp.exp(-decay_rate)
    lam_re = magnitude * jnp.cos(rotation)
    lam_im = magnitude * jnp.sin(rotation)
    norm_in = jnp.sqrt(-jnp.expm1(-2.0 * decay_rate))
    scanned = lax.associative_scan(combine, (keep_mask * lam_re, keep_mask * lam_im, norm_in * driven[..., :P_SIZE], norm_in * driven[..., P_SIZE:]), reverse=reverse, axis=1)
    states = jnp.concatenate((scanned[2], scanned[3]), axis=-1)
    mixed_out = low_back(jnp.einsum('rts,sh->rth', low(states), c_proj, precision=highest) + skip_gain * masked)
    active = jax.nn.gelu(mixed_out, approximate=False)
    gate_pre = low_back(jnp.einsum('rth,hk->rtk', low(active), w_gate, precision=highest) + gate_bias)
    return (current + valid_mask * active * jax.nn.sigmoid(gate_pre), center, spread)

def reference(tokens, starts, lengths, cotangent, norm_gain, norm_shift, b_proj, log_rate, rotation, c_proj, skip_gain, w_gate, gate_bias, run_mean, run_var):
    groups = ROWS // (MICRO * ROWS_DEV)
    positions = jnp.arange(LEN, dtype=jnp.int32)
    resets = jnp.any(starts[:, :, None] == positions[None, None, :], axis=1).astype(jnp.float32)
    keep_here = (1.0 - resets)[:, :, None]
    keep_next = jnp.concatenate((keep_here[:, 1:], jnp.zeros((ROWS, 1, 1), jnp.float32)), axis=1)
    valid_mask = (positions[None, :] < lengths[:, None]).astype(jnp.float32)[:, :, None]
    params = tuple((item.astype(jnp.float32) for item in (norm_gain, norm_shift, b_proj, log_rate, rotation, c_proj, skip_gain, w_gate, gate_bias)))

    def select_rows(array, micro_index):
        shaped = array.reshape((groups, MICRO, ROWS_DEV) + array.shape[1:])
        return shaped[:, micro_index].reshape((groups * ROWS_DEV,) + array.shape[1:])

    def forward(inputs, weights):
        results = []
        statistics = []
        lower = tuple((item[0] for item in weights))
        upper = tuple((item[1] for item in weights))
        for micro_index in range(MICRO):
            current = select_rows(inputs, micro_index)
            valid_rows = select_rows(valid_mask, micro_index)
            current, center_a, spread_a = apply_layer(current, valid_rows, select_rows(keep_here, micro_index), lower, False)
            current, center_b, spread_b = apply_layer(current, valid_rows, select_rows(keep_next, micro_index), upper, True)
            results.append(current.reshape((groups, ROWS_DEV, LEN, current.shape[-1])))
            statistics.append((center_a, spread_a, center_b, spread_b))
        stacked = jnp.stack(results, axis=1).reshape((ROWS, LEN, inputs.shape[-1]))
        return (stacked, statistics)
    final, pullback, statistics = jax.vjp(forward, tokens.astype(jnp.float32), params, has_aux=True)
    tokens_grad, gradients = pullback(cotangent.astype(jnp.float32))
    new_mean = run_mean
    new_var = run_var
    for center_a, spread_a, center_b, spread_b in statistics:
        new_mean = (1.0 - momentum) * new_mean + momentum * jnp.stack((center_a, center_b))
        new_var = (1.0 - momentum) * new_var + momentum * jnp.stack((spread_a, spread_b))
    return (final.astype(jnp.bfloat16), tokens_grad, gradients[0], gradients[1], gradients[2], gradients[3], gradients[4], gradients[5], gradients[6], gradients[7], gradients[8], new_mean, new_var)
```

```python
import functools

import jax
import jax.numpy as jnp
from jax import lax
from jax.experimental import pallas as pl
from jax.experimental.pallas import tpu as pltpu
from jax.sharding import PartitionSpec as P

epsilon = 1e-05
momentum = 0.1
F32 = jnp.float32
BF16 = jnp.bfloat16

SUB = 8
LANE = 128
TILE = 256


def in_vmem(count):
    return [pl.BlockSpec(memory_space=pltpu.VMEM)] * count


def call(name, body, outs, args, scratch=(), scalars=0):
    specs = [pl.BlockSpec(memory_space=pltpu.SMEM)] * scalars + in_vmem(len(args) - scalars)
    return pl.pallas_call(
        body,
        name=name,
        out_shape=outs,
        in_specs=specs,
        out_specs=in_vmem(len(outs)),
        scratch_shapes=list(scratch),
        compiler_params=pltpu.CompilerParams(vmem_limit_bytes=56 * 1024 * 1024),
    )(*args)


def shaped(shape, dtype=F32):
    return jax.ShapeDtypeStruct(shape, dtype)


def tile_mask(lim_ref, i):
    steps = TILE // SUB
    t = lax.broadcasted_iota(jnp.int32, (steps,) + lim_ref.shape, 0) + i * steps
    return t < lim_ref[...][None]


def folded(values):
    return values.reshape((values.shape[0] // SUB, SUB, values.shape[1]))


def flat(values):
    return values.reshape((values.shape[0] * SUB, values.shape[2]))


def times(ar, ai, br, bi):
    return (ar * br - ai * bi, ar * bi + ai * br)


def scan(d_ref, keep_ref, par_ref, start, reverse, conj, visit=None, extra=(), unroll=8):
    width = par_ref.shape[1]
    count = d_ref.shape[0] // SUB
    tiles = width // LANE
    lam = []
    for j in range(tiles):
        lanes = slice(j * LANE, (j + 1) * LANE)
        lr = jnp.broadcast_to(par_ref[0:1, lanes], (SUB, LANE))
        li = jnp.broadcast_to(par_ref[1:2, lanes], (SUB, LANE))
        lam.append((lr, -li if conj else li))
    state = tuple(
        (start[0][:, j * LANE : (j + 1) * LANE], start[1][:, j * LANE : (j + 1) * LANE])
        for j in range(tiles)
    )

    def step(i, carry):
        state, extra = carry
        t = count - 1 - i if reverse else i
        at = pl.ds(pl.multiple_of(t * SUB, SUB), SUB)
        keep = keep_ref[at, :]
        fresh = []
        for j in range(tiles):
            re, im = state[j]
            a = keep * lam[j][0]
            b = keep * lam[j][1]
            dr = d_ref[at, j * LANE : (j + 1) * LANE]
            di = d_ref[at, width + j * LANE : width + (j + 1) * LANE]
            fresh.append((a * re - b * im + dr, a * im + b * re + di))
        fresh = tuple(fresh)
        if visit is not None:
            extra = visit(t, keep, fresh, extra)
        return (fresh, extra)

    state, extra = lax.fori_loop(0, count, step, (state, tuple(extra)), unroll=unroll)
    re = jnp.concatenate([part[0] for part in state], axis=1)
    im = jnp.concatenate([part[1] for part in state], axis=1)
    return re, im, extra


def wide(values, width):
    return jnp.concatenate([values] * (width // LANE), axis=1)


def chunk_end(ends, kp_ref, par_ref, reverse, conj):
    width = par_ref.shape[1]
    re, im = ends
    shift = SUB - 1 if reverse else 1
    pr, pi = pltpu.roll(re, shift, 0), pltpu.roll(im, shift, 0)
    keep = wide(kp_ref[...], width)
    lr = keep * par_ref[2:3, :]
    li = keep * par_ref[3:4, :]
    li = -li if conj else li
    qr, qi = times(lr, li, pr, pi)
    odd = lax.broadcasted_iota(jnp.int32, (SUB, width), 0) % 2
    last = odd == (0 if reverse else 1)
    return jnp.where(last, qr + re, re), jnp.where(last, qi + im, im)


def enter(me_ref, got_ref, kd_ref, kp_ref, par_ref, reverse, conj):
    width = par_ref.shape[1]
    n = got_ref.shape[0]
    me = me_ref[0, 0]
    lr = jnp.broadcast_to(par_ref[4:5, :], (SUB, width))
    li = jnp.broadcast_to(par_ref[5:6, :], (SUB, width))
    li = -li if conj else li

    def step(i, x):
        j = n - 1 - i if reverse else i
        keep = wide(kd_ref[j], width)
        qr, qi = times(keep * lr, keep * li, x[0], x[1])
        use = (j > me) if reverse else (j < me)
        use = jnp.where(use, 1.0, 0.0)
        nr = qr + got_ref[j, :, :width]
        ni = qi + got_ref[j, :, width:]
        return (x[0] + use * (nr - x[0]), x[1] + use * (ni - x[1]))

    zero = jnp.zeros((SUB, width), F32)
    xr, xi = lax.fori_loop(0, n, step, (zero, zero), unroll=n <= 8)
    own_r = got_ref[me, :, :width]
    own_i = got_ref[me, :, width:]
    near, far = (1, SUB - 1) if reverse else (SUB - 1, 1)
    sr, si = pltpu.roll(xr, near, 0), pltpu.roll(xi, near, 0)
    keep = wide(kp_ref[...], width)
    hr = keep * par_ref[2:3, :]
    hi = keep * par_ref[3:4, :]
    hi = -hi if conj else hi
    tr, ti = times(hr, hi, sr, si)
    tr, ti = pltpu.roll(tr + own_r, far, 0), pltpu.roll(ti + own_i, far, 0)
    odd = lax.broadcasted_iota(jnp.int32, (SUB, width), 0) % 2
    second = odd == (0 if reverse else 1)
    return jnp.where(second, tr, sr), jnp.where(second, ti, si)


def put_ends(e_ref, ends):
    e_ref[...] = jnp.concatenate(ends, axis=1)


def zeros_state(par_ref):
    zero = jnp.zeros((SUB, par_ref.shape[1]), F32)
    return (zero, zero)


def per_micro(values):
    return (
        jnp.sum(values[0:4], axis=0, keepdims=True),
        jnp.sum(values[4:8], axis=0, keepdims=True),
    )


def pack_rows(out_ref, rows):
    at = 0
    for row in rows:
        for j in range(row.shape[1] // LANE):
            out_ref[at : at + 1, :] = row[:, j * LANE : (j + 1) * LANE]
            at += 1


def unpack_rows(values, count, width):
    tiles = width // LANE
    return [
        jnp.concatenate(
            [values[r * tiles + j : r * tiles + j + 1, :] for j in range(tiles)], axis=1
        )
        for r in range(count)
    ]


def by_micro(first, second):
    sub = lax.broadcasted_iota(jnp.int32, (SUB, first.shape[1]), 0)
    return jnp.where(sub < 4, jnp.broadcast_to(first, sub.shape), jnp.broadcast_to(second, sub.shape))


def dot(a, b):
    return jnp.dot(a, b, preferred_element_type=F32)


def dot_nt(a, b):
    return lax.dot_general(a, b, (((1,), (1,)), ((), ())), preferred_element_type=F32)


def dot_tn(a, b):
    return lax.dot_general(a, b, (((0,), (0,)), ((), ())), preferred_element_type=F32)


def normed_tile(u_ref, stat_ref, i):
    x = folded(u_ref[pl.ds(pl.multiple_of(i * TILE, TILE), TILE), :])
    return (x - stat_ref[0:8, :][None]) * stat_ref[8:16, :][None]


def masked_tile(u_ref, stat_ref, vec_ref, lim_ref, i):
    normed = normed_tile(u_ref, stat_ref, i)
    z = normed * vec_ref[0:1, :][None] + vec_ref[1:2, :][None]
    return jnp.where(tile_mask(lim_ref, i), z, 0.0)


def rows_at(i):
    return pl.ds(pl.multiple_of(i * TILE, TILE), TILE)


def spread_in(src_ref, dst_ref, lines_ref):
    half = src_ref.shape[1] // 2
    tiles = src_ref.shape[2] // LANE
    for s in range(SUB):
        part = src_ref[s // 2, (s % 2) * half : (s % 2 + 1) * half, :].astype(F32)
        for j in range(tiles):
            lines_ref[j, pl.ds(s, half, stride=SUB), :] = part[:, j * LANE : (j + 1) * LANE]
    for j in range(tiles):
        dst_ref[:, j * LANE : (j + 1) * LANE] = lines_ref[j]


def spread_out(lines_ref, dst_ref):
    half = dst_ref.shape[1] // 2
    tiles = dst_ref.shape[2] // LANE
    for s in range(SUB):
        for j in range(tiles):
            part = lines_ref[j, pl.ds(s, half, stride=SUB), :]
            dst_ref[s // 2, (s % 2) * half : (s % 2 + 1) * half, j * LANE : (j + 1) * LANE] = part.astype(dst_ref.dtype)


def put_lines(lines_ref, i, values):
    for j in range(lines_ref.shape[0]):
        lines_ref[j, rows_at(i), :] = values[:, j * LANE : (j + 1) * LANE]


def moment_sums(u_ref, lim_ref, upto):
    def step(i, sums):
        x = jnp.where(tile_mask(lim_ref, i), folded(u_ref[rows_at(i), :]), 0.0)
        return (sums[0] + jnp.sum(x, axis=0), sums[1] + jnp.sum(x * x, axis=0))

    zero = jnp.zeros(lim_ref.shape, F32)
    return lax.fori_loop(0, upto, step, (zero, zero))


def k_input(tokens_ref, lim_ref, u_ref, st_ref, lines_ref):
    spread_in(tokens_ref, u_ref, lines_ref)
    half = tokens_ref.shape[1] // 2
    sums, squares = moment_sums(u_ref, lim_ref, u_ref.shape[0] // TILE)
    a, b = per_micro(sums)
    c, d = per_micro(squares)
    st_ref[...] = jnp.zeros(st_ref.shape, F32)
    pack_rows(st_ref, (a, c, b, d))
    counts = jnp.clip(lim_ref[:, :LANE], 0, half).astype(F32)
    a, b = per_micro(counts)
    st_ref[16:17, :] = a
    st_ref[17:18, :] = b


def k_drive(reverse, st_ref, cnt_ref, u_ref, lim_ref, vec_ref, par_ref, b_ref, keep_ref, kp_ref,
            d_ref, ml_ref, stat_ref, e_ref):
    total = jnp.sum(st_ref[...], axis=0)
    a, c, b, d = unpack_rows(total, 4, u_ref.shape[1])
    if cnt_ref is None:
        counts = (total[16:17, :], total[17:18, :])
    else:
        counts = (cnt_ref[0:1, :], cnt_ref[1:2, :])
    parts = []
    for summed, squares, count in ((a, c, counts[0]), (b, d, counts[1])):
        inverse = 1.0 / wide(count, u_ref.shape[1])
        center = summed * inverse
        spread = squares * inverse - center * center
        parts.append((center, spread, lax.rsqrt(spread + epsilon), inverse))
    stat_ref[0:8, :] = by_micro(parts[0][0], parts[1][0])
    stat_ref[8:16, :] = by_micro(parts[0][2], parts[1][2])
    stat_ref[16:24, :] = by_micro(parts[0][3], parts[1][3])
    stat_ref[24:25, :] = parts[0][0]
    stat_ref[25:26, :] = parts[1][0]
    stat_ref[26:27, :] = parts[0][1]
    stat_ref[27:28, :] = parts[1][1]
    stat_ref[28:29, :] = wide(counts[0], u_ref.shape[1])
    stat_ref[29:30, :] = wide(counts[1], u_ref.shape[1])
    stat_ref[30:32, :] = jnp.zeros((2, u_ref.shape[1]), F32)
    both = jnp.concatenate((par_ref[6:7, :], par_ref[6:7, :]), axis=1)

    def step(i, unused):
        low = flat(masked_tile(u_ref, stat_ref, vec_ref, lim_ref, i)).astype(BF16)
        ml_ref[rows_at(i), :] = low
        d_ref[rows_at(i), :] = dot(low, b_ref[...]) * both
        return unused

    lax.fori_loop(0, u_ref.shape[0] // TILE, step, 0)
    re, im, unused = scan(d_ref, keep_ref, par_ref, zeros_state(par_ref), reverse, False)
    put_ends(e_ref, chunk_end((re, im), kp_ref, par_ref, reverse, False))


def k_drive_first(reverse, st_ref, *refs):
    k_drive(reverse, st_ref, None, *refs)


def run_states(me_ref, got_ref, d_ref, keep_ref, kp_ref, kd_ref, par_ref, s_ref, reverse):
    width = par_ref.shape[1]
    first = 0 if reverse else SUB
    start = enter(me_ref, got_ref, kd_ref, kp_ref, par_ref, reverse, False)
    s_ref[(s_ref.shape[0] - SUB if reverse else 0) : (s_ref.shape[0] if reverse else SUB), :] = (
        jnp.concatenate(start, axis=1)
    )

    def visit(t, keep, states, extra):
        at = pl.ds(pl.multiple_of(t * SUB + first, SUB), SUB)
        for j, (re, im) in enumerate(states):
            s_ref[at, j * LANE : (j + 1) * LANE] = re
            s_ref[at, width + j * LANE : width + (j + 1) * LANE] = im
        return extra

    scan(d_ref, keep_ref, par_ref, start, reverse, False, visit)
    return first


def gelu_parts(x):
    cdf = 0.5 * (1.0 + lax.erf(x * 0.7071067811865476))
    return x * cdf, cdf + x * jnp.exp(-0.5 * x * x) * 0.3989422804014327


def states_low(s_ref, first, i):
    return s_ref[pl.ds(pl.multiple_of(i * TILE + first, SUB), TILE), :].astype(BF16)


def k_finish_first(me_ref, got_ref, d_ref, u_ref, stat_ref, lim_ref, vec_ref, par_ref, keep_ref, kp_ref, kd_ref,
                   c_ref, w_ref, s_ref, al_ref, sig_ref, q_ref, slope_ref, next_ref, st_ref):
    first = run_states(me_ref, got_ref, d_ref, keep_ref, kp_ref, kd_ref, par_ref, s_ref, False)

    def step(i, sums):
        at = rows_at(i)
        valid = tile_mask(lim_ref, i)
        masked = masked_tile(u_ref, stat_ref, vec_ref, lim_ref, i)
        mixed = dot(states_low(s_ref, first, i), c_ref[...]) + vec_ref[2:3, :] * flat(masked)
        active, slope = gelu_parts(mixed)
        low = active.astype(BF16)
        sig = jax.nn.sigmoid(dot(low, w_ref[...]) + vec_ref[3:4, :])
        gated = active * sig
        al_ref[at, :] = low
        sig_ref[at, :] = sig
        slope_ref[at, :] = slope
        q_ref[at, :] = gated * (1.0 - sig)
        fresh = folded(u_ref[at, :]) + jnp.where(valid, folded(gated), 0.0)
        next_ref[at, :] = flat(fresh)
        x = jnp.where(valid, fresh, 0.0)
        return (sums[0] + jnp.sum(x, axis=0), sums[1] + jnp.sum(x * x, axis=0))

    zero = jnp.zeros(lim_ref.shape, F32)
    sums, squares = lax.fori_loop(0, u_ref.shape[0] // TILE, step, (zero, zero))
    a, b = per_micro(sums)
    c, d = per_micro(squares)
    pack_rows(st_ref, (a, c, b, d))


def gate_backward(upstream, q, sig, slope, low, masked, s_low, state, c_ref, w_ref, mix_ref, sg_ref, gw_ref, gc_ref, i):
    at = rows_at(i)
    gate = (upstream * q).astype(BF16)
    gw_ref[...] += dot_tn(low, gate)
    act = upstream * sig + dot_nt(gate, w_ref[...])
    mix = (act * slope).astype(BF16)
    mix_ref[at, :] = mix
    gc_ref[...] += dot_tn(s_low, mix)
    sg = dot_nt(mix, c_ref[...])
    sg_ref[at, :] = sg
    wide_sum = jnp.sum(folded(sg * state), axis=0)
    half = wide_sum.shape[1] // 2
    return (
        jnp.sum(folded(gate.astype(F32)), axis=0),
        jnp.sum(folded(mix.astype(F32) * masked), axis=0),
        wide_sum[:, :half] + wide_sum[:, half:],
    )


def put_sums(sums_ref, sums):
    sums_ref[...] = jnp.zeros(sums_ref.shape, F32)
    pack_rows(sums_ref, [jnp.sum(part, axis=0, keepdims=True) for part in sums])


def zero_sums(width, states):
    return (jnp.zeros((SUB, width), F32), jnp.zeros((SUB, width), F32), jnp.zeros((SUB, states), F32))


def k_middle(me_ref, got_ref, d_ref, u_ref, stat_ref, lim_ref, vec_ref, par_ref, keep_ref, kp_ref, kd_ref,
             keep_adj_ref, kp_adj_ref, c_ref, w_ref, cot_ref,
             out_ref, s_ref, cot32_ref, mix_ref, sg_ref, gw_ref, gc_ref, sums_ref, e_ref, lines_ref):
    spread_in(cot_ref, cot32_ref, lines_ref)
    first = run_states(me_ref, got_ref, d_ref, keep_ref, kp_ref, kd_ref, par_ref, s_ref, True)
    gw_ref[...] = jnp.zeros(gw_ref.shape, F32)
    gc_ref[...] = jnp.zeros(gc_ref.shape, F32)

    def step(i, sums):
        at = rows_at(i)
        valid = tile_mask(lim_ref, i)
        masked = flat(masked_tile(u_ref, stat_ref, vec_ref, lim_ref, i))
        state = s_ref[pl.ds(pl.multiple_of(i * TILE + first, SUB), TILE), :]
        s_low = state.astype(BF16)
        mixed = dot(s_low, c_ref[...]) + vec_ref[2:3, :] * masked
        active, slope = gelu_parts(mixed)
        low = active.astype(BF16)
        sig = jax.nn.sigmoid(dot(low, w_ref[...]) + vec_ref[3:4, :])
        gated = active * sig
        put_lines(lines_ref, i, flat(folded(u_ref[at, :]) + jnp.where(valid, folded(gated), 0.0)))
        upstream = flat(jnp.where(valid, folded(cot32_ref[at, :]), 0.0))
        more = gate_backward(upstream, gated * (1.0 - sig), sig, slope, low, masked, s_low, state,
                             c_ref, w_ref, mix_ref, sg_ref, gw_ref, gc_ref, i)
        return tuple(x + y for x, y in zip(sums, more))

    sums = lax.fori_loop(0, u_ref.shape[0] // TILE, step, zero_sums(u_ref.shape[1], par_ref.shape[1]))
    put_sums(sums_ref, sums)
    spread_out(lines_ref, out_ref)
    re, im, unused = scan(sg_ref, keep_adj_ref, par_ref, zeros_state(par_ref), False, True)
    put_ends(e_ref, chunk_end((re, im), kp_adj_ref, par_ref, False, True))


def k_lower(st_ref, z_ref, cot32_ref, u1_ref, stat1_ref, vec1_ref, lim_ref,
            s_ref, al_ref, sig_ref, q_ref, slope_ref, u_ref, stat_ref, vec_ref, par_ref, c_ref, w_ref,
            keep_adj_ref, kp_adj_ref,
            grad_ref, mix_ref, sg_ref, gw_ref, gc_ref, sums_ref, e_ref, bn_ref):
    first = SUB
    c1, c2 = norm_sums(st_ref, stat1_ref, vec1_ref, bn_ref)
    gw_ref[...] = jnp.zeros(gw_ref.shape, F32)
    gc_ref[...] = jnp.zeros(gc_ref.shape, F32)

    def step(i, sums):
        at = rows_at(i)
        valid = tile_mask(lim_ref, i)
        extra = norm_backward(z_ref, u1_ref, stat1_ref, vec1_ref, c1, c2, valid, i)
        grad = folded(cot32_ref[at, :]) + extra
        grad_ref[at, :] = flat(grad)
        upstream = flat(jnp.where(valid, grad, 0.0))
        masked = flat(masked_tile(u_ref, stat_ref, vec_ref, lim_ref, i))
        state = s_ref[pl.ds(pl.multiple_of(i * TILE + first, SUB), TILE), :]
        more = gate_backward(upstream, q_ref[at, :], sig_ref[at, :], slope_ref[at, :], al_ref[at, :], masked,
                             state.astype(BF16), state, c_ref, w_ref, mix_ref, sg_ref, gw_ref, gc_ref, i)
        return tuple(x + y for x, y in zip(sums, more))

    sums = lax.fori_loop(0, u_ref.shape[0] // TILE, step, zero_sums(u_ref.shape[1], par_ref.shape[1]))
    put_sums(sums_ref, sums)
    re, im, unused = scan(sg_ref, keep_adj_ref, par_ref, zeros_state(par_ref), True, True)
    put_ends(e_ref, chunk_end((re, im), kp_adj_ref, par_ref, True, True))


def norm_sums(st_ref, stat_ref, vec_ref, bn_ref):
    width = vec_ref.shape[1]
    a, c, b, d = unpack_rows(jnp.sum(st_ref[...], axis=0), 4, width)
    bn_ref[...] = jnp.concatenate((a + b, c + d, jnp.zeros((6, width), F32)), axis=0)
    gain = vec_ref[0:1, :]
    inverse = stat_ref[16:24, :]
    return by_micro(a * gain, b * gain) * inverse, by_micro(c * gain, d * gain) * inverse


def norm_backward(z_ref, u_ref, stat_ref, vec_ref, c1, c2, valid, i):
    normed = normed_tile(u_ref, stat_ref, i)
    z = folded(z_ref[rows_at(i), :]) * vec_ref[0:1, :][None]
    return jnp.where(valid, stat_ref[8:16, :][None] * (z - c1[None] - normed * c2[None]), 0.0)


def k_adjoint(reverse, me_ref, got_ref, sg_ref, s_ref, mix_ref, ml_ref, u_ref, stat_ref, lim_ref, vec_ref, par_ref,
              keep_adj_ref, kp_adj_ref, kd_adj_ref, keep_ref, b_ref,
              z_ref, gb_ref, lg_ref, st_ref, a_ref):
    width = par_ref.shape[1]
    tiles = width // LANE
    behind = 0 if reverse else SUB
    start = enter(me_ref, got_ref, kd_adj_ref, kp_adj_ref, par_ref, reverse, True)
    scale = [jnp.broadcast_to(par_ref[6:7, j * LANE : (j + 1) * LANE], (SUB, LANE)) for j in range(tiles)]

    def visit(t, unused, adjoint, sums):
        at = pl.ds(pl.multiple_of(t * SUB, SUB), SUB)
        before = pl.ds(pl.multiple_of(t * SUB + behind, SUB), SUB)
        keep = keep_ref[at, :]
        fresh = []
        for j, (re, im) in enumerate(adjoint):
            a_ref[at, j * LANE : (j + 1) * LANE] = re * scale[j]
            a_ref[at, width + j * LANE : width + (j + 1) * LANE] = im * scale[j]
            pr = s_ref[before, j * LANE : (j + 1) * LANE]
            pi = s_ref[before, width + j * LANE : width + (j + 1) * LANE]
            kr, ki = keep * re, keep * im
            fresh.append((sums[j][0] + (kr * pr + ki * pi), sums[j][1] + (ki * pr - kr * pi)))
        return tuple(fresh)

    zero = jnp.zeros((SUB, LANE), F32)
    unused, unused, sums = scan(sg_ref, keep_adj_ref, par_ref, start, reverse, True, visit,
                                tuple((zero, zero) for j in range(tiles)))
    lg_ref[...] = jnp.zeros(lg_ref.shape, F32)
    pack_rows(lg_ref, [
        jnp.sum(jnp.concatenate([part[k] for part in sums], axis=1), axis=0, keepdims=True) for k in range(2)
    ])
    gb_ref[...] = jnp.zeros(gb_ref.shape, F32)

    def step(i, sums):
        at = rows_at(i)
        drive = a_ref[at, :].astype(BF16)
        gb_ref[...] += dot_tn(ml_ref[at, :], drive)
        back = dot_nt(drive, b_ref[...]) + vec_ref[2:3, :] * mix_ref[at, :].astype(F32)
        z = jnp.where(tile_mask(lim_ref, i), folded(back), 0.0)
        z_ref[at, :] = flat(z)
        return (sums[0] + jnp.sum(z, axis=0), sums[1] + jnp.sum(z * normed_tile(u_ref, stat_ref, i), axis=0))

    zero = jnp.zeros(lim_ref.shape, F32)
    sums = lax.fori_loop(0, u_ref.shape[0] // TILE, step, (zero, zero))
    a, b = per_micro(sums[0])
    c, d = per_micro(sums[1])
    pack_rows(st_ref, (a, c, b, d))


def k_output(st_ref, z_ref, grad_ref, u_ref, stat_ref, vec_ref, lim_ref, out_ref, bn_ref, lines_ref):
    c1, c2 = norm_sums(st_ref, stat_ref, vec_ref, bn_ref)

    def step(i, unused):
        extra = norm_backward(z_ref, u_ref, stat_ref, vec_ref, c1, c2, tile_mask(lim_ref, i), i)
        put_lines(lines_ref, i, grad_ref[rows_at(i), :] + flat(extra))
        return unused

    lax.fori_loop(0, u_ref.shape[0] // TILE, step, 0)
    spread_out(lines_ref, out_ref)


BOTH = ("batch", "tm")


def index_bits():
    nb, nt = lax.axis_size("batch"), lax.axis_size("tm")
    core = ("tm", 1, 1)
    outer = [("batch", 1 << k, nt << k) for k in range(nb.bit_length() - 1)]
    line = [("tm", 1 << k, 1 << k) for k in range(1, nt.bit_length() - 1)]
    return core, outer, line


def swap(block, distance):
    total = lax.axis_size("batch") * lax.axis_size("tm")
    return lax.ppermute(block, BOTH, [(i, i ^ distance) for i in range(total)])


def swap_by_core(block, even, odd):
    total = lax.axis_size("batch") * lax.axis_size("tm")
    return lax.ppermute(block, BOTH, [(i, i ^ (odd if i & 1 else even)) for i in range(total)])


def sums_of_all(block):
    block = block + swap(block, 1)
    total = lax.axis_size("batch") * lax.axis_size("tm")
    groups = [list(range(0, total, 2)), list(range(1, total, 2))]
    spread = jnp.broadcast_to(block[None], (total // 2,) + block.shape)
    return lax.all_to_all(spread, BOTH, 0, 0, axis_index_groups=groups)


def blocks_of_row(block):
    n = lax.axis_size("tm")
    return lax.all_to_all(jnp.broadcast_to(block[None], (n,) + block.shape), "tm", 0, 0)


def bit_of(axis, bit):
    return jnp.where((lax.axis_index(axis) & bit) != 0, 1, 0)


def plan():
    core, outer, line = index_bits()
    is_odd = bit_of("tm", 1)
    steps = [(is_odd, lambda block: swap(block, 1))]
    turned = outer[::-1]
    for even, odd in zip(outer, turned):
        side = jnp.where(is_odd == 1, bit_of(odd[0], odd[1]), bit_of(even[0], even[1]))
        steps.append((side, functools.partial(swap_by_core, even=even[2], odd=odd[2])))
    for axis, bit, distance in line:
        steps.append((bit_of(axis, bit), functools.partial(swap, distance=distance)))
    return steps


def sum_large(block):
    steps = plan()
    for side, exchange in steps:
        half = block.shape[0] // 2
        given = lax.dynamic_slice_in_dim(block, (1 - side) * half, half, 0)
        kept = lax.dynamic_slice_in_dim(block, side * half, half, 0)
        block = kept + exchange(given)
    for side, exchange in steps[::-1]:
        other = exchange(block)
        low = jnp.where(side == 1, other, block)
        high = jnp.where(side == 1, block, other)
        block = jnp.concatenate((low, high), axis=0)
    return block


def power(re, im, doublings):
    for unused in range(doublings):
        re, im = times(re, im, re, im)
    return re, im


def local(tokens, starts, lengths, cotangent, norm_gain, norm_shift, b_proj, log_rate, rotation, c_proj, skip_gain,
          w_gate, gate_bias, run_mean, run_var):
    rows, length, width = tokens.shape
    states = log_rate.shape[1]
    half = length // 2
    count = rows * length
    n = lax.axis_size("tm")
    me = lax.axis_index("tm")
    offset = me * length

    places = offset + jnp.arange(length + 1, dtype=jnp.int32)
    resets = jnp.any(starts[:, :, None] == places[None, None, :], axis=1)
    keeping = 1.0 - resets.astype(F32)
    here = keeping[:, :length].reshape((SUB, half))
    following = (keeping[:, 1:] * (places[None, 1:] < n * length).astype(F32)).reshape((SUB, half))

    def over_lanes(values):
        return jnp.broadcast_to(values[..., None], values.shape + (LANE,))

    def by_tile(values):
        return over_lanes(values.T).reshape((count, LANE))

    keep_f, keep_r = by_tile(here), by_tile(following)
    kp_f, kp_r = over_lanes(jnp.min(here, axis=1)), over_lanes(jnp.min(following, axis=1))
    devices = jnp.arange(n, dtype=jnp.int32)[:, None, None]

    def whole(first):
        hit = jnp.any((first[None] >= devices * length) & (first[None] < (devices + 1) * length), axis=2)
        return over_lanes(jnp.repeat(1.0 - hit.astype(F32), 2, axis=1))

    kd_f, kd_r = whole(starts), whole(starts - 1)
    halves = jnp.arange(SUB, dtype=jnp.int32) % 2
    lim = jnp.broadcast_to(
        (jnp.repeat(lengths, 2) - offset - halves * half)[:, None], (SUB, width)
    )

    decay = jnp.exp(log_rate)
    magnitude = jnp.exp(-decay)
    lam_re, lam_im = magnitude * jnp.cos(rotation), magnitude * jnp.sin(rotation)
    norm_in = jnp.sqrt(-jnp.expm1(-2.0 * decay))
    doublings = half.bit_length() - 1
    half_re, half_im = power(lam_re, lam_im, doublings)
    full_re, full_im = times(half_re, half_im, half_re, half_im)
    par = jnp.stack((lam_re, lam_im, half_re, half_im, full_re, full_im, norm_in, norm_in), axis=1)
    vec = jnp.stack((norm_gain, norm_shift, skip_gain, gate_bias) * 2, axis=1)
    place = me.astype(jnp.int32).reshape((1, 1))

    big = lambda w, dtype=F32: shaped((count, w), dtype)
    ends = shaped((SUB, 2 * states))
    kept = shaped((count + SUB, 2 * states))
    small = shaped((16, LANE))
    lines = pltpu.VMEM((width // LANE, count, LANE), F32)

    u0, st = call("enter", k_input, [big(width), shaped((24, LANE))], [tokens, lim], scratch=[lines])
    st = sums_of_all(st)
    d0, ml0, stat0, e = call(
        "drive0", functools.partial(k_drive_first, False),
        [big(2 * states), big(width, BF16), shaped((32, width)), ends],
        [st, u0, lim, vec[0], par[0], b_proj[0], keep_f, kp_f],
    )
    got = blocks_of_row(e)
    s0, al0, sig0, q0, slope0, u1, st = call(
        "finish0", k_finish_first,
        [kept, big(width, BF16), big(width), big(width), big(width), big(width), small],
        [place, got, d0, u0, stat0, lim, vec[0], par[0], keep_f, kp_f, kd_f, c_proj[0], w_gate[0]],
        scalars=1,
    )
    st = sums_of_all(st)
    counts = stat0[28:30, :LANE]
    d1, ml1, stat1, e = call(
        "drive1", functools.partial(k_drive, True),
        [big(2 * states), big(width, BF16), shaped((32, width)), ends],
        [st, counts, u1, lim, vec[1], par[1], b_proj[1], keep_r, kp_r],
    )
    got = blocks_of_row(e)
    grads = [shaped((width, width)), shaped((2 * states, width)), shaped((16, LANE)), ends]
    output, s1, cot32, mix1, sg1, gw1, gc1, sums1, e = call(
        "middle", k_middle,
        [shaped(tokens.shape, BF16), kept, big(width), big(width, BF16), big(2 * states)] + grads,
        [place, got, d1, u1, stat1, lim, vec[1], par[1], keep_r, kp_r, kd_r, keep_f, kp_f, c_proj[1], w_gate[1],
         cotangent],
        scratch=[lines], scalars=1,
    )
    got = blocks_of_row(e)
    wc1 = sum_large(jnp.concatenate((gw1, gc1), axis=0))
    adjoint = [big(width), shaped((width, 2 * states)), shaped((8, LANE)), small]
    z1, gb1, lg1, st = call(
        "adjoint1", functools.partial(k_adjoint, False), adjoint,
        [place, got, sg1, s1, mix1, ml1, u1, stat1, lim, vec[1], par[1], keep_f, kp_f, kd_f, keep_r, b_proj[1]],
        scratch=[pltpu.VMEM((count, 2 * states), F32)], scalars=1,
    )
    st = sums_of_all(st)
    b1 = sum_large(gb1)
    g0, mix0, sg0, gw0, gc0, sums0, e, bn1 = call(
        "lower", k_lower,
        [big(width), big(width, BF16), big(2 * states)] + grads + [shaped((8, width))],
        [st, z1, cot32, u1, stat1, vec[1], lim, s0, al0, sig0, q0, slope0, u0, stat0, vec[0], par[0],
         c_proj[0], w_gate[0], keep_r, kp_r],
    )
    got = blocks_of_row(e)
    wc0 = sum_large(jnp.concatenate((gw0, gc0), axis=0))
    z0, gb0, lg0, st = call(
        "adjoint0", functools.partial(k_adjoint, True), adjoint,
        [place, got, sg0, s0, mix0, ml0, u0, stat0, lim, vec[0], par[0], keep_r, kp_r, kd_r, keep_f, b_proj[0]],
        scratch=[pltpu.VMEM((count, 2 * states), F32)], scalars=1,
    )
    st = sums_of_all(jnp.concatenate((st, sums0, lg0, sums1, lg1), axis=0))
    b0 = sum_large(gb0)
    tokens_grad, bn0 = call(
        "leave", k_output, [shaped(tokens.shape), shaped((8, width))],
        [st, z0, g0, u0, stat0, vec[0], lim],
        scratch=[lines],
    )
    sums = jnp.sum(st[:, 16:], axis=0).reshape((2, 24, LANE))
    per = width // LANE
    per_state = states // LANE

    def taken(first, lines):
        return sums[:, first : first + lines].reshape((2, lines * LANE))

    grad_bias = taken(0, per)
    grad_skip = taken(per, per)
    product = taken(2 * per, per_state)
    lam_grad_re, lam_grad_im = taken(16, per_state), taken(16 + per_state, per_state)
    grad_rotation = lam_re * lam_grad_im - lam_im * lam_grad_re
    grad_rate = decay * (
        -(lam_re * lam_grad_re + lam_im * lam_grad_im)
        + product * jnp.exp(-2.0 * decay) / (norm_in * norm_in)
    )
    new_mean, new_var = run_mean, run_var
    for micro in range(2):
        center = jnp.stack((stat0[24 + micro], stat1[24 + micro]))
        spread = jnp.stack((stat0[26 + micro], stat1[26 + micro]))
        new_mean = (1.0 - momentum) * new_mean + momentum * center
        new_var = (1.0 - momentum) * new_var + momentum * spread
    return (
        output,
        tokens_grad,
        jnp.stack((bn0[1], bn1[1])),
        jnp.stack((bn0[0], bn1[0])),
        jnp.stack((b0, b1)),
        grad_rate,
        grad_rotation,
        jnp.stack((wc0[width:], wc1[width:])),
        grad_skip,
        jnp.stack((wc0[:width], wc1[:width])),
        grad_bias,
        new_mean,
        new_var,
    )


def solution(mesh):
    tokens_spec = P("batch", "tm", None)
    return jax.shard_map(
        local,
        mesh=mesh,
        in_specs=(tokens_spec, P("batch", None), P("batch"), tokens_spec) + (P(),) * 11,
        out_specs=(tokens_spec, tokens_spec) + (P(),) * 11,
        check_vma=False,
    )
```

```python
import functools
import math

import jax
import jax.numpy as jnp
from jax import lax
from jax.experimental import pallas as pl
from jax.experimental.pallas import tpu as pltpu
from jax.sharding import PartitionSpec as P

epsilon = 1e-05
momentum = 0.1
F32 = jnp.float32
BF16 = jnp.bfloat16

SUB = 8
LANE = 128
TILE = 256


def in_vmem(count):
    return [pl.BlockSpec(memory_space=pltpu.VMEM)] * count


def call(name, body, outs, args, scratch=(), scalars=0, results=0):
    room = 6 * 1024 * 1024 + sum(4 * math.prod(item.shape) for item in list(scratch) + list(outs[:results]))
    specs = [pl.BlockSpec(memory_space=pltpu.SMEM)] * scalars + in_vmem(len(args) - scalars)
    return pl.pallas_call(
        body,
        name=name,
        out_shape=outs,
        in_specs=specs,
        out_specs=in_vmem(len(outs)),
        scratch_shapes=list(scratch),
        compiler_params=pltpu.CompilerParams(vmem_limit_bytes=room),
    )(*args)


def shaped(shape, dtype=F32):
    return jax.ShapeDtypeStruct(shape, dtype)


def tile_mask(lim_ref, i):
    steps = TILE // SUB
    t = lax.broadcasted_iota(jnp.int32, (steps,) + lim_ref.shape, 0) + i * steps
    return t < lim_ref[...][None]


def folded(values):
    return values.reshape((values.shape[0] // SUB, SUB, values.shape[1]))


def flat(values):
    return values.reshape((values.shape[0] * SUB, values.shape[2]))


def times(ar, ai, br, bi):
    return (ar * br - ai * bi, ar * bi + ai * br)


def scan(d_ref, keep_ref, par_ref, start, reverse, conj, visit=None, extra=(), unroll=8):
    width = par_ref.shape[1]
    count = d_ref.shape[0] // SUB
    tiles = width // LANE
    lam = []
    for j in range(tiles):
        lanes = slice(j * LANE, (j + 1) * LANE)
        lr = jnp.broadcast_to(par_ref[0:1, lanes], (SUB, LANE))
        li = jnp.broadcast_to(par_ref[1:2, lanes], (SUB, LANE))
        lam.append((lr, -li if conj else li))
    state = tuple(
        (start[0][:, j * LANE : (j + 1) * LANE], start[1][:, j * LANE : (j + 1) * LANE])
        for j in range(tiles)
    )

    def step(i, carry):
        state, extra = carry
        t = count - 1 - i if reverse else i
        at = pl.ds(pl.multiple_of(t * SUB, SUB), SUB)
        keep = keep_ref[at, :]
        fresh = []
        for j in range(tiles):
            re, im = state[j]
            a = keep * lam[j][0]
            b = keep * lam[j][1]
            dr = d_ref[at, j * LANE : (j + 1) * LANE]
            di = d_ref[at, width + j * LANE : width + (j + 1) * LANE]
            fresh.append((a * re - b * im + dr, a * im + b * re + di))
        fresh = tuple(fresh)
        if visit is not None:
            extra = visit(t, keep, fresh, extra)
        return (fresh, extra)

    state, extra = lax.fori_loop(0, count, step, (state, tuple(extra)), unroll=unroll)
    re = jnp.concatenate([part[0] for part in state], axis=1)
    im = jnp.concatenate([part[1] for part in state], axis=1)
    return re, im, extra


def wide(values, width):
    return jnp.concatenate([values] * (width // LANE), axis=1)


def chunk_end(ends, kp_ref, par_ref, reverse, conj):
    width = par_ref.shape[1]
    re, im = ends
    shift = SUB - 1 if reverse else 1
    pr, pi = pltpu.roll(re, shift, 0), pltpu.roll(im, shift, 0)
    keep = wide(kp_ref[...], width)
    lr = keep * par_ref[2:3, :]
    li = keep * par_ref[3:4, :]
    li = -li if conj else li
    qr, qi = times(lr, li, pr, pi)
    odd = lax.broadcasted_iota(jnp.int32, (SUB, width), 0) % 2
    last = odd == (0 if reverse else 1)
    return jnp.where(last, qr + re, re), jnp.where(last, qi + im, im)


def chip_and_core():
    me = lax.axis_index("tm")
    return me // 2, me % 2


def enter(got_refs, e_ref, other_ref, all_ref, kd_ref, kp_ref, par_ref, reverse, conj):
    width = par_ref.shape[1]
    chips = all_ref.shape[0]
    chip, core = chip_and_core()
    sign = -1.0 if conj else 1.0
    at = 0
    for ref in got_refs:
        for k in range(ref.shape[0] // SUB):
            all_ref[at] = ref[k * SUB : (k + 1) * SUB, :]
            at += 1
    lr, li = par_ref[4:5, :], sign * par_ref[5:6, :]
    cr, ci = times(lr, li, lr, li)
    lr, li, cr, ci = (jnp.broadcast_to(x, (SUB, width)) for x in (lr, li, cr, ci))

    def step(i, x):
        j = chips - 1 - i if reverse else i
        keep = wide(kd_ref[2 * j] * kd_ref[2 * j + 1], width)
        qr, qi = times(keep * cr, keep * ci, x[0], x[1])
        use = (j > chip) if reverse else (j < chip)
        use = jnp.where(use, 1.0, 0.0)
        k = jnp.bitwise_xor(j, chip)
        nr = qr + all_ref[k, :, :width]
        ni = qi + all_ref[k, :, width:]
        return (x[0] + use * (nr - x[0]), x[1] + use * (ni - x[1]))

    zero = jnp.zeros((SUB, width), F32)
    xr, xi = lax.fori_loop(0, chips, step, (zero, zero), unroll=chips <= 4)
    first = 1 if reverse else 0
    keep = wide(kd_ref[2 * chip + first], width)
    qr, qi = times(keep * lr, keep * li, xr, xi)
    use = jnp.where(core == first, 0.0, 1.0)
    xr = xr + use * (qr + other_ref[:, :width] - xr)
    xi = xi + use * (qi + other_ref[:, width:] - xi)
    near, far = (1, SUB - 1) if reverse else (SUB - 1, 1)
    sr, si = pltpu.roll(xr, near, 0), pltpu.roll(xi, near, 0)
    keep = wide(kp_ref[...], width)
    hr = keep * par_ref[2:3, :]
    hi = sign * keep * par_ref[3:4, :]
    tr, ti = times(hr, hi, sr, si)
    tr = pltpu.roll(tr + e_ref[:, :width], far, 0)
    ti = pltpu.roll(ti + e_ref[:, width:], far, 0)
    odd = lax.broadcasted_iota(jnp.int32, (SUB, width), 0) % 2
    second = odd == (0 if reverse else 1)
    return jnp.where(second, tr, sr), jnp.where(second, ti, si)


def put_ends(e_ref, ends):
    e_ref[...] = jnp.concatenate(ends, axis=1)


def zeros_state(par_ref):
    zero = jnp.zeros((SUB, par_ref.shape[1]), F32)
    return (zero, zero)


def per_micro(values):
    return (
        jnp.sum(values[0:4], axis=0, keepdims=True),
        jnp.sum(values[4:8], axis=0, keepdims=True),
    )


def pack_rows(out_ref, rows):
    at = 0
    for row in rows:
        for j in range(row.shape[1] // LANE):
            out_ref[at : at + 1, :] = row[:, j * LANE : (j + 1) * LANE]
            at += 1


def unpack_rows(values, count, width):
    tiles = width // LANE
    return [
        jnp.concatenate(
            [values[r * tiles + j : r * tiles + j + 1, :] for j in range(tiles)], axis=1
        )
        for r in range(count)
    ]


def by_micro(first, second):
    sub = lax.broadcasted_iota(jnp.int32, (SUB, first.shape[1]), 0)
    return jnp.where(sub < 4, jnp.broadcast_to(first, sub.shape), jnp.broadcast_to(second, sub.shape))


def dot(a, b):
    return jnp.dot(a, b, preferred_element_type=F32)


def dot_nt(a, b):
    return lax.dot_general(a, b, (((1,), (1,)), ((), ())), preferred_element_type=F32)


def dot_tn(a, b):
    return lax.dot_general(a, b, (((0,), (0,)), ((), ())), preferred_element_type=F32)


def normed_tile(u_ref, stat_ref, i):
    x = folded(u_ref[pl.ds(pl.multiple_of(i * TILE, TILE), TILE), :])
    return (x - stat_ref[0:8, :][None]) * stat_ref[8:16, :][None]


def masked_tile(u_ref, stat_ref, vec_ref, lim_ref, i):
    normed = normed_tile(u_ref, stat_ref, i)
    z = normed * vec_ref[0:1, :][None] + vec_ref[1:2, :][None]
    return jnp.where(tile_mask(lim_ref, i), z, 0.0)


def rows_at(i):
    return pl.ds(pl.multiple_of(i * TILE, TILE), TILE)


def spread_in(src_ref, dst_ref, lines_ref):
    half = src_ref.shape[1] // 2
    tiles = src_ref.shape[2] // LANE
    for s in range(SUB):
        part = src_ref[s // 2, (s % 2) * half : (s % 2 + 1) * half, :].astype(F32)
        for j in range(tiles):
            lines_ref[j, pl.ds(s, half, stride=SUB), :] = part[:, j * LANE : (j + 1) * LANE]
    for j in range(tiles):
        dst_ref[:, j * LANE : (j + 1) * LANE] = lines_ref[j]


def spread_out(lines_ref, dst_ref):
    half = dst_ref.shape[1] // 2
    tiles = dst_ref.shape[2] // LANE
    for s in range(SUB):
        for j in range(tiles):
            part = lines_ref[j, pl.ds(s, half, stride=SUB), :]
            dst_ref[s // 2, (s % 2) * half : (s % 2 + 1) * half, j * LANE : (j + 1) * LANE] = part.astype(dst_ref.dtype)


def put_lines(lines_ref, i, values):
    for j in range(lines_ref.shape[0]):
        lines_ref[j, rows_at(i), :] = values[:, j * LANE : (j + 1) * LANE]


def moment_sums(u_ref, lim_ref, upto):
    def step(i, sums):
        x = jnp.where(tile_mask(lim_ref, i), folded(u_ref[rows_at(i), :]), 0.0)
        return (sums[0] + jnp.sum(x, axis=0), sums[1] + jnp.sum(x * x, axis=0))

    zero = jnp.zeros(lim_ref.shape, F32)
    return lax.fori_loop(0, upto, step, (zero, zero))


def fill_lim(lengths_ref, lim_ref, half):
    sub = lax.broadcasted_iota(jnp.int32, lim_ref.shape, 0)
    length = jnp.zeros(lim_ref.shape, jnp.int32)
    for r in range(lengths_ref.shape[0]):
        length = jnp.where(sub // 2 == r, lengths_ref[r], length)
    lim_ref[...] = length - lax.axis_index("tm") * (2 * half) - (sub % 2) * half


def k_input(lengths_ref, tokens_ref, u_ref, st_ref, lim_ref, lines_ref):
    half = tokens_ref.shape[1] // 2
    fill_lim(lengths_ref, lim_ref, half)
    spread_in(tokens_ref, u_ref, lines_ref)
    sums, squares = moment_sums(u_ref, lim_ref, u_ref.shape[0] // TILE)
    a, b = per_micro(sums)
    c, d = per_micro(squares)
    st_ref[...] = jnp.zeros(st_ref.shape, F32)
    pack_rows(st_ref, (a, c, b, d))
    counts = jnp.clip(lim_ref[:, :LANE], 0, half).astype(F32)
    a, b = per_micro(counts)
    st_ref[16:17, :] = a
    st_ref[17:18, :] = b


def one_minus_exp(x):
    series = jnp.full(x.shape, 1.0 / 9.0, F32)
    for k in range(8, 0, -1):
        series = (1.0 - x * series) / k if k > 1 else 1.0 - x * series
    return jnp.where(x < 0.5, x * series, 1.0 - jnp.exp(-x))


def k_prepare(starts_ref, rate_ref, rotation_ref, gain_ref, shift_ref, skip_ref, bias_ref,
              keep_f_ref, keep_r_ref, kp_f_ref, kp_r_ref, kd_f_ref, kd_r_ref, par_ref, vec_ref):
    rows, segments = starts_ref.shape
    steps = keep_f_ref.shape[0] // SUB
    n = kd_f_ref.shape[0]
    length = 2 * steps
    sub = lax.broadcasted_iota(jnp.int32, (SUB, LANE), 0)
    starts = []
    for k in range(segments):
        start = jnp.zeros((SUB, LANE), jnp.int32)
        for r in range(rows):
            start = jnp.where(sub // 2 == r, starts_ref[r, k], start)
        starts.append(start)
    base = lax.axis_index("tm") * length + (sub % 2) * steps
    block = 8

    def fill(i, least):
        t = lax.broadcasted_iota(jnp.int32, (block, SUB, LANE), 0) + i * block
        place = t + base[None]
        here = starts[0][None] == place
        following = starts[0][None] == place + 1
        for start in starts[1:]:
            here = here | (start[None] == place)
            following = following | (start[None] == place + 1)
        following = following | (place == n * length - 1)
        here = jnp.where(here, 0.0, 1.0)
        following = jnp.where(following, 0.0, 1.0)
        at = pl.ds(pl.multiple_of(i * block * SUB, SUB), block * SUB)
        keep_f_ref[at, :] = flat(here)
        keep_r_ref[at, :] = flat(following)
        return (jnp.minimum(least[0], jnp.min(here, axis=0)), jnp.minimum(least[1], jnp.min(following, axis=0)))

    ones = jnp.ones((SUB, LANE), F32)
    least = lax.fori_loop(0, steps // block, fill, (ones, ones))
    kp_f_ref[...], kp_r_ref[...] = least

    def fill_devices(j, unused):
        first = j * length
        forward = jnp.zeros((SUB, LANE), jnp.bool_)
        backward = jnp.zeros((SUB, LANE), jnp.bool_)
        for start in starts:
            forward = forward | ((start >= first) & (start < first + length))
            backward = backward | ((start > first) & (start <= first + length))
        kd_f_ref[j] = jnp.where(forward, 0.0, 1.0)
        kd_r_ref[j] = jnp.where(backward, 0.0, 1.0)
        return unused

    lax.fori_loop(0, n, fill_devices, 0)
    for layer in range(2):
        decay = jnp.exp(rate_ref[layer : layer + 1, :])
        magnitude = jnp.exp(-decay)
        angle = rotation_ref[layer : layer + 1, :]
        re, im = magnitude * jnp.cos(angle), magnitude * jnp.sin(angle)
        at = layer * SUB
        norm_in = jnp.sqrt(one_minus_exp(2.0 * decay))
        par_ref[at : at + 1, :] = re
        par_ref[at + 1 : at + 2, :] = im
        for unused in range(steps.bit_length() - 1):
            re, im = times(re, im, re, im)
        par_ref[at + 2 : at + 3, :] = re
        par_ref[at + 3 : at + 4, :] = im
        re, im = times(re, im, re, im)
        par_ref[at + 4 : at + 5, :] = re
        par_ref[at + 5 : at + 6, :] = im
        par_ref[at + 6 : at + 7, :] = norm_in
        par_ref[at + 7 : at + 8, :] = decay
        vec_ref[at : at + SUB, :] = jnp.zeros((SUB, vec_ref.shape[1]), F32)
        for k, ref in enumerate((gain_ref, shift_ref, skip_ref, bias_ref)):
            vec_ref[at + k : at + k + 1, :] = ref[layer : layer + 1, :]


def of_layer(ref, layer):
    return ref.at[layer * SUB : (layer + 1) * SUB]


def k_combine(layer, reverse, conj, e_ref, other_ref, kd_ref, par_ref, out_ref):
    par_ref = of_layer(par_ref, layer)
    width = par_ref.shape[1]
    chip, core = chip_and_core()
    keep = wide(kd_ref[2 * chip + (0 if reverse else 1)], width)
    lr = keep * par_ref[4:5, :]
    li = keep * par_ref[5:6, :] * (-1.0 if conj else 1.0)
    is_first = core == (1 if reverse else 0)
    e, other = e_ref[...], other_ref[...]
    pick = jnp.where(is_first, 1.0, 0.0)
    first = other + pick * (e - other)
    last = e + pick * (other - e)
    qr, qi = times(lr, li, first[:, :width], first[:, width:])
    out_ref[...] = jnp.concatenate((qr, qi), axis=1) + last


def k_drive(layer, reverse, st_ref, cnt_ref, u_ref, lim_ref, vec_ref, par_ref, b_ref, keep_ref, kp_ref,
            d_ref, ml_ref, stat_ref, e_ref):
    vec_ref, par_ref = of_layer(vec_ref, layer), of_layer(par_ref, layer)
    total = st_ref[...]
    a, c, b, d = unpack_rows(total, 4, u_ref.shape[1])
    if cnt_ref is None:
        counts = (total[16:17, :], total[17:18, :])
    else:
        counts = (cnt_ref[28:29, :LANE], cnt_ref[29:30, :LANE])
    parts = []
    for summed, squares, count in ((a, c, counts[0]), (b, d, counts[1])):
        inverse = 1.0 / wide(count, u_ref.shape[1])
        center = summed * inverse
        spread = squares * inverse - center * center
        parts.append((center, spread, lax.rsqrt(spread + epsilon), inverse))
    stat_ref[0:8, :] = by_micro(parts[0][0], parts[1][0])
    stat_ref[8:16, :] = by_micro(parts[0][2], parts[1][2])
    stat_ref[16:24, :] = by_micro(parts[0][3], parts[1][3])
    stat_ref[24:25, :] = parts[0][0]
    stat_ref[25:26, :] = parts[1][0]
    stat_ref[26:27, :] = parts[0][1]
    stat_ref[27:28, :] = parts[1][1]
    stat_ref[28:29, :] = wide(counts[0], u_ref.shape[1])
    stat_ref[29:30, :] = wide(counts[1], u_ref.shape[1])
    stat_ref[30:32, :] = jnp.zeros((2, u_ref.shape[1]), F32)
    both = jnp.concatenate((par_ref[6:7, :], par_ref[6:7, :]), axis=1)

    def step(i, unused):
        low = flat(masked_tile(u_ref, stat_ref, vec_ref, lim_ref, i)).astype(BF16)
        ml_ref[rows_at(i), :] = low
        d_ref[rows_at(i), :] = dot(low, b_ref[layer]) * both
        return unused

    lax.fori_loop(0, u_ref.shape[0] // TILE, step, 0)
    re, im, unused = scan(d_ref, keep_ref, par_ref, zeros_state(par_ref), reverse, False)
    put_ends(e_ref, chunk_end((re, im), kp_ref, par_ref, reverse, False))


def k_drive_first(layer, reverse, st_ref, *refs):
    k_drive(layer, reverse, st_ref, None, *refs)


def run_states(carry, d_ref, keep_ref, kp_ref, kd_ref, par_ref, s_ref, reverse):
    width = par_ref.shape[1]
    first = 0 if reverse else SUB
    start = enter(*carry, kd_ref, kp_ref, par_ref, reverse, False)
    s_ref[(s_ref.shape[0] - SUB if reverse else 0) : (s_ref.shape[0] if reverse else SUB), :] = (
        jnp.concatenate(start, axis=1)
    )

    def visit(t, keep, states, extra):
        at = pl.ds(pl.multiple_of(t * SUB + first, SUB), SUB)
        for j, (re, im) in enumerate(states):
            s_ref[at, j * LANE : (j + 1) * LANE] = re
            s_ref[at, width + j * LANE : width + (j + 1) * LANE] = im
        return extra

    scan(d_ref, keep_ref, par_ref, start, reverse, False, visit)
    return first


def gelu_parts(x):
    cdf = 0.5 * (1.0 + lax.erf(x * 0.7071067811865476))
    return x * cdf, cdf + x * jnp.exp(-0.5 * x * x) * 0.3989422804014327


def states_low(s_ref, first, i):
    return s_ref[pl.ds(pl.multiple_of(i * TILE + first, SUB), TILE), :].astype(BF16)


def take_carry(refs, parts):
    return (refs[:parts], refs[parts], refs[parts + 1], refs[-1]), refs[parts + 2 : -1]


def k_finish_first(layer, parts, *refs):
    carry, refs = take_carry(refs, parts)
    (d_ref, u_ref, stat_ref, lim_ref, vec_ref, par_ref, keep_ref, kp_ref, kd_ref, c_ref, w_ref,
     s_ref, al_ref, sig_ref, q_ref, slope_ref, next_ref, st_ref) = refs
    vec_ref, par_ref = of_layer(vec_ref, layer), of_layer(par_ref, layer)
    first = run_states(carry, d_ref, keep_ref, kp_ref, kd_ref, par_ref, s_ref, False)

    def step(i, sums):
        at = rows_at(i)
        valid = tile_mask(lim_ref, i)
        masked = masked_tile(u_ref, stat_ref, vec_ref, lim_ref, i)
        mixed = dot(states_low(s_ref, first, i), c_ref[layer]) + vec_ref[2:3, :] * flat(masked)
        active, slope = gelu_parts(mixed)
        low = active.astype(BF16)
        sig = jax.nn.sigmoid(dot(low, w_ref[layer]) + vec_ref[3:4, :])
        gated = active * sig
        al_ref[at, :] = low
        sig_ref[at, :] = sig
        slope_ref[at, :] = slope
        q_ref[at, :] = gated * (1.0 - sig)
        fresh = folded(u_ref[at, :]) + jnp.where(valid, folded(gated), 0.0)
        next_ref[at, :] = flat(fresh)
        x = jnp.where(valid, fresh, 0.0)
        return (sums[0] + jnp.sum(x, axis=0), sums[1] + jnp.sum(x * x, axis=0))

    zero = jnp.zeros(lim_ref.shape, F32)
    sums, squares = lax.fori_loop(0, u_ref.shape[0] // TILE, step, (zero, zero))
    a, b = per_micro(sums)
    c, d = per_micro(squares)
    pack_rows(st_ref, (a, c, b, d))


def gate_backward(layer, upstream, q, sig, slope, low, masked, s_low, state, c_ref, w_ref, mix_ref, sg_ref, wc_ref, i):
    at = rows_at(i)
    gate = (upstream * q).astype(BF16)
    wc_ref[: gate.shape[1], :] += dot_tn(low, gate)
    act = upstream * sig + dot_nt(gate, w_ref[layer])
    mix = (act * slope).astype(BF16)
    mix_ref[at, :] = mix
    wc_ref[gate.shape[1] :, :] += dot_tn(s_low, mix)
    sg = dot_nt(mix, c_ref[layer])
    sg_ref[at, :] = sg
    wide_sum = jnp.sum(folded(sg * state), axis=0)
    half = wide_sum.shape[1] // 2
    return (
        jnp.sum(folded(gate.astype(F32)), axis=0),
        jnp.sum(folded(mix.astype(F32) * masked), axis=0),
        wide_sum[:, :half] + wide_sum[:, half:],
    )


def put_sums(sums_ref, sums):
    sums_ref[...] = jnp.zeros(sums_ref.shape, F32)
    pack_rows(sums_ref, [jnp.sum(part, axis=0, keepdims=True) for part in sums])


def zero_sums(width, states):
    return (jnp.zeros((SUB, width), F32), jnp.zeros((SUB, width), F32), jnp.zeros((SUB, states), F32))


def k_middle(layer, parts, *refs):
    carry, refs = take_carry(refs, parts)
    (d_ref, u_ref, stat_ref, lim_ref, vec_ref, par_ref, keep_ref, kp_ref, kd_ref,
     keep_adj_ref, kp_adj_ref, c_ref, w_ref, cot_ref,
     out_ref, s_ref, cot32_ref, mix_ref, sg_ref, wc_ref, sums_ref, e_ref, lines_ref) = refs
    vec_ref, par_ref = of_layer(vec_ref, layer), of_layer(par_ref, layer)
    spread_in(cot_ref, cot32_ref, lines_ref)
    first = run_states(carry, d_ref, keep_ref, kp_ref, kd_ref, par_ref, s_ref, True)
    wc_ref[...] = jnp.zeros(wc_ref.shape, F32)

    def step(i, sums):
        at = rows_at(i)
        valid = tile_mask(lim_ref, i)
        masked = flat(masked_tile(u_ref, stat_ref, vec_ref, lim_ref, i))
        state = s_ref[pl.ds(pl.multiple_of(i * TILE + first, SUB), TILE), :]
        s_low = state.astype(BF16)
        mixed = dot(s_low, c_ref[layer]) + vec_ref[2:3, :] * masked
        active, slope = gelu_parts(mixed)
        low = active.astype(BF16)
        sig = jax.nn.sigmoid(dot(low, w_ref[layer]) + vec_ref[3:4, :])
        gated = active * sig
        put_lines(lines_ref, i, flat(folded(u_ref[at, :]) + jnp.where(valid, folded(gated), 0.0)))
        upstream = flat(jnp.where(valid, folded(cot32_ref[at, :]), 0.0))
        more = gate_backward(layer, upstream, gated * (1.0 - sig), sig, slope, low, masked, s_low, state,
                             c_ref, w_ref, mix_ref, sg_ref, wc_ref, i)
        return tuple(x + y for x, y in zip(sums, more))

    sums = lax.fori_loop(0, u_ref.shape[0] // TILE, step, zero_sums(u_ref.shape[1], par_ref.shape[1]))
    put_sums(sums_ref, sums)
    spread_out(lines_ref, out_ref)
    re, im, unused = scan(sg_ref, keep_adj_ref, par_ref, zeros_state(par_ref), False, True)
    put_ends(e_ref, chunk_end((re, im), kp_adj_ref, par_ref, False, True))


def k_lower(layer, st_ref, z_ref, cot32_ref, u1_ref, stat1_ref, lim_ref,
            s_ref, al_ref, sig_ref, q_ref, slope_ref, u_ref, stat_ref, vec_ref, par_ref, c_ref, w_ref,
            keep_adj_ref, kp_adj_ref,
            grad_ref, mix_ref, sg_ref, wc_ref, sums_ref, e_ref, bn_ref):
    vec1_ref = of_layer(vec_ref, layer + 1)
    vec_ref, par_ref = of_layer(vec_ref, layer), of_layer(par_ref, layer)
    first = SUB
    c1, c2 = norm_sums(st_ref, stat1_ref, vec1_ref, bn_ref)
    wc_ref[...] = jnp.zeros(wc_ref.shape, F32)

    def step(i, sums):
        at = rows_at(i)
        valid = tile_mask(lim_ref, i)
        extra = norm_backward(z_ref, u1_ref, stat1_ref, vec1_ref, c1, c2, valid, i)
        grad = folded(cot32_ref[at, :]) + extra
        grad_ref[at, :] = flat(grad)
        upstream = flat(jnp.where(valid, grad, 0.0))
        masked = flat(masked_tile(u_ref, stat_ref, vec_ref, lim_ref, i))
        state = s_ref[pl.ds(pl.multiple_of(i * TILE + first, SUB), TILE), :]
        more = gate_backward(layer, upstream, q_ref[at, :], sig_ref[at, :], slope_ref[at, :], al_ref[at, :], masked,
                             state.astype(BF16), state, c_ref, w_ref, mix_ref, sg_ref, wc_ref, i)
        return tuple(x + y for x, y in zip(sums, more))

    sums = lax.fori_loop(0, u_ref.shape[0] // TILE, step, zero_sums(u_ref.shape[1], par_ref.shape[1]))
    put_sums(sums_ref, sums)
    re, im, unused = scan(sg_ref, keep_adj_ref, par_ref, zeros_state(par_ref), True, True)
    put_ends(e_ref, chunk_end((re, im), kp_adj_ref, par_ref, True, True))


def norm_sums(st_ref, stat_ref, vec_ref, bn_ref):
    width = vec_ref.shape[1]
    a, c, b, d = unpack_rows(st_ref[...], 4, width)
    bn_ref[...] = jnp.concatenate((a + b, c + d, jnp.zeros((6, width), F32)), axis=0)
    gain = vec_ref[0:1, :]
    inverse = stat_ref[16:24, :]
    return by_micro(a * gain, b * gain) * inverse, by_micro(c * gain, d * gain) * inverse


def norm_backward(z_ref, u_ref, stat_ref, vec_ref, c1, c2, valid, i):
    normed = normed_tile(u_ref, stat_ref, i)
    z = folded(z_ref[rows_at(i), :]) * vec_ref[0:1, :][None]
    return jnp.where(valid, stat_ref[8:16, :][None] * (z - c1[None] - normed * c2[None]), 0.0)


def k_adjoint(layer, reverse, parts, extra, *refs):
    carry, refs = take_carry(refs, parts)
    sent_refs, refs = refs[:extra], refs[extra:]
    (sg_ref, s_ref, mix_ref, ml_ref, u_ref, stat_ref, lim_ref, vec_ref, par_ref,
     keep_adj_ref, kp_adj_ref, kd_adj_ref, keep_ref, b_ref, z_ref, gb_ref, lg_ref, st_ref, a_ref) = refs
    vec_ref, par_ref = of_layer(vec_ref, layer), of_layer(par_ref, layer)
    width = par_ref.shape[1]
    tiles = width // LANE
    behind = 0 if reverse else SUB
    start = enter(*carry, kd_adj_ref, kp_adj_ref, par_ref, reverse, True)
    scale = [jnp.broadcast_to(par_ref[6:7, j * LANE : (j + 1) * LANE], (SUB, LANE)) for j in range(tiles)]

    def visit(t, unused, adjoint, sums):
        at = pl.ds(pl.multiple_of(t * SUB, SUB), SUB)
        before = pl.ds(pl.multiple_of(t * SUB + behind, SUB), SUB)
        keep = keep_ref[at, :]
        fresh = []
        for j, (re, im) in enumerate(adjoint):
            a_ref[at, j * LANE : (j + 1) * LANE] = re * scale[j]
            a_ref[at, width + j * LANE : width + (j + 1) * LANE] = im * scale[j]
            pr = s_ref[before, j * LANE : (j + 1) * LANE]
            pi = s_ref[before, width + j * LANE : width + (j + 1) * LANE]
            kr, ki = keep * re, keep * im
            fresh.append((sums[j][0] + (kr * pr + ki * pi), sums[j][1] + (ki * pr - kr * pi)))
        return tuple(fresh)

    zero = jnp.zeros((SUB, LANE), F32)
    unused, unused, sums = scan(sg_ref, keep_adj_ref, par_ref, start, reverse, True, visit,
                                tuple((zero, zero) for j in range(tiles)))
    lg_ref[...] = jnp.zeros(lg_ref.shape, F32)
    pack_rows(lg_ref, [
        jnp.sum(jnp.concatenate([part[k] for part in sums], axis=1), axis=0, keepdims=True) for k in range(2)
    ])
    gb_ref[...] = jnp.zeros(gb_ref.shape, F32)

    def step(i, sums):
        at = rows_at(i)
        drive = a_ref[at, :].astype(BF16)
        gb = dot_tn(ml_ref[at, :], drive)
        rows = gb.shape[0]
        gb_ref[:rows, :] += gb[:, :rows]
        gb_ref[rows:, : rows // 2] += gb[: rows // 2, rows:]
        gb_ref[rows:, rows // 2 :] += gb[rows // 2 :, rows:]
        back = dot_nt(drive, b_ref[layer]) + vec_ref[2:3, :] * mix_ref[at, :].astype(F32)
        z = jnp.where(tile_mask(lim_ref, i), folded(back), 0.0)
        z_ref[at, :] = flat(z)
        return (sums[0] + jnp.sum(z, axis=0), sums[1] + jnp.sum(z * normed_tile(u_ref, stat_ref, i), axis=0))

    zero = jnp.zeros(lim_ref.shape, F32)
    sums = lax.fori_loop(0, u_ref.shape[0] // TILE, step, (zero, zero))
    a, b = per_micro(sums[0])
    c, d = per_micro(sums[1])
    pack_rows(st_ref, (a, c, b, d))
    at = 16
    if extra:
        for ref in sent_refs + (lg_ref,):
            st_ref[at : at + ref.shape[0], :] = ref[...]
            at += ref.shape[0]


def k_output(st_ref, z_ref, grad_ref, u_ref, stat_ref, vec_ref, lim_ref, par_ref, stat1_ref, bn1_ref,
             run_mean_ref, run_var_ref,
             out_ref, gain_ref, shift_ref, skip_ref, bias_ref, rate_ref, rotation_ref, mean_ref, var_ref,
             bn_ref, lines_ref):
    vec0_ref = of_layer(vec_ref, 0)
    c1, c2 = norm_sums(st_ref, stat_ref, vec0_ref, bn_ref)

    def step(i, unused):
        extra = norm_backward(z_ref, u_ref, stat_ref, vec0_ref, c1, c2, tile_mask(lim_ref, i), i)
        put_lines(lines_ref, i, grad_ref[rows_at(i), :] + flat(extra))
        return unused

    lax.fori_loop(0, u_ref.shape[0] // TILE, step, 0)
    spread_out(lines_ref, out_ref)
    width, states = gain_ref.shape[1], rate_ref.shape[1]
    per, per_state = width // LANE, states // LANE

    def line(at, count):
        return jnp.concatenate([st_ref[at + j : at + j + 1, :] for j in range(count)], axis=1)

    for layer, (stats_ref, norms_ref) in enumerate(((stat_ref, bn_ref), (stat1_ref, bn1_ref))):
        row = slice(layer, layer + 1)
        at = 40 - 24 * layer
        bias_ref[row, :] = line(at, per)
        skip_ref[row, :] = line(at + per, per)
        product = line(at + 2 * per, per_state)
        grad_re, grad_im = line(at + 16, per_state), line(at + 16 + per_state, per_state)
        par = of_layer(par_ref, layer)
        lam_re, lam_im, norm_in, decay = par[0:1, :], par[1:2, :], par[6:7, :], par[7:8, :]
        rotation_ref[row, :] = lam_re * grad_im - lam_im * grad_re
        rate_ref[row, :] = decay * (
            product * jnp.exp(-2.0 * decay) / (norm_in * norm_in) - (lam_re * grad_re + lam_im * grad_im)
        )
        shift_ref[row, :] = norms_ref[0:1, :]
        gain_ref[row, :] = norms_ref[1:2, :]
        mean, var = run_mean_ref[row, :], run_var_ref[row, :]
        for micro in range(2):
            mean = (1.0 - momentum) * mean + momentum * stats_ref[24 + micro : 25 + micro, :]
            var = (1.0 - momentum) * var + momentum * stats_ref[26 + micro : 27 + micro, :]
        mean_ref[row, :] = mean
        var_ref[row, :] = var


def k_split(side, x_ref, give_ref):
    half = give_ref.shape[0]
    give_ref[...] = x_ref[pl.ds(pl.multiple_of((1 - side()) * half, SUB), half), :]


def k_fold(before, side, kept_ref, got_ref, give_ref, keep_ref):
    half = give_ref.shape[0]
    base = 0 if before is None else before() * got_ref.shape[0]
    mine = side()
    for ref, at in ((give_ref, (1 - mine) * half), (keep_ref, mine * half)):
        here = kept_ref[pl.ds(pl.multiple_of(base + at, SUB), half), :]
        ref[...] = here + got_ref[pl.ds(pl.multiple_of(at, SUB), half), :]


def k_join(side, own_ref, got_ref, out_ref):
    half = own_ref.shape[0]
    mine = side()
    out_ref[pl.ds(pl.multiple_of(mine * half, SUB), half), :] = own_ref[...]
    out_ref[pl.ds(pl.multiple_of((1 - mine) * half, SUB), half), :] = got_ref[...]


def k_maps(side, wc1_ref, own_ref, got_ref, w_ref, c_ref, wc_ref):
    k_join(side, own_ref, got_ref, wc_ref)
    width = w_ref.shape[1]
    for layer, ref in enumerate((wc_ref, wc1_ref)):
        w_ref[layer] = ref[:width, :]
        c_ref[layer] = ref[width:, :]


def k_drives(side, b1_ref, own_ref, got_ref, out_ref, b_ref):
    k_join(side, own_ref, got_ref, b_ref)
    width = out_ref.shape[1]
    for layer, ref in enumerate((b_ref, b1_ref)):
        out_ref[layer, :, :width] = ref[:width, :]
        out_ref[layer, : width // 2, width:] = ref[width:, : width // 2]
        out_ref[layer, width // 2 :, width:] = ref[width:, width // 2 :]


BOTH = ("batch", "tm")

TAIL = "s D A s C D B s D C A s D B s leave C D A D B C D A C D B C D A C B".replace("leave", "L")


def outer_bits():
    nb, nt = lax.axis_size("batch"), lax.axis_size("tm")
    return [("batch", 1 << k, nt << k) for k in range(nb.bit_length() - 1)]


def line_bits():
    return [("tm", 1 << k, 1 << k) for k in range(1, lax.axis_size("tm").bit_length() - 1)]


def swap(block, distance):
    total = lax.axis_size("batch") * lax.axis_size("tm")
    return lax.ppermute(block, BOTH, [(i, i ^ distance) for i in range(total)])


def swap_by_core(block, even, odd):
    total = lax.axis_size("batch") * lax.axis_size("tm")
    return lax.ppermute(block, BOTH, [(i, i ^ (odd if i & 1 else even)) for i in range(total)])


def sum_over(block, bits):
    if len(bits) == 2:
        near, far = bits[0][2], bits[1][2]
        others = [swap(block, distance | 1) for distance in (near, far, near | far)]
        return (block + others[0]) + (others[1] + others[2])
    for unused, unused, distance in bits:
        block = block + swap(block, distance | 1)
    return block


def sums_of_all(block, order=None, between=()):
    stages = [lambda block: block + swap(block, 1), lambda block: sum_over(block, outer_bits()),
              lambda block: sum_over(block, line_bits())]
    for k, stage in enumerate(stages):
        if order is not None:
            block, = order(block)
        block = stage(block)
        if k < len(between):
            between[k]()
    if order is not None:
        order.token = block
    return block


def carries(e, kd, par, layer, reverse, conj):
    other = swap(e, 1)
    block, = call("combine", functools.partial(k_combine, layer, reverse, conj), [shaped(e.shape)], [e, other, kd, par])
    bits = line_bits()
    if len(bits) == 2:
        near, far = bits[0][2], bits[1][2]
        return [block] + [swap(block, distance | 1) for distance in (near, far, near | far)] + [e, other]
    for unused, unused, distance in bits:
        block = jnp.concatenate((block, swap(block, distance | 1)), axis=0)
    return [block, e, other]


def bit_of(axis, bit):
    return lax.div(lax.axis_index(axis), bit) % 2


def plan(rows):
    outer, line = outer_bits(), line_bits()
    is_odd = functools.partial(bit_of, "tm", 1)
    steps = [(is_odd, lambda block: swap(block, 1))]
    for even, odd in zip(outer, outer[::-1]):
        def side(even=even, odd=odd):
            return jnp.where(is_odd() == 1, bit_of(odd[0], odd[1]), bit_of(even[0], even[1]))

        steps.append((side, functools.partial(swap_by_core, even=even[2], odd=odd[2])))
    for axis, bit, distance in line:
        steps.append((functools.partial(bit_of, axis, bit), functools.partial(swap, distance=distance)))
    cuts = 0
    while cuts < len(steps) and rows % (SUB << (cuts + 1)) == 0 and cuts < 4:
        cuts += 1
    return steps[:cuts], [exchange for unused, exchange in steps[cuts:]]


class Order:
    def __init__(self):
        self.token = None

    def __call__(self, *values):
        if self.token is None:
            return values
        tied = lax.optimization_barrier(tuple(values) + (self.token,))
        return tied[:-1]


class Large:
    def __init__(self, order, block):
        self.order = order
        self.rows, self.width = block.shape
        self.cuts, self.whole = plan(self.rows)
        self.block = block
        self.at = 0
        self.got = None

    def half(self):
        return shaped((self.rows >> (self.at + 1), self.width))

    def send(self):
        cuts, at = self.cuts, self.at
        count = len(cuts)
        if at == 0:
            self.block, = self.order(self.block)
        else:
            self.block, self.got = self.order(self.block, self.got)
        if at < count:
            side, exchange = cuts[at]
            if at == 0:
                give, = call("split", functools.partial(k_split, side), [self.half()], [self.block])
            else:
                before = cuts[0][0] if at == 1 else None
                give, self.block = call(
                    "fold", functools.partial(k_fold, before, side), [self.half()] * 2, [self.block, self.got]
                )
        elif at <= count + len(self.whole):
            give = self.block = self.block + self.got
            exchange = (self.whole + [step[1] for step in cuts[::-1]])[at - count]
        else:
            back = at - count - len(self.whole)
            give = self.block = self.joined()
            exchange = cuts[count - 1 - back][1]
        self.order.token = give
        self.got = exchange(give)
        self.at += 1

    def joined(self):
        rows, width = self.block.shape
        side = self.cuts[len(self.cuts) - 1 - (self.at - 1 - len(self.cuts) - len(self.whole))][0]
        out, = call("join", functools.partial(k_join, side), [shaped((2 * rows, width))], [self.block, self.got])
        return out

    def result(self):
        self.block, self.got = self.order(self.block, self.got)
        self.block = self.joined()
        self.order.token = self.block
        return self.block

    def left(self):
        return 2 * len(self.cuts) + len(self.whole) - self.at


def sum_slowly(order, block):
    for distance in [1] + [bit[2] | 1 for bit in outer_bits() + line_bits()]:
        block, = order(block)
        got = swap(block, distance)
        yield None
        block, got = order(block, got)
        block = block + got
        order.token = block
    yield block


def local(tokens, starts, lengths, cotangent, norm_gain, norm_shift, b_proj, log_rate, rotation, c_proj, skip_gain,
          w_gate, gate_bias, run_mean, run_var):
    rows, length, width = tokens.shape
    states = log_rate.shape[1]
    count = rows * length
    n = lax.axis_size("tm")
    chips = n // 2
    parts = 4 if chips == 4 else 1

    big = lambda w, dtype=F32: shaped((count, w), dtype)
    ends = shaped((SUB, 2 * states))
    kept = shaped((count + SUB, 2 * states))
    small = shaped((16, LANE))
    lines = pltpu.VMEM((width // LANE, count, LANE), F32)
    everyone = pltpu.VMEM((chips, SUB, 2 * states), F32)
    keeps = shaped((count, LANE))
    vector, state_vector = shaped((2, width)), shaped((2, states))

    u0, st, lim = call("enter", k_input, [big(width), shaped((24, LANE)), shaped((SUB, width), jnp.int32)],
                       [lengths, tokens], scratch=[lines], scalars=1)
    keep_f, keep_r, kp_f, kp_r, kd_f, kd_r, par, vec = call(
        "prepare", k_prepare,
        [keeps, keeps, shaped((SUB, LANE)), shaped((SUB, LANE)), shaped((n, SUB, LANE)), shaped((n, SUB, LANE)),
         shaped((2 * SUB, states)), shaped((2 * SUB, width))],
        [starts, log_rate, rotation, norm_gain, norm_shift, skip_gain, gate_bias], scalars=1,
    )
    st = sums_of_all(st)
    d0, ml0, stat0, e = call(
        "drive0", functools.partial(k_drive_first, 0, False),
        [big(2 * states), big(width, BF16), shaped((32, width)), ends],
        [st, u0, lim, vec, par, b_proj, keep_f, kp_f],
    )
    s0, al0, sig0, q0, slope0, u1, st = call(
        "finish0", functools.partial(k_finish_first, 0, parts),
        [kept, big(width, BF16), big(width), big(width), big(width), big(width), small],
        carries(e, kd_f, par, 0, False, False)
        + [d0, u0, stat0, lim, vec, par, keep_f, kp_f, kd_f, c_proj, w_gate],
        scratch=[everyone],
    )
    st = sums_of_all(st)
    d1, ml1, stat1, e = call(
        "drive1", functools.partial(k_drive, 1, True),
        [big(2 * states), big(width, BF16), shaped((32, width)), ends],
        [st, stat0, u1, lim, vec, par, b_proj, keep_r, kp_r],
    )
    grads = [shaped((width + 2 * states, width)), small, ends]
    output, s1, cot32, mix1, sg1, wc1, sums1, e = call(
        "middle", functools.partial(k_middle, 1, parts),
        [shaped(tokens.shape, BF16), kept, big(width), big(width, BF16), big(2 * states)] + grads,
        carries(e, kd_r, par, 1, True, False)
        + [d1, u1, stat1, lim, vec, par, keep_r, kp_r, kd_r, keep_f, kp_f, c_proj, w_gate, cotangent],
        scratch=[lines, everyone], results=1,
    )
    order = Order()
    wc1 = Large(order, wc1)
    wc1.send()
    got = carries(e, kd_f, par, 1, False, True)
    wc1.send()
    adjoint = [big(width), shaped((2 * states, width)), shaped((8, LANE))]
    z1, gb1, lg1, st = call(
        "adjoint1", functools.partial(k_adjoint, 1, False, parts, 0), adjoint + [small],
        list(order(*got)) + [sg1, s1, mix1, ml1, u1, stat1, lim, vec, par, keep_f, kp_f, kd_f, keep_r, b_proj],
        scratch=[pltpu.VMEM((count, 2 * states), F32), everyone],
    )
    order.token = st
    b1 = Large(order, gb1)
    st = sums_of_all(st, order, [b1.send, wc1.send, b1.send])
    g0, mix0, sg0, wc0, sums0, e, bn1 = call(
        "lower", functools.partial(k_lower, 0),
        [big(width), big(width, BF16), big(2 * states)] + grads + [shaped((8, width))],
        list(order(st)) + [z1, cot32, u1, stat1, lim, s0, al0, sig0, q0, slope0, u0, stat0, vec, par,
                           c_proj, w_gate, keep_r, kp_r],
    )
    order.token = e
    wc0 = Large(order, wc0)
    wc1.send()
    wc0.send()
    got = carries(e, kd_r, par, 0, True, True)
    b1.send()
    wc0.send()
    z0, gb0, lg0, st = call(
        "adjoint0", functools.partial(k_adjoint, 0, True, parts, 3), adjoint + [shaped((64, LANE))],
        list(order(*got)) + [sums1, lg1, sums0]
        + [sg0, s0, mix0, ml0, u0, stat0, lim, vec, par, keep_r, kp_r, kd_r, keep_f, b_proj],
        scratch=[pltpu.VMEM((count, 2 * states), F32), everyone],
    )
    order.token = st
    b0 = Large(order, gb0)
    small_sum = sum_slowly(order, st)
    queue = TAIL.split()
    returned = {}
    for item in queue:
        if item == "s":
            st = next(small_sum)
        elif item == "L":
            for unused in small_sum:
                st = unused if unused is not None else st
            (tokens_grad, grad_gain, grad_shift, grad_skip, grad_bias, grad_rate, grad_rotation, new_mean, new_var,
             bn0) = call(
                "leave", k_output,
                [shaped(tokens.shape), vector, vector, vector, vector, state_vector, state_vector, vector, vector,
                 shaped((SUB, width))],
                list(order(st)) + [z0, g0, u0, stat0, vec, lim, par, stat1, bn1, run_mean, run_var],
                scratch=[lines], results=9,
            )
            order.token = bn0
        else:
            large = {"A": wc1, "B": b1, "C": wc0, "D": b0}[item]
            if large.left():
                large.send()
            elif item in "AB":
                returned[item] = large.result()
    for large in (wc1, b1, wc0, b0):
        while large.left():
            large.send()
    wc1 = returned["A"] if "A" in returned else wc1.result()
    b1 = returned["B"] if "B" in returned else b1.result()
    last = wc0.cuts[0][0]
    wc0.block, wc0.got = order(wc0.block, wc0.got)
    grad_w, grad_c, unused = call(
        "maps", functools.partial(k_maps, last),
        [shaped((2, width, width)), shaped((2, 2 * states, width)), shaped((width + 2 * states, width))],
        [wc1, wc0.block, wc0.got], results=2,
    )
    order.token = unused
    b0.block, b0.got = order(b0.block, b0.got)
    grad_b, unused = call(
        "drives", functools.partial(k_drives, last),
        [shaped((2, width, 2 * states)), shaped((2 * states, width))],
        [b1, b0.block, b0.got], results=1,
    )
    return (output, tokens_grad, grad_gain, grad_shift, grad_b, grad_rate, grad_rotation, grad_c, grad_skip, grad_w,
            grad_bias, new_mean, new_var)


def solution(mesh):
    tokens_spec = P("batch", "tm", None)
    return jax.shard_map(
        local,
        mesh=mesh,
        in_specs=(tokens_spec, P("batch", None), P("batch"), tokens_spec) + (P(),) * 11,
        out_specs=(tokens_spec, tokens_spec) + (P(),) * 11,
        check_vma=False,
    )
```

```python
import functools
import math

import jax
import jax.numpy as jnp
from jax import lax
from jax.experimental import pallas as pl
from jax.experimental.pallas import tpu as pltpu
from jax.sharding import PartitionSpec as P

epsilon = 1e-05
momentum = 0.1
F32 = jnp.float32
BF16 = jnp.bfloat16

SUB = 8
LANE = 128
TILE = 256
WORK = 5 * 10**9


def in_vmem(count):
    return [pl.BlockSpec(memory_space=pltpu.VMEM)] * count


class Order:
    def __init__(self):
        self.token = None


def call(name, body, outs, args, scratch=(), scalars=0, results=0, order=None, token=0, far=(), alias=None, out_far=0, work=WORK):
    room = 6 * 1024 * 1024 + sum(4 * math.prod(item.shape) for item in list(scratch) + list(outs[:results]) if hasattr(item, "shape"))
    specs = [pl.BlockSpec(memory_space=pltpu.SMEM)] * scalars + in_vmem(len(args) - scalars)
    for k in far:
        specs[k] = pl.BlockSpec(memory_space=pltpu.HBM)
    count = len(args)
    args = list(args)
    run = body
    if order is not None and order.token is not None:
        args.append(order.token)
        specs.append(pl.BlockSpec(memory_space=pl.ANY))
        run = lambda *refs: body(*refs[:count], *refs[count + 1 :])
    out_specs = in_vmem(len(outs))
    for k in range(out_far):
        out_specs[k] = pl.BlockSpec(memory_space=pltpu.HBM)
    done = pl.pallas_call(
        run,
        name=name,
        out_shape=outs,
        in_specs=specs,
        out_specs=out_specs,
        scratch_shapes=list(scratch),
        input_output_aliases=alias or {},
        compiler_params=pltpu.CompilerParams(vmem_limit_bytes=room),
        cost_estimate=pl.CostEstimate(flops=work, bytes_accessed=1, transcendentals=0),
    )(*args)
    if order is not None:
        order.token = done[token]
    return done


def shaped(shape, dtype=F32):
    return jax.ShapeDtypeStruct(shape, dtype)


def tile_mask(lim_ref, i):
    steps = TILE // SUB
    t = lax.broadcasted_iota(jnp.int32, (steps,) + lim_ref.shape, 0) + i * steps
    return t < lim_ref[...][None]


def folded(values):
    return values.reshape((values.shape[0] // SUB, SUB, values.shape[1]))


def flat(values):
    return values.reshape((values.shape[0] * SUB, values.shape[2]))


def times(ar, ai, br, bi):
    return (ar * br - ai * bi, ar * bi + ai * br)


def scan(d_ref, keep_ref, par_ref, start, reverse, conj, visit=None, extra=(), unroll=8):
    width = par_ref.shape[1]
    count = d_ref.shape[0] // SUB
    tiles = width // LANE
    lam = []
    for j in range(tiles):
        lanes = slice(j * LANE, (j + 1) * LANE)
        lr = jnp.broadcast_to(par_ref[0:1, lanes], (SUB, LANE))
        li = jnp.broadcast_to(par_ref[1:2, lanes], (SUB, LANE))
        lam.append((lr, -li if conj else li))
    state = tuple(
        (start[0][:, j * LANE : (j + 1) * LANE], start[1][:, j * LANE : (j + 1) * LANE])
        for j in range(tiles)
    )

    def step(i, carry):
        state, extra = carry
        t = count - 1 - i if reverse else i
        at = pl.ds(pl.multiple_of(t * SUB, SUB), SUB)
        keep = keep_ref[at, :]
        fresh = []
        for j in range(tiles):
            re, im = state[j]
            a = keep * lam[j][0]
            b = keep * lam[j][1]
            dr = d_ref[at, j * LANE : (j + 1) * LANE]
            di = d_ref[at, width + j * LANE : width + (j + 1) * LANE]
            fresh.append((a * re - b * im + dr, a * im + b * re + di))
        fresh = tuple(fresh)
        if visit is not None:
            extra = visit(t, keep, fresh, extra)
        return (fresh, extra)

    state, extra = lax.fori_loop(0, count, step, (state, tuple(extra)), unroll=unroll)
    re = jnp.concatenate([part[0] for part in state], axis=1)
    im = jnp.concatenate([part[1] for part in state], axis=1)
    return re, im, extra


def wide(values, width):
    return jnp.concatenate([values] * (width // LANE), axis=1)


def chunk_end(ends, kp_ref, par_ref, reverse, conj):
    width = par_ref.shape[1]
    re, im = ends
    shift = SUB - 1 if reverse else 1
    pr, pi = pltpu.roll(re, shift, 0), pltpu.roll(im, shift, 0)
    keep = wide(kp_ref[...], width)
    lr = keep * par_ref[2:3, :]
    li = keep * par_ref[3:4, :]
    li = -li if conj else li
    qr, qi = times(lr, li, pr, pi)
    odd = lax.broadcasted_iota(jnp.int32, (SUB, width), 0) % 2
    last = odd == (0 if reverse else 1)
    return jnp.where(last, qr + re, re), jnp.where(last, qi + im, im)


def chip_and_core():
    me = lax.axis_index("tm")
    return me // 2, me % 2


def enter(got_refs, e_ref, other_ref, all_ref, kd_ref, kp_ref, par_ref, reverse, conj):
    width = par_ref.shape[1]
    chips = all_ref.shape[0]
    chip, core = chip_and_core()
    sign = -1.0 if conj else 1.0
    at = 0
    for ref in got_refs:
        for k in range(ref.shape[0] // SUB):
            all_ref[at] = ref[k * SUB : (k + 1) * SUB, :]
            at += 1
    lr, li = par_ref[4:5, :], sign * par_ref[5:6, :]
    cr, ci = times(lr, li, lr, li)
    lr, li, cr, ci = (jnp.broadcast_to(x, (SUB, width)) for x in (lr, li, cr, ci))

    def step(i, x):
        j = chips - 1 - i if reverse else i
        keep = wide(kd_ref[2 * j] * kd_ref[2 * j + 1], width)
        qr, qi = times(keep * cr, keep * ci, x[0], x[1])
        use = (j > chip) if reverse else (j < chip)
        use = jnp.where(use, 1.0, 0.0)
        k = jnp.bitwise_xor(j, chip)
        nr = qr + all_ref[k, :, :width]
        ni = qi + all_ref[k, :, width:]
        return (x[0] + use * (nr - x[0]), x[1] + use * (ni - x[1]))

    zero = jnp.zeros((SUB, width), F32)
    xr, xi = lax.fori_loop(0, chips, step, (zero, zero), unroll=chips <= 4)
    first = 1 if reverse else 0
    keep = wide(kd_ref[2 * chip + first], width)
    qr, qi = times(keep * lr, keep * li, xr, xi)
    use = jnp.where(core == first, 0.0, 1.0)
    xr = xr + use * (qr + other_ref[:, :width] - xr)
    xi = xi + use * (qi + other_ref[:, width:] - xi)
    near, far = (1, SUB - 1) if reverse else (SUB - 1, 1)
    sr, si = pltpu.roll(xr, near, 0), pltpu.roll(xi, near, 0)
    keep = wide(kp_ref[...], width)
    hr = keep * par_ref[2:3, :]
    hi = sign * keep * par_ref[3:4, :]
    tr, ti = times(hr, hi, sr, si)
    tr = pltpu.roll(tr + e_ref[:, :width], far, 0)
    ti = pltpu.roll(ti + e_ref[:, width:], far, 0)
    odd = lax.broadcasted_iota(jnp.int32, (SUB, width), 0) % 2
    second = odd == (0 if reverse else 1)
    return jnp.where(second, tr, sr), jnp.where(second, ti, si)


def put_ends(e_ref, ends):
    e_ref[...] = jnp.concatenate(ends, axis=1)


def zeros_state(par_ref):
    zero = jnp.zeros((SUB, par_ref.shape[1]), F32)
    return (zero, zero)


def per_micro(values):
    return (
        jnp.sum(values[0:4], axis=0, keepdims=True),
        jnp.sum(values[4:8], axis=0, keepdims=True),
    )


def pack_rows(out_ref, rows):
    at = 0
    for row in rows:
        for j in range(row.shape[1] // LANE):
            out_ref[at : at + 1, :] = row[:, j * LANE : (j + 1) * LANE]
            at += 1


def unpack_rows(values, count, width):
    tiles = width // LANE
    return [
        jnp.concatenate(
            [values[r * tiles + j : r * tiles + j + 1, :] for j in range(tiles)], axis=1
        )
        for r in range(count)
    ]


def by_micro(first, second):
    sub = lax.broadcasted_iota(jnp.int32, (SUB, first.shape[1]), 0)
    return jnp.where(sub < 4, jnp.broadcast_to(first, sub.shape), jnp.broadcast_to(second, sub.shape))


def dot(a, b):
    return jnp.dot(a, b, preferred_element_type=F32)


def dot_nt(a, b):
    return lax.dot_general(a, b, (((1,), (1,)), ((), ())), preferred_element_type=F32)


def dot_tn(a, b):
    return lax.dot_general(a, b, (((0,), (0,)), ((), ())), preferred_element_type=F32)


def normed_tile(u_ref, stat_ref, i):
    x = folded(u_ref[pl.ds(pl.multiple_of(i * TILE, TILE), TILE), :])
    return (x - stat_ref[0:8, :][None]) * stat_ref[8:16, :][None]


def masked_tile(u_ref, stat_ref, vec_ref, lim_ref, i):
    normed = normed_tile(u_ref, stat_ref, i)
    z = normed * vec_ref[0:1, :][None] + vec_ref[1:2, :][None]
    return jnp.where(tile_mask(lim_ref, i), z, 0.0)


def rows_at(i):
    return pl.ds(pl.multiple_of(i * TILE, TILE), TILE)


def spread_in(src_ref, dst_ref, lines_ref):
    half = src_ref.shape[1] // 2
    tiles = src_ref.shape[2] // LANE
    for s in range(SUB):
        part = src_ref[s // 2, (s % 2) * half : (s % 2 + 1) * half, :].astype(F32)
        for j in range(tiles):
            lines_ref[j, pl.ds(s, half, stride=SUB), :] = part[:, j * LANE : (j + 1) * LANE]
    for j in range(tiles):
        dst_ref[:, j * LANE : (j + 1) * LANE] = lines_ref[j]


def spread_out(lines_ref, dst_ref):
    half = dst_ref.shape[1] // 2
    tiles = dst_ref.shape[2] // LANE
    for s in range(SUB):
        for j in range(tiles):
            part = lines_ref[j, pl.ds(s, half, stride=SUB), :]
            dst_ref[s // 2, (s % 2) * half : (s % 2 + 1) * half, j * LANE : (j + 1) * LANE] = part.astype(dst_ref.dtype)


def put_lines(lines_ref, i, values):
    for j in range(lines_ref.shape[0]):
        lines_ref[j, rows_at(i), :] = values[:, j * LANE : (j + 1) * LANE]


def moment_sums(u_ref, lim_ref, upto):
    def step(i, sums):
        x = jnp.where(tile_mask(lim_ref, i), folded(u_ref[rows_at(i), :]), 0.0)
        return (sums[0] + jnp.sum(x, axis=0), sums[1] + jnp.sum(x * x, axis=0))

    zero = jnp.zeros(lim_ref.shape, F32)
    return lax.fori_loop(0, upto, step, (zero, zero))


def fill_lim(lengths_ref, lim_ref, half):
    sub = lax.broadcasted_iota(jnp.int32, lim_ref.shape, 0)
    length = jnp.zeros(lim_ref.shape, jnp.int32)
    for r in range(lengths_ref.shape[0]):
        length = jnp.where(sub // 2 == r, lengths_ref[r], length)
    lim_ref[...] = length - lax.axis_index("tm") * (2 * half) - (sub % 2) * half


def k_input(lengths_ref, tokens_ref, u_ref, st_ref, lim_ref, lines_ref):
    half = tokens_ref.shape[1] // 2
    fill_lim(lengths_ref, lim_ref, half)
    spread_in(tokens_ref, u_ref, lines_ref)
    sums, squares = moment_sums(u_ref, lim_ref, u_ref.shape[0] // TILE)
    a, b = per_micro(sums)
    c, d = per_micro(squares)
    st_ref[...] = jnp.zeros(st_ref.shape, F32)
    pack_rows(st_ref, (a, c, b, d))
    counts = jnp.clip(lim_ref[:, :LANE], 0, half).astype(F32)
    a, b = per_micro(counts)
    st_ref[16:17, :] = a
    st_ref[17:18, :] = b


def one_minus_exp(x):
    series = jnp.full(x.shape, 1.0 / 9.0, F32)
    for k in range(8, 0, -1):
        series = (1.0 - x * series) / k if k > 1 else 1.0 - x * series
    return jnp.where(x < 0.5, x * series, 1.0 - jnp.exp(-x))


def all_starts(starts_ref):
    rows, segments = starts_ref.shape
    sub = lax.broadcasted_iota(jnp.int32, (SUB, LANE), 0)
    starts = []
    for k in range(segments):
        start = jnp.zeros((SUB, LANE), jnp.int32)
        for r in range(rows):
            start = jnp.where(sub // 2 == r, starts_ref[r, k], start)
        starts.append(start)
    return starts


def k_keep(reverse, starts_ref, keep_ref, kp_ref, kd_ref):
    steps = keep_ref.shape[0] // SUB
    n = kd_ref.shape[0]
    length = 2 * steps
    starts = all_starts(starts_ref)
    sub = lax.broadcasted_iota(jnp.int32, (SUB, LANE), 0)
    base = lax.axis_index("tm") * length + (sub % 2) * steps + (1 if reverse else 0)
    block = 8

    def fill(i, least):
        place = lax.broadcasted_iota(jnp.int32, (block, SUB, LANE), 0) + i * block + base[None]
        hit = starts[0][None] == place
        for start in starts[1:]:
            hit = hit | (start[None] == place)
        if reverse:
            hit = hit | (place == n * length)
        keep = jnp.where(hit, 0.0, 1.0)
        keep_ref[pl.ds(pl.multiple_of(i * block * SUB, SUB), block * SUB), :] = flat(keep)
        return jnp.minimum(least, jnp.min(keep, axis=0))

    kp_ref[...] = lax.fori_loop(0, steps // block, fill, jnp.ones((SUB, LANE), F32))

    def fill_devices(j, unused):
        first = j * length + (1 if reverse else 0)
        hit = jnp.zeros((SUB, LANE), jnp.bool_)
        for start in starts:
            hit = hit | ((start >= first) & (start < first + length))
        kd_ref[j] = jnp.where(hit, 0.0, 1.0)
        return unused

    lax.fori_loop(0, n, fill_devices, 0)


def k_prepare(starts_ref, rate_ref, rotation_ref, gain_ref, shift_ref, skip_ref, bias_ref,
              keep_ref, kp_ref, kd_ref, par_ref, vec_ref):
    k_keep(False, starts_ref, keep_ref, kp_ref, kd_ref)
    doublings = (keep_ref.shape[0] // SUB).bit_length() - 1
    for layer in range(2):
        decay = jnp.exp(rate_ref[layer : layer + 1, :])
        magnitude = jnp.exp(-decay)
        angle = rotation_ref[layer : layer + 1, :]
        re, im = magnitude * jnp.cos(angle), magnitude * jnp.sin(angle)
        at = layer * SUB
        norm_in = jnp.sqrt(one_minus_exp(2.0 * decay))
        par_ref[at : at + 1, :] = re
        par_ref[at + 1 : at + 2, :] = im
        for unused in range(doublings):
            re, im = times(re, im, re, im)
        par_ref[at + 2 : at + 3, :] = re
        par_ref[at + 3 : at + 4, :] = im
        re, im = times(re, im, re, im)
        par_ref[at + 4 : at + 5, :] = re
        par_ref[at + 5 : at + 6, :] = im
        par_ref[at + 6 : at + 7, :] = norm_in
        par_ref[at + 7 : at + 8, :] = decay
        vec_ref[at : at + SUB, :] = jnp.zeros((SUB, vec_ref.shape[1]), F32)
        for k, ref in enumerate((gain_ref, shift_ref, skip_ref, bias_ref)):
            vec_ref[at + k : at + k + 1, :] = ref[layer : layer + 1, :]


def of_layer(ref, layer):
    return ref.at[layer * SUB : (layer + 1) * SUB]


def k_combine(layer, reverse, conj, e_ref, other_ref, kd_ref, par_ref, out_ref):
    par_ref = of_layer(par_ref, layer)
    width = par_ref.shape[1]
    chip, core = chip_and_core()
    keep = wide(kd_ref[2 * chip + (0 if reverse else 1)], width)
    lr = keep * par_ref[4:5, :]
    li = keep * par_ref[5:6, :] * (-1.0 if conj else 1.0)
    is_first = core == (1 if reverse else 0)
    e, other = e_ref[...], other_ref[...]
    pick = jnp.where(is_first, 1.0, 0.0)
    first = other + pick * (e - other)
    last = e + pick * (other - e)
    qr, qi = times(lr, li, first[:, :width], first[:, width:])
    out_ref[...] = jnp.concatenate((qr, qi), axis=1) + last


def k_drive(layer, reverse, st_ref, cnt_ref, u_ref, lim_ref, vec_ref, par_ref, b_ref, keep_ref, kp_ref,
            d_ref, ml_ref, stat_ref, e_ref):
    vec_ref, par_ref = of_layer(vec_ref, layer), of_layer(par_ref, layer)
    total = st_ref[...]
    a, c, b, d = unpack_rows(total, 4, u_ref.shape[1])
    if cnt_ref is None:
        counts = (total[16:17, :], total[17:18, :])
    else:
        counts = (cnt_ref[28:29, :LANE], cnt_ref[29:30, :LANE])
    parts = []
    for summed, squares, count in ((a, c, counts[0]), (b, d, counts[1])):
        inverse = 1.0 / wide(count, u_ref.shape[1])
        center = summed * inverse
        spread = squares * inverse - center * center
        parts.append((center, spread, lax.rsqrt(spread + epsilon), inverse))
    stat_ref[0:8, :] = by_micro(parts[0][0], parts[1][0])
    stat_ref[8:16, :] = by_micro(parts[0][2], parts[1][2])
    stat_ref[16:24, :] = by_micro(parts[0][3], parts[1][3])
    stat_ref[24:25, :] = parts[0][0]
    stat_ref[25:26, :] = parts[1][0]
    stat_ref[26:27, :] = parts[0][1]
    stat_ref[27:28, :] = parts[1][1]
    stat_ref[28:29, :] = wide(counts[0], u_ref.shape[1])
    stat_ref[29:30, :] = wide(counts[1], u_ref.shape[1])
    stat_ref[30:32, :] = jnp.zeros((2, u_ref.shape[1]), F32)
    both = jnp.concatenate((par_ref[6:7, :], par_ref[6:7, :]), axis=1)

    def step(i, unused):
        low = flat(masked_tile(u_ref, stat_ref, vec_ref, lim_ref, i)).astype(BF16)
        ml_ref[rows_at(i), :] = low
        d_ref[rows_at(i), :] = dot(low, b_ref[layer]) * both
        return unused

    lax.fori_loop(0, u_ref.shape[0] // TILE, step, 0, unroll=True)
    re, im, unused = scan(d_ref, keep_ref, par_ref, zeros_state(par_ref), reverse, False)
    put_ends(e_ref, chunk_end((re, im), kp_ref, par_ref, reverse, False))


def k_drive_first(layer, reverse, st_ref, *refs):
    k_drive(layer, reverse, st_ref, None, *refs)


def run_states(carry, d_ref, keep_ref, kp_ref, kd_ref, par_ref, s_ref, reverse):
    width = par_ref.shape[1]
    first = 0 if reverse else SUB
    start = enter(*carry, kd_ref, kp_ref, par_ref, reverse, False)
    s_ref[(s_ref.shape[0] - SUB if reverse else 0) : (s_ref.shape[0] if reverse else SUB), :] = (
        jnp.concatenate(start, axis=1)
    )

    def visit(t, keep, states, extra):
        at = pl.ds(pl.multiple_of(t * SUB + first, SUB), SUB)
        for j, (re, im) in enumerate(states):
            s_ref[at, j * LANE : (j + 1) * LANE] = re
            s_ref[at, width + j * LANE : width + (j + 1) * LANE] = im
        return extra

    scan(d_ref, keep_ref, par_ref, start, reverse, False, visit)
    return first


def sigmoid(x):
    return 0.5 + 0.5 * jnp.tanh(0.5 * x)


def gelu_parts(x):
    bell = jnp.exp(-0.5 * x * x)
    base = 1.0 + (0.3275911 * 0.7071067811865476) * jnp.abs(x)
    near = pl.reciprocal(base, approx=True)
    near = near * (2.0 - base * near)
    tail = near * (0.5 * 1.061405429) + (0.5 * -1.453152027)
    tail = tail * near + (0.5 * 1.421413741)
    tail = tail * near + (0.5 * -0.284496736)
    tail = tail * near + (0.5 * 0.254829592)
    tail = tail * near * bell
    cdf = jnp.where(x < 0.0, tail, 1.0 - tail)
    return x * cdf, cdf + (0.3989422804014327 * x) * bell


def states_low(s_ref, first, i):
    return s_ref[pl.ds(pl.multiple_of(i * TILE + first, SUB), TILE), :].astype(BF16)


def take_carry(refs, parts):
    return (refs[:parts], refs[parts], refs[parts + 1], refs[-1]), refs[parts + 2 : -1]


def k_finish_first(layer, parts, *refs):
    carry, refs = take_carry(refs, parts)
    (d_ref, u_ref, stat_ref, lim_ref, vec_ref, par_ref, keep_ref, kp_ref, kd_ref, c_ref, w_ref,
     s_ref, al_ref, sig_ref, q_ref, slope_ref, next_ref, st_ref) = refs
    vec_ref, par_ref = of_layer(vec_ref, layer), of_layer(par_ref, layer)
    first = run_states(carry, d_ref, keep_ref, kp_ref, kd_ref, par_ref, s_ref, False)

    def step(i, sums):
        at = rows_at(i)
        valid = tile_mask(lim_ref, i)
        masked = masked_tile(u_ref, stat_ref, vec_ref, lim_ref, i)
        mixed = dot(states_low(s_ref, first, i), c_ref[layer]) + vec_ref[2:3, :] * flat(masked)
        active, slope = gelu_parts(mixed)
        low = active.astype(BF16)
        sig = sigmoid(dot(low, w_ref[layer]) + vec_ref[3:4, :])
        gated = active * sig
        al_ref[at, :] = low
        sig_ref[at, :] = sig
        slope_ref[at, :] = slope
        q_ref[at, :] = gated * (1.0 - sig)
        fresh = folded(u_ref[at, :]) + jnp.where(valid, folded(gated), 0.0)
        next_ref[at, :] = flat(fresh)
        x = jnp.where(valid, fresh, 0.0)
        return (sums[0] + jnp.sum(x, axis=0), sums[1] + jnp.sum(x * x, axis=0))

    zero = jnp.zeros(lim_ref.shape, F32)
    sums, squares = lax.fori_loop(0, u_ref.shape[0] // TILE, step, (zero, zero), unroll=True)
    a, b = per_micro(sums)
    c, d = per_micro(squares)
    pack_rows(st_ref, (a, c, b, d))


def gate_backward(layer, upstream, q, sig, slope, low, masked, s_low, state, c_ref, w_ref, mix_ref, sg_ref, gw_ref, gc_ref, i):
    at = rows_at(i)
    gate = (upstream * q).astype(BF16)
    gw_ref[...] += dot_tn(low, gate)
    act = upstream * sig + dot_nt(gate, w_ref[layer])
    mix = (act * slope).astype(BF16)
    mix_ref[at, :] = mix
    gc_ref[...] += dot_tn(s_low, mix)
    sg = dot_nt(mix, c_ref[layer])
    sg_ref[at, :] = sg
    wide_sum = jnp.sum(folded(sg * state), axis=0)
    half = wide_sum.shape[1] // 2
    return (
        jnp.sum(folded(gate.astype(F32)), axis=0),
        jnp.sum(folded(mix.astype(F32) * masked), axis=0),
        wide_sum[:, :half] + wide_sum[:, half:],
    )


def put_sums(sums_ref, sums):
    sums_ref[...] = jnp.zeros(sums_ref.shape, F32)
    pack_rows(sums_ref, [jnp.sum(part, axis=0, keepdims=True) for part in sums])


def zero_sums(width, states):
    return (jnp.zeros((SUB, width), F32), jnp.zeros((SUB, width), F32), jnp.zeros((SUB, states), F32))


def k_middle(layer, parts, *refs):
    carry, refs = take_carry(refs, parts)
    (d_ref, u_ref, stat_ref, lim_ref, vec_ref, par_ref, keep_ref, kp_ref, kd_ref,
     keep_adj_ref, kp_adj_ref, c_ref, w_ref, cot32_ref,
     lines_ref, s_ref, mix_ref, sg_ref, wc_ref, sums_ref, e_ref) = refs
    vec_ref, par_ref = of_layer(vec_ref, layer), of_layer(par_ref, layer)
    first = run_states(carry, d_ref, keep_ref, kp_ref, kd_ref, par_ref, s_ref, True)
    wc_ref[...] = jnp.zeros(wc_ref.shape, F32)
    gw_ref, gc_ref = wc_ref.at[: u_ref.shape[1]], wc_ref.at[u_ref.shape[1] :]

    def step(i, sums):
        at = rows_at(i)
        valid = tile_mask(lim_ref, i)
        masked = flat(masked_tile(u_ref, stat_ref, vec_ref, lim_ref, i))
        state = s_ref[pl.ds(pl.multiple_of(i * TILE + first, SUB), TILE), :]
        s_low = state.astype(BF16)
        mixed = dot(s_low, c_ref[layer]) + vec_ref[2:3, :] * masked
        active, slope = gelu_parts(mixed)
        low = active.astype(BF16)
        sig = sigmoid(dot(low, w_ref[layer]) + vec_ref[3:4, :])
        gated = active * sig
        put_lines(lines_ref, i, flat(folded(u_ref[at, :]) + jnp.where(valid, folded(gated), 0.0)))
        upstream = flat(jnp.where(valid, folded(cot32_ref[at, :]), 0.0))
        more = gate_backward(layer, upstream, gated * (1.0 - sig), sig, slope, low, masked, s_low, state,
                             c_ref, w_ref, mix_ref, sg_ref, gw_ref, gc_ref, i)
        return tuple(x + y for x, y in zip(sums, more))

    sums = lax.fori_loop(0, u_ref.shape[0] // TILE, step, zero_sums(u_ref.shape[1], par_ref.shape[1]), unroll=True)
    put_sums(sums_ref, sums)
    re, im, unused = scan(sg_ref, keep_adj_ref, par_ref, zeros_state(par_ref), False, True)
    put_ends(e_ref, chunk_end((re, im), kp_adj_ref, par_ref, False, True))


def k_lower(layer, st_ref, z_ref, cot32_ref, u1_ref, stat1_ref, lim_ref,
            s_ref, al_ref, sig_ref, q_ref, slope_ref, u_ref, stat_ref, vec_ref, par_ref, c_ref, w_ref,
            keep_adj_ref, kp_adj_ref,
            grad_ref, mix_ref, sg_ref, gw_ref, gc_ref, sums_ref, e_ref, bn_ref):
    vec1_ref = of_layer(vec_ref, layer + 1)
    vec_ref, par_ref = of_layer(vec_ref, layer), of_layer(par_ref, layer)
    first = SUB
    c1, c2 = norm_sums(st_ref, stat1_ref, vec1_ref, bn_ref)
    gw_ref[...] = jnp.zeros(gw_ref.shape, F32)
    gc_ref[...] = jnp.zeros(gc_ref.shape, F32)

    def step(i, sums):
        at = rows_at(i)
        valid = tile_mask(lim_ref, i)
        extra = norm_backward(z_ref, u1_ref, stat1_ref, vec1_ref, c1, c2, valid, i)
        grad = folded(cot32_ref[at, :]) + extra
        grad_ref[at, :] = flat(grad)
        upstream = flat(jnp.where(valid, grad, 0.0))
        masked = flat(masked_tile(u_ref, stat_ref, vec_ref, lim_ref, i))
        state = s_ref[pl.ds(pl.multiple_of(i * TILE + first, SUB), TILE), :]
        more = gate_backward(layer, upstream, q_ref[at, :], sig_ref[at, :], slope_ref[at, :], al_ref[at, :], masked,
                             state.astype(BF16), state, c_ref, w_ref, mix_ref, sg_ref, gw_ref, gc_ref, i)
        return tuple(x + y for x, y in zip(sums, more))

    sums = lax.fori_loop(0, u_ref.shape[0] // TILE, step, zero_sums(u_ref.shape[1], par_ref.shape[1]), unroll=True)
    put_sums(sums_ref, sums)
    re, im, unused = scan(sg_ref, keep_adj_ref, par_ref, zeros_state(par_ref), True, True)
    put_ends(e_ref, chunk_end((re, im), kp_adj_ref, par_ref, True, True))


def norm_sums(st_ref, stat_ref, vec_ref, bn_ref):
    width = vec_ref.shape[1]
    a, c, b, d = unpack_rows(st_ref[...], 4, width)
    bn_ref[...] = jnp.concatenate((a + b, c + d, jnp.zeros((6, width), F32)), axis=0)
    gain = vec_ref[0:1, :]
    inverse = stat_ref[16:24, :]
    return by_micro(a * gain, b * gain) * inverse, by_micro(c * gain, d * gain) * inverse


def norm_backward(z_ref, u_ref, stat_ref, vec_ref, c1, c2, valid, i):
    normed = normed_tile(u_ref, stat_ref, i)
    z = folded(z_ref[rows_at(i), :]) * vec_ref[0:1, :][None]
    return jnp.where(valid, stat_ref[8:16, :][None] * (z - c1[None] - normed * c2[None]), 0.0)


def k_adjoint(layer, reverse, parts, extra, *refs):
    carry, refs = take_carry(refs, parts)
    sent_refs, refs = refs[:extra], refs[extra:]
    (sg_ref, s_ref, mix_ref, ml_ref, u_ref, stat_ref, lim_ref, vec_ref, par_ref,
     keep_adj_ref, kp_adj_ref, kd_adj_ref, keep_ref, b_ref, z_ref, gb_ref, lg_ref, st_ref, a_ref) = refs
    vec_ref, par_ref = of_layer(vec_ref, layer), of_layer(par_ref, layer)
    width = par_ref.shape[1]
    tiles = width // LANE
    behind = 0 if reverse else SUB
    start = enter(*carry, kd_adj_ref, kp_adj_ref, par_ref, reverse, True)
    scale = [jnp.broadcast_to(par_ref[6:7, j * LANE : (j + 1) * LANE], (SUB, LANE)) for j in range(tiles)]

    def visit(t, unused, adjoint, sums):
        at = pl.ds(pl.multiple_of(t * SUB, SUB), SUB)
        before = pl.ds(pl.multiple_of(t * SUB + behind, SUB), SUB)
        keep = keep_ref[at, :]
        fresh = []
        for j, (re, im) in enumerate(adjoint):
            a_ref[at, j * LANE : (j + 1) * LANE] = re * scale[j]
            a_ref[at, width + j * LANE : width + (j + 1) * LANE] = im * scale[j]
            pr = s_ref[before, j * LANE : (j + 1) * LANE]
            pi = s_ref[before, width + j * LANE : width + (j + 1) * LANE]
            kr, ki = keep * re, keep * im
            fresh.append((sums[j][0] + (kr * pr + ki * pi), sums[j][1] + (ki * pr - kr * pi)))
        return tuple(fresh)

    zero = jnp.zeros((SUB, LANE), F32)
    unused, unused, sums = scan(sg_ref, keep_adj_ref, par_ref, start, reverse, True, visit,
                                tuple((zero, zero) for j in range(tiles)))
    lg_ref[...] = jnp.zeros(lg_ref.shape, F32)
    pack_rows(lg_ref, [
        jnp.sum(jnp.concatenate([part[k] for part in sums], axis=1), axis=0, keepdims=True) for k in range(2)
    ])
    gb_ref[...] = jnp.zeros(gb_ref.shape, F32)

    def step(i, sums):
        at = rows_at(i)
        drive = a_ref[at, :].astype(BF16)
        gb = dot_tn(ml_ref[at, :], drive)
        rows = gb.shape[0]
        gb_ref[:rows, :] += gb[:, :rows]
        gb_ref[rows:, : rows // 2] += gb[: rows // 2, rows:]
        gb_ref[rows:, rows // 2 :] += gb[rows // 2 :, rows:]
        back = dot_nt(drive, b_ref[layer]) + vec_ref[2:3, :] * mix_ref[at, :].astype(F32)
        z = jnp.where(tile_mask(lim_ref, i), folded(back), 0.0)
        z_ref[at, :] = flat(z)
        return (sums[0] + jnp.sum(z, axis=0), sums[1] + jnp.sum(z * normed_tile(u_ref, stat_ref, i), axis=0))

    zero = jnp.zeros(lim_ref.shape, F32)
    sums = lax.fori_loop(0, u_ref.shape[0] // TILE, step, (zero, zero), unroll=True)
    a, b = per_micro(sums[0])
    c, d = per_micro(sums[1])
    pack_rows(st_ref, (a, c, b, d))
    at = 16
    if extra:
        for ref in sent_refs + (lg_ref,):
            st_ref[at : at + ref.shape[0], :] = ref[...]
            at += ref.shape[0]


def k_output(st_ref, z_ref, grad_ref, u_ref, stat_ref, vec_ref, lim_ref, par_ref, stat1_ref, bn1_ref,
             run_mean_ref, run_var_ref,
             out_ref, gain_ref, shift_ref, skip_ref, bias_ref, rate_ref, rotation_ref, mean_ref, var_ref,
             bn_ref, lines_ref):
    vec0_ref = of_layer(vec_ref, 0)
    c1, c2 = norm_sums(st_ref, stat_ref, vec0_ref, bn_ref)

    def step(i, unused):
        extra = norm_backward(z_ref, u_ref, stat_ref, vec0_ref, c1, c2, tile_mask(lim_ref, i), i)
        put_lines(lines_ref, i, grad_ref[rows_at(i), :] + flat(extra))
        return unused

    lax.fori_loop(0, u_ref.shape[0] // TILE, step, 0, unroll=True)
    spread_out(lines_ref, out_ref)
    width, states = gain_ref.shape[1], rate_ref.shape[1]
    per, per_state = width // LANE, states // LANE

    def line(at, count):
        return jnp.concatenate([st_ref[at + j : at + j + 1, :] for j in range(count)], axis=1)

    for layer, (stats_ref, norms_ref) in enumerate(((stat_ref, bn_ref), (stat1_ref, bn1_ref))):
        row = slice(layer, layer + 1)
        at = 40 - 24 * layer
        bias_ref[row, :] = line(at, per)
        skip_ref[row, :] = line(at + per, per)
        product = line(at + 2 * per, per_state)
        grad_re, grad_im = line(at + 16, per_state), line(at + 16 + per_state, per_state)
        par = of_layer(par_ref, layer)
        lam_re, lam_im, norm_in, decay = par[0:1, :], par[1:2, :], par[6:7, :], par[7:8, :]
        rotation_ref[row, :] = lam_re * grad_im - lam_im * grad_re
        rate_ref[row, :] = decay * (
            product * jnp.exp(-2.0 * decay) / (norm_in * norm_in) - (lam_re * grad_re + lam_im * grad_im)
        )
        shift_ref[row, :] = norms_ref[0:1, :]
        gain_ref[row, :] = norms_ref[1:2, :]
        mean, var = run_mean_ref[row, :], run_var_ref[row, :]
        for micro in range(2):
            mean = (1.0 - momentum) * mean + momentum * stats_ref[24 + micro : 25 + micro, :]
            var = (1.0 - momentum) * var + momentum * stats_ref[26 + micro : 27 + micro, :]
        mean_ref[row, :] = mean
        var_ref[row, :] = var


def k_split(side, x_ref, give_ref):
    half = give_ref.shape[0]
    give_ref[...] = x_ref[pl.ds(pl.multiple_of((1 - side()) * half, SUB), half), :]


def k_fold(before, side, kept_ref, got_ref, give_ref, keep_ref):
    half = give_ref.shape[0]
    base = 0 if before is None else before() * got_ref.shape[0]
    mine = side()
    for ref, at in ((give_ref, (1 - mine) * half), (keep_ref, mine * half)):
        here = kept_ref[pl.ds(pl.multiple_of(base + at, SUB), half), :]
        ref[...] = here + got_ref[pl.ds(pl.multiple_of(at, SUB), half), :]


def k_copy(src_ref, dst_ref):
    dst_ref[...] = src_ref[...]


def k_add(*refs):
    total = refs[1][...]
    for ref in refs[2:-1]:
        total = total + ref[...]
    refs[-1][...] = refs[0][...] + total


def k_join(side, own_ref, got_ref, out_ref):
    half = own_ref.shape[0]
    mine = side()
    out_ref[pl.ds(pl.multiple_of(mine * half, SUB), half), :] = own_ref[...]
    out_ref[pl.ds(pl.multiple_of((1 - mine) * half, SUB), half), :] = got_ref[...]


def copy_all(pairs, sem_ref):
    copies = [pltpu.make_async_copy(src, dst, sem_ref.at[k]) for k, (src, dst) in enumerate(pairs)]
    for copy in copies:
        copy.start()
    for copy in copies:
        copy.wait()


def cut_to(layer, first, src_ref, outs):
    pairs = []
    for begin, end, place in outs:
        low, high = max(begin, first), min(end, first + src_ref.shape[0])
        if low < high:
            pairs.extend(place(src_ref, low - first, low - begin, high - low))
    return pairs


def rows_to(layer, ref):
    return lambda src, at, row, size: [(src.at[pl.ds(at, size), :], ref.at[layer, pl.ds(row, size), :])]


def map_places(layer, *refs):
    places, first = [], 0
    for ref in refs:
        places.append((first, first + ref.shape[1], rows_to(layer, ref)))
        first += ref.shape[1]
    return places


def drive_places(layer, b_ref):
    width = b_ref.shape[1]

    def left(src, at, row, size):
        return [(src.at[pl.ds(at, size), :], b_ref.at[layer, pl.ds(row, size), pl.ds(0, width)])]

    def right(src, at, row, size):
        part = width // 2
        return [
            (src.at[pl.ds(at, size), pl.ds(k * part, part)],
             b_ref.at[layer, pl.ds(k * part + row, size), pl.ds(width, part)])
            for k in range(2)
        ]

    return [(0, width, left), (width, width + width // 2, right)]


def k_place(side, places, layer, count, own_ref, got_ref, *refs):
    token_ref, sem_ref = refs[-2:]
    outs = refs[-2 - count : -2]
    token_ref[...] = jnp.zeros(token_ref.shape, F32)
    half = own_ref.shape[0]
    for mine in range(2):
        @pl.when(side() == mine)
        def _():
            where = places(layer, *outs)
            copy_all(
                cut_to(layer, mine * half, own_ref, where) + cut_to(layer, (1 - mine) * half, got_ref, where), sem_ref
            )


def place(large, places, layer, shapes, into=None):
    count = len(shapes)
    args = [large.block, large.got] + list(into or [])
    alias = {2 + k: k for k in range(count)} if into else {}
    return list(call(
        "place", functools.partial(k_place, large.side(), places, layer, count), shapes + [shaped((SUB, LANE))], args,
        scratch=[pltpu.SemaphoreType.DMA((8,))], order=large.order, token=count, far=range(2, len(args)), alias=alias,
        out_far=count,
    ))[:count]


BOTH = ("batch", "tm")

TAIL = ("DABSDECBSA", "DCBEADCSBD", "EASCBDECDB", "SCEDALBCAE", "CDBED")


def outer_bits():
    nb, nt = lax.axis_size("batch"), lax.axis_size("tm")
    return [("batch", 1 << k, nt << k) for k in range(nb.bit_length() - 1)]


def line_bits():
    return [("tm", 1 << k, 1 << k) for k in range(1, lax.axis_size("tm").bit_length() - 1)]


def swap(block, distance):
    total = lax.axis_size("batch") * lax.axis_size("tm")
    return lax.ppermute(block, BOTH, [(i, i ^ distance) for i in range(total)])


def swap_by_core(block, even, odd):
    total = lax.axis_size("batch") * lax.axis_size("tm")
    return lax.ppermute(block, BOTH, [(i, i ^ (odd if i & 1 else even)) for i in range(total)])


def sum_four(block, others, order=None):
    block, = call("add", k_add, [shaped(block.shape)], [block, others[0]], order=order, work=1)
    return call("add", k_add, [shaped(block.shape)], [block] + others[1:], order=order, work=1)[0]


def sum_over(block, bits):
    if len(bits) == 2:
        near, far = bits[0][2], bits[1][2]
        return sum_four(block, [swap(block, distance | 1) for distance in (near | far, far, near)])
    for unused, unused, distance in bits:
        block = block + swap(block, distance | 1)
    return block


def sums_of_all(block):
    block = block + swap(block, 1)
    return sum_over(sum_over(block, outer_bits()), line_bits())


def sums_in_order(block, order, between):
    for bits, start in zip(([("tm", 1, 0)], outer_bits(), line_bits()), between):
        if len(bits) == 2:
            near, far = bits[0][2], bits[1][2]
            got = [swap(block, distance | 1) for distance in (near | far, far, near)]
            start()
            block = sum_four(block, got, order)
        else:
            for k, bit in enumerate(bits):
                got = swap(block, bit[2] | 1)
                if k == 0:
                    start()
                block, = call("add", k_add, [shaped(block.shape)], [block, got], order=order)
    return block


def carries(e, kd, par, layer, reverse, conj, order=None):
    other = swap(e, 1)
    block, = call("combine", functools.partial(k_combine, layer, reverse, conj), [shaped(e.shape)], [e, other, kd, par],
                  order=order)
    bits = line_bits()
    if len(bits) == 2:
        near, far = bits[0][2], bits[1][2]
        last = swap(block, near | far | 1)
        others = [swap(block, distance | 1) for distance in (near, far)]
        last, = call("copy", k_copy, [shaped(block.shape)], [last], work=1)
        return [block] + others + [last, e, other]
    for unused, unused, distance in bits:
        block = jnp.concatenate((block, swap(block, distance | 1)), axis=0)
    return [block, e, other]


def bit_of(axis, bit):
    return lax.div(lax.axis_index(axis), bit) % 2


def plan(rows, line_first):
    outer, line = outer_bits(), line_bits()
    is_odd = functools.partial(bit_of, "tm", 1)
    steps = []
    for even, odd in zip(outer, outer[::-1]):
        def side(even=even, odd=odd):
            return jnp.where(is_odd() == 1, bit_of(odd[0], odd[1]), bit_of(even[0], even[1]))

        steps.append((side, functools.partial(swap_by_core, even=even[2], odd=odd[2])))
    along = [(functools.partial(bit_of, axis, bit), functools.partial(swap, distance=distance))
             for axis, bit, distance in line]
    steps = [(is_odd, lambda block: swap(block, 1))] + (along + steps if line_first else steps + along)
    most = 3 if line_first else 4
    cuts = 0
    while cuts < len(steps) and rows % (SUB << (cuts + 1)) == 0 and cuts < most:
        cuts += 1
    return steps[:cuts], [exchange for unused, exchange in steps[cuts:]]


class Large:
    def __init__(self, order, block, line_first=False):
        self.order = order
        self.rows, self.width = block.shape
        self.cuts, self.whole = plan(self.rows, line_first)
        self.block = block
        self.at = 0
        self.got = None

    def call(self, name, body, outs):
        args = [self.block] if self.got is None else [self.block, self.got]
        return call(name, body, outs, args, order=self.order)

    def send(self):
        cuts, at = self.cuts, self.at
        count = len(cuts)
        if at < count:
            side, exchange = cuts[at]
            half = shaped((self.rows >> (at + 1), self.width))
            if at == 0:
                give, = self.call("split", functools.partial(k_split, side), [half])
            else:
                before = cuts[0][0] if at == 1 else None
                give, self.block = self.call("fold", functools.partial(k_fold, before, side), [half, half])
        else:
            if at <= count + len(self.whole):
                give, = self.call("add", k_add, [shaped(self.got.shape)])
            else:
                give, = self.call("join", functools.partial(k_join, self.side()), [self.doubled()])
            self.block = give
            exchange = (self.whole + [step[1] for step in cuts[::-1]])[at - count]
        self.got = exchange(give)
        self.at += 1

    def side(self):
        return self.cuts[2 * len(self.cuts) + len(self.whole) - self.at][0]

    def doubled(self):
        return shaped((2 * self.block.shape[0], self.width))

    def left(self):
        return 2 * len(self.cuts) + len(self.whole) - self.at


def small_sum(order, block):
    for distance in [1] + [bit[2] | 1 for bit in outer_bits() + line_bits()]:
        got = swap(block, distance)
        yield None
        block, = call("add", k_add, [shaped(block.shape)], [block, got], order=order)
    yield block


def local(tokens, starts, lengths, cotangent, norm_gain, norm_shift, b_proj, log_rate, rotation, c_proj, skip_gain,
          w_gate, gate_bias, run_mean, run_var):
    rows, length, width = tokens.shape
    states = log_rate.shape[1]
    count = rows * length
    n = lax.axis_size("tm")
    chips = n // 2
    parts = 4 if chips == 4 else 1

    big = lambda w, dtype=F32: shaped((count, w), dtype)
    ends = shaped((SUB, 2 * states))
    kept = shaped((count + SUB, 2 * states))
    small = shaped((16, LANE))
    lines = pltpu.VMEM((width // LANE, count, LANE), F32)
    everyone = pltpu.VMEM((chips, SUB, 2 * states), F32)
    keeps = shaped((count, LANE))
    vector, state_vector = shaped((2, width)), shaped((2, states))

    u0, st, lim = call("enter", k_input, [big(width), shaped((24, LANE)), shaped((SUB, width), jnp.int32)],
                       [lengths, tokens], scratch=[lines], scalars=1)
    keep_shapes = [keeps, shaped((SUB, LANE)), shaped((n, SUB, LANE))]
    keep_f, kp_f, kd_f, par, vec = call(
        "prepare", k_prepare, keep_shapes + [shaped((2 * SUB, states)), shaped((2 * SUB, width))],
        [starts, log_rate, rotation, norm_gain, norm_shift, skip_gain, gate_bias], scalars=1,
    )
    st = sums_of_all(st)
    d0, ml0, stat0, e = call(
        "drive0", functools.partial(k_drive_first, 0, False),
        [big(2 * states), big(width, BF16), shaped((32, width)), ends],
        [st, u0, lim, vec, par, b_proj, keep_f, kp_f],
    )
    side = Order()
    side.token = e
    keep_r, kp_r, kd_r = call(
        "keep", functools.partial(k_keep, True), keep_shapes, [starts], scalars=1, order=side,
    )
    s0, al0, sig0, q0, slope0, u1, st = call(
        "finish0", functools.partial(k_finish_first, 0, parts),
        [kept, big(width, BF16), big(width), big(width), big(width), big(width), small],
        carries(e, kd_f, par, 0, False, False)
        + [d0, u0, stat0, lim, vec, par, keep_f, kp_f, kd_f, c_proj, w_gate],
        scratch=[everyone],
    )
    st = sums_of_all(st)
    d1, ml1, stat1, e = call(
        "drive1", functools.partial(k_drive, 1, True),
        [big(2 * states), big(width, BF16), shaped((32, width)), ends],
        [st, stat0, u1, lim, vec, par, b_proj, keep_r, kp_r],
    )
    grads = [shaped((width + 2 * states, width)), small, ends]
    side.token = u1
    cot32, = call("cotangent", spread_in, [big(width)], [cotangent], scratch=[lines], order=side)
    out32, s1, mix1, sg1, wc1, sums1, e = call(
        "middle", functools.partial(k_middle, 1, parts),
        [shaped((width // LANE, count, LANE)), kept, big(width, BF16), big(2 * states)] + grads,
        carries(e, kd_r, par, 1, True, False)
        + [d1, u1, stat1, lim, vec, par, keep_r, kp_r, kd_r, keep_f, kp_f, c_proj, w_gate, cot32],
        scratch=[everyone],
    )
    order = Order()
    order.token = e
    wc1 = Large(order, wc1)
    got = carries(e, kd_f, par, 1, False, True, order)
    wc1.send()
    wc1.send()
    adjoint = [big(width), shaped((2 * states, width)), shaped((8, LANE))]
    z1, gb1, lg1, st = call(
        "adjoint1", functools.partial(k_adjoint, 1, False, parts, 0), adjoint + [small],
        got + [sg1, s1, mix1, ml1, u1, stat1, lim, vec, par, keep_f, kp_f, kd_f, keep_r, b_proj],
        scratch=[pltpu.VMEM((count, 2 * states), F32), everyone], order=order, token=3,
    )
    b1 = Large(order, gb1)
    emitted = []

    def emit():
        emitted.extend(call("emit", spread_out, [shaped(tokens.shape, BF16)], [out32], results=1, order=order))

    st = sums_in_order(st, order, [b1.send, wc1.send, emit])
    b1.send()
    wc1.send()
    output, = emitted
    g0, mix0, sg0, gw0, gc0, sums0, e, bn1 = call(
        "lower", functools.partial(k_lower, 0),
        [big(width), big(width, BF16), big(2 * states), shaped((width, width)), shaped((2 * states, width)), small, ends,
         shaped((SUB, width))],
        [st, z1, cot32, u1, stat1, lim, s0, al0, sig0, q0, slope0, u0, stat0, vec, par,
         c_proj, w_gate, keep_r, kp_r],
        order=order, token=6,
    )
    w0, c0 = Large(order, gw0, True), Large(order, gc0)
    got = carries(e, kd_r, par, 0, True, True, order)
    c0.send()
    w0.send()
    c0.send()
    w0.send()
    z0, gb0, lg0, st = call(
        "adjoint0", functools.partial(k_adjoint, 0, True, parts, 3), adjoint + [shaped((64, LANE))],
        got + [sums1, lg1, sums0]
        + [sg0, s0, mix0, ml0, u0, stat0, lim, vec, par, keep_r, kp_r, kd_r, keep_f, b_proj],
        scratch=[pltpu.VMEM((count, 2 * states), F32), everyone], order=order, token=3,
    )
    b0 = Large(order, gb0)
    steps = small_sum(order, st)
    w_shape, c_shape = shaped((2, width, width)), shaped((2, 2 * states, width))
    drive_shapes = [shaped((2, width, 2 * states))]
    larges = {"A": wc1, "B": b1, "C": c0, "E": w0, "D": b0}
    into = {}

    def step(item):
        if item == "S":
            return next(steps, None)
        large = larges[item]
        if large.left():
            large.send()
        elif item == "A":
            into["E"], into["C"] = ([made] for made in place(large, map_places, 1, [w_shape, c_shape]))
        elif item == "B":
            into["D"] = place(large, drive_places, 1, drive_shapes)
        elif item in "CDE" and item not in into:
            step("B" if item == "D" else "A")
            step(item)
        elif item in "CE":
            if len(into[item]) == 1:
                into[item] = place(large, map_places, 0, [c_shape if item == "C" else w_shape], into[item]) + [None]
        elif len(into["D"]) == 1:
            into["D"] = place(large, drive_places, 0, drive_shapes, into["D"]) + [None]
        return None

    for item in "".join(TAIL):
        if item != "L":
            sent = step(item)
            st = st if sent is None else sent
            continue
        for sent in steps:
            st = st if sent is None else sent
        (tokens_grad, grad_gain, grad_shift, grad_skip, grad_bias, grad_rate, grad_rotation, new_mean, new_var,
         unused) = call(
            "leave", k_output,
            [shaped(tokens.shape), vector, vector, vector, vector, state_vector, state_vector, vector, vector,
             shaped((SUB, width))],
            [st, z0, g0, u0, stat0, vec, lim, par, stat1, bn1, run_mean, run_var],
            scratch=[lines], results=9, order=order, token=9,
        )
    for item in "CED":
        while len(into.get(item, ())) < 2:
            step(item)
    (grad_w, unused), (grad_c, unused), (grad_b, unused) = into["E"], into["C"], into["D"]
    return (output, tokens_grad, grad_gain, grad_shift, grad_b, grad_rate, grad_rotation, grad_c, grad_skip, grad_w,
            grad_bias, new_mean, new_var)


def solution(mesh):
    tokens_spec = P("batch", "tm", None)
    return jax.shard_map(
        local,
        mesh=mesh,
        in_specs=(tokens_spec, P("batch", None), P("batch"), tokens_spec) + (P(),) * 11,
        out_specs=(tokens_spec, tokens_spec) + (P(),) * 11,
        check_vma=False,
    )
```

```python
import functools
import math

import jax
import jax.numpy as jnp
from jax import lax
from jax.experimental import pallas as pl
from jax.experimental.pallas import tpu as pltpu
from jax.sharding import PartitionSpec as P

epsilon = 1e-05
momentum = 0.1
F32 = jnp.float32
BF16 = jnp.bfloat16

SUB = 8
LANE = 128
TILE = 256
WORK = 5 * 10**9


def in_vmem(count):
    return [pl.BlockSpec(memory_space=pltpu.VMEM)] * count


class Order:
    def __init__(self):
        self.token = None


def call(name, body, outs, args, scratch=(), scalars=0, results=0, order=None, token=0, far=(), alias=None, out_far=0, work=WORK):
    room = 6 * 1024 * 1024 + sum(4 * math.prod(item.shape) for item in list(scratch) + list(outs[:results]) if hasattr(item, "shape"))
    specs = [pl.BlockSpec(memory_space=pltpu.SMEM)] * scalars + in_vmem(len(args) - scalars)
    for k in far:
        specs[k] = pl.BlockSpec(memory_space=pltpu.HBM)
    count = len(args)
    args = list(args)
    run = body
    if order is not None and order.token is not None:
        args.append(order.token)
        specs.append(pl.BlockSpec(memory_space=pl.ANY))
        run = lambda *refs: body(*refs[:count], *refs[count + 1 :])
    out_specs = in_vmem(len(outs))
    for k in range(out_far):
        out_specs[k] = pl.BlockSpec(memory_space=pltpu.HBM)
    done = pl.pallas_call(
        run,
        name=name,
        out_shape=outs,
        in_specs=specs,
        out_specs=out_specs,
        scratch_shapes=list(scratch),
        input_output_aliases=alias or {},
        compiler_params=pltpu.CompilerParams(vmem_limit_bytes=room),
        cost_estimate=pl.CostEstimate(flops=work, bytes_accessed=1, transcendentals=0),
    )(*args)
    if order is not None:
        order.token = done[token]
    return done


def shaped(shape, dtype=F32):
    return jax.ShapeDtypeStruct(shape, dtype)


def tile_mask(lim_ref, i):
    steps = TILE // SUB
    t = lax.broadcasted_iota(jnp.int32, (steps,) + lim_ref.shape, 0) + i * steps
    return t < lim_ref[...][None]


def folded(values):
    return values.reshape((values.shape[0] // SUB, SUB, values.shape[1]))


def flat(values):
    return values.reshape((values.shape[0] * SUB, values.shape[2]))


def times(ar, ai, br, bi):
    return (ar * br - ai * bi, ar * bi + ai * br)


class Scan:
    def __init__(self, d_ref, keep_ref, par_ref, start, reverse, conj, visit=None, extra=()):
        self.d_ref, self.keep_ref, self.reverse = d_ref, keep_ref, reverse
        self.width = par_ref.shape[1]
        self.visit, self.extra = visit, extra
        self.lanes = [slice(j * LANE, (j + 1) * LANE) for j in range(self.width // LANE)]
        self.lam = []
        for lanes in self.lanes:
            re = jnp.broadcast_to(par_ref[0:1, lanes], (SUB, LANE))
            im = jnp.broadcast_to(par_ref[1:2, lanes], (SUB, LANE))
            self.lam.append((re, -im if conj else im))
        self.state = [(start[0][:, lanes], start[1][:, lanes]) for lanes in self.lanes]

    def tiles(self):
        count = self.d_ref.shape[0] // TILE
        return range(count - 1, -1, -1) if self.reverse else range(count)

    def ahead(self):
        order = list(self.tiles())
        self.run(order[0])
        for k, i in enumerate(order):
            if k + 1 < len(order):
                self.run(order[k + 1])
            yield i

    def run(self, i):
        steps = TILE // SUB
        for k in range(steps):
            t = i * steps + (steps - 1 - k if self.reverse else k)
            at = pl.ds(t * SUB, SUB)
            keep = self.keep_ref[at, :]
            fresh = []
            for (re, im), (lam_re, lam_im), lanes in zip(self.state, self.lam, self.lanes):
                a, b = keep * lam_re, keep * lam_im
                dr = self.d_ref[at, lanes]
                di = self.d_ref[at, lanes.start + self.width : lanes.stop + self.width]
                fresh.append((a * re - b * im + dr, a * im + b * re + di))
            self.state = fresh
            if self.visit is not None:
                self.extra = self.visit(t, fresh, self.extra)

    def ends(self):
        return tuple(jnp.concatenate([part[k] for part in self.state], axis=1) for k in range(2))


def wide(values, width):
    return jnp.concatenate([values] * (width // LANE), axis=1)


def chunk_end(ends, kp_ref, par_ref, reverse, conj):
    width = par_ref.shape[1]
    re, im = ends
    shift = SUB - 1 if reverse else 1
    pr, pi = pltpu.roll(re, shift, 0), pltpu.roll(im, shift, 0)
    keep = wide(kp_ref[:SUB, :], width)
    lr = keep * par_ref[2:3, :]
    li = keep * par_ref[3:4, :]
    li = -li if conj else li
    qr, qi = times(lr, li, pr, pi)
    odd = lax.broadcasted_iota(jnp.int32, (SUB, width), 0) % 2
    last = odd == (0 if reverse else 1)
    return jnp.where(last, qr + re, re), jnp.where(last, qi + im, im)


def chip_and_core():
    me = lax.axis_index("tm")
    return me // 2, me % 2


def enter(got_refs, e_ref, other_ref, all_ref, kd_ref, kp_ref, par_ref, reverse, conj):
    width = par_ref.shape[1]
    chips = all_ref.shape[0]
    chip, core = chip_and_core()
    sign = -1.0 if conj else 1.0
    at = 0
    for ref in got_refs:
        for k in range(ref.shape[0] // SUB):
            all_ref[at] = ref[k * SUB : (k + 1) * SUB, :]
            at += 1
    lr, li = par_ref[4:5, :], sign * par_ref[5:6, :]
    cr, ci = times(lr, li, lr, li)
    lr, li, cr, ci = (jnp.broadcast_to(x, (SUB, width)) for x in (lr, li, cr, ci))

    def step(i, x):
        j = chips - 1 - i if reverse else i
        keep = wide(kd_ref[2 * j] * kd_ref[2 * j + 1], width)
        qr, qi = times(keep * cr, keep * ci, x[0], x[1])
        use = (j > chip) if reverse else (j < chip)
        use = jnp.where(use, 1.0, 0.0)
        k = jnp.bitwise_xor(j, chip)
        nr = qr + all_ref[k, :, :width]
        ni = qi + all_ref[k, :, width:]
        return (x[0] + use * (nr - x[0]), x[1] + use * (ni - x[1]))

    zero = jnp.zeros((SUB, width), F32)
    xr, xi = lax.fori_loop(0, chips, step, (zero, zero), unroll=chips <= 4)
    first = 1 if reverse else 0
    keep = wide(kd_ref[2 * chip + first], width)
    qr, qi = times(keep * lr, keep * li, xr, xi)
    use = jnp.where(core == first, 0.0, 1.0)
    xr = xr + use * (qr + other_ref[:, :width] - xr)
    xi = xi + use * (qi + other_ref[:, width:] - xi)
    near, far = (1, SUB - 1) if reverse else (SUB - 1, 1)
    sr, si = pltpu.roll(xr, near, 0), pltpu.roll(xi, near, 0)
    keep = wide(kp_ref[:SUB, :], width)
    hr = keep * par_ref[2:3, :]
    hi = sign * keep * par_ref[3:4, :]
    tr, ti = times(hr, hi, sr, si)
    tr = pltpu.roll(tr + e_ref[:, :width], far, 0)
    ti = pltpu.roll(ti + e_ref[:, width:], far, 0)
    odd = lax.broadcasted_iota(jnp.int32, (SUB, width), 0) % 2
    second = odd == (0 if reverse else 1)
    return jnp.where(second, tr, sr), jnp.where(second, ti, si)


def put_ends(e_ref, ends):
    e_ref[...] = jnp.concatenate(ends, axis=1)


def zeros_state(par_ref):
    zero = jnp.zeros((SUB, par_ref.shape[1]), F32)
    return (zero, zero)


def per_micro(values):
    return (
        jnp.sum(values[0:4], axis=0, keepdims=True),
        jnp.sum(values[4:8], axis=0, keepdims=True),
    )


def pack_rows(out_ref, rows):
    at = 0
    for row in rows:
        for j in range(row.shape[1] // LANE):
            out_ref[at : at + 1, :] = row[:, j * LANE : (j + 1) * LANE]
            at += 1


def unpack_rows(values, count, width):
    tiles = width // LANE
    return [
        jnp.concatenate(
            [values[r * tiles + j : r * tiles + j + 1, :] for j in range(tiles)], axis=1
        )
        for r in range(count)
    ]


def by_micro(first, second):
    sub = lax.broadcasted_iota(jnp.int32, (SUB, first.shape[1]), 0)
    return jnp.where(sub < 4, jnp.broadcast_to(first, sub.shape), jnp.broadcast_to(second, sub.shape))


def dot(a, b):
    return jnp.dot(a, b, preferred_element_type=F32)


def dot_nt(a, b):
    return lax.dot_general(a, b, (((1,), (1,)), ((), ())), preferred_element_type=F32)


def dot_tn(a, b):
    return lax.dot_general(a, b, (((0,), (0,)), ((), ())), preferred_element_type=F32)


def normed_tile(u_ref, stat_ref, i):
    x = folded(u_ref[pl.ds(pl.multiple_of(i * TILE, TILE), TILE), :])
    return (x - stat_ref[0:8, :][None]) * stat_ref[8:16, :][None]


def masked_tile(u_ref, stat_ref, vec_ref, lim_ref, i):
    normed = normed_tile(u_ref, stat_ref, i)
    z = normed * vec_ref[0:1, :][None] + vec_ref[1:2, :][None]
    return jnp.where(tile_mask(lim_ref, i), z, 0.0)


def rows_at(i):
    return pl.ds(pl.multiple_of(i * TILE, TILE), TILE)


def spread_in(src_ref, dst_ref, lines_ref):
    half = src_ref.shape[1] // 2
    tiles = src_ref.shape[2] // LANE
    for s in range(SUB):
        part = src_ref[s // 2, (s % 2) * half : (s % 2 + 1) * half, :].astype(F32)
        for j in range(tiles):
            lines_ref[j, pl.ds(s, half, stride=SUB), :] = part[:, j * LANE : (j + 1) * LANE]
    for j in range(tiles):
        dst_ref[:, j * LANE : (j + 1) * LANE] = lines_ref[j]


def spread_out(lines_ref, dst_ref):
    half = dst_ref.shape[1] // 2
    tiles = dst_ref.shape[2] // LANE
    for s in range(SUB):
        for j in range(tiles):
            part = lines_ref[j, pl.ds(s, half, stride=SUB), :]
            dst_ref[s // 2, (s % 2) * half : (s % 2 + 1) * half, j * LANE : (j + 1) * LANE] = part.astype(dst_ref.dtype)


def k_emit(lines_ref, out_ref, token_ref):
    token_ref[...] = jnp.zeros(token_ref.shape, F32)
    spread_out(lines_ref, out_ref)


def put_lines(lines_ref, i, values):
    for j in range(lines_ref.shape[0]):
        lines_ref[j, rows_at(i), :] = values[:, j * LANE : (j + 1) * LANE]


def moment_sums(u_ref, lim_ref, upto):
    def step(i, sums):
        x = jnp.where(tile_mask(lim_ref, i), folded(u_ref[rows_at(i), :]), 0.0)
        return (sums[0] + jnp.sum(x, axis=0), sums[1] + jnp.sum(x * x, axis=0))

    zero = jnp.zeros(lim_ref.shape, F32)
    return lax.fori_loop(0, upto, step, (zero, zero))


def fill_lim(lengths_ref, lim_ref, half):
    sub = lax.broadcasted_iota(jnp.int32, lim_ref.shape, 0)
    length = jnp.zeros(lim_ref.shape, jnp.int32)
    for r in range(lengths_ref.shape[0]):
        length = jnp.where(sub // 2 == r, lengths_ref[r], length)
    lim_ref[...] = length - lax.axis_index("tm") * (2 * half) - (sub % 2) * half


def k_input(lengths_ref, tokens_ref, u_ref, st_ref, lim_ref, lines_ref):
    half = tokens_ref.shape[1] // 2
    fill_lim(lengths_ref, lim_ref, half)
    spread_in(tokens_ref, u_ref, lines_ref)
    sums, squares = moment_sums(u_ref, lim_ref, u_ref.shape[0] // TILE)
    a, b = per_micro(sums)
    c, d = per_micro(squares)
    st_ref[...] = jnp.zeros(st_ref.shape, F32)
    pack_rows(st_ref, (a, c, b, d))
    counts = jnp.clip(lim_ref[:, :LANE], 0, half).astype(F32)
    a, b = per_micro(counts)
    st_ref[16:17, :] = a
    st_ref[17:18, :] = b


def one_minus_exp(x):
    series = jnp.full(x.shape, 1.0 / 9.0, F32)
    for k in range(8, 0, -1):
        series = (1.0 - x * series) / k if k > 1 else 1.0 - x * series
    return jnp.where(x < 0.5, x * series, 1.0 - jnp.exp(-x))


def k_keep(reverse, starts_ref, keep_ref, kp_ref, kd_ref):
    count = keep_ref.shape[0] - SUB
    steps = count // SUB
    length = 2 * steps
    n = kd_ref.shape[0] - 1
    base = lax.axis_index("tm") * length
    for ref in (keep_ref, kp_ref, kd_ref):
        ref[...] = jnp.ones(ref.shape, F32)
    none = jnp.zeros((1, LANE), F32)

    def mark(r, place):
        local = place - base
        here = (local >= 0) & (local < length)
        second = jnp.where(local >= steps, 1, 0)
        row = (local - second * steps) * SUB + 2 * r + second
        keep_ref[pl.ds(jnp.where(here, row, count), 1), :] = none
        kp_ref[pl.ds(jnp.where(here, 2 * r + second, SUB), 1), :] = none

    def each(k, unused):
        for r in range(starts_ref.shape[0]):
            place = starts_ref[r, k] - (1 if reverse else 0)
            mark(r, place)
            device = jnp.where(place >= 0, lax.div(place, length), n)
            kd_ref[device, 2 * r : 2 * r + 2, :] = jnp.zeros((2, LANE), F32)
        return unused

    lax.fori_loop(0, starts_ref.shape[1], each, 0)
    if reverse:
        for r in range(starts_ref.shape[0]):
            mark(r, n * length - 1)


def k_prepare(starts_ref, rate_ref, rotation_ref, gain_ref, shift_ref, skip_ref, bias_ref,
              keep_ref, kp_ref, kd_ref, par_ref, vec_ref):
    k_keep(False, starts_ref, keep_ref, kp_ref, kd_ref)
    doublings = ((keep_ref.shape[0] - SUB) // SUB).bit_length() - 1
    for layer in range(2):
        decay = jnp.exp(rate_ref[layer : layer + 1, :])
        magnitude = jnp.exp(-decay)
        angle = rotation_ref[layer : layer + 1, :]
        re, im = magnitude * jnp.cos(angle), magnitude * jnp.sin(angle)
        at = layer * SUB
        norm_in = jnp.sqrt(one_minus_exp(2.0 * decay))
        par_ref[at : at + 1, :] = re
        par_ref[at + 1 : at + 2, :] = im
        for unused in range(doublings):
            re, im = times(re, im, re, im)
        par_ref[at + 2 : at + 3, :] = re
        par_ref[at + 3 : at + 4, :] = im
        re, im = times(re, im, re, im)
        par_ref[at + 4 : at + 5, :] = re
        par_ref[at + 5 : at + 6, :] = im
        par_ref[at + 6 : at + 7, :] = norm_in
        par_ref[at + 7 : at + 8, :] = decay
        vec_ref[at : at + SUB, :] = jnp.zeros((SUB, vec_ref.shape[1]), F32)
        for k, ref in enumerate((gain_ref, shift_ref, skip_ref, bias_ref)):
            vec_ref[at + k : at + k + 1, :] = ref[layer : layer + 1, :]


def of_layer(ref, layer):
    return ref.at[layer * SUB : (layer + 1) * SUB]


def k_combine(layer, reverse, conj, e_ref, other_ref, kd_ref, par_ref, out_ref):
    par_ref = of_layer(par_ref, layer)
    width = par_ref.shape[1]
    chip, core = chip_and_core()
    keep = wide(kd_ref[2 * chip + (0 if reverse else 1)], width)
    lr = keep * par_ref[4:5, :]
    li = keep * par_ref[5:6, :] * (-1.0 if conj else 1.0)
    is_first = core == (1 if reverse else 0)
    e, other = e_ref[...], other_ref[...]
    pick = jnp.where(is_first, 1.0, 0.0)
    first = other + pick * (e - other)
    last = e + pick * (other - e)
    qr, qi = times(lr, li, first[:, :width], first[:, width:])
    out_ref[...] = jnp.concatenate((qr, qi), axis=1) + last


def k_drive(layer, reverse, st_ref, cnt_ref, u_ref, lim_ref, vec_ref, par_ref, b_ref, keep_ref, kp_ref,
            d_ref, ml_ref, m_ref, stat_ref, e_ref):
    vec_ref, par_ref = of_layer(vec_ref, layer), of_layer(par_ref, layer)
    total = st_ref[...]
    a, c, b, d = unpack_rows(total, 4, u_ref.shape[1])
    if cnt_ref is None:
        counts = (total[16:17, :], total[17:18, :])
    else:
        counts = (cnt_ref[28:29, :LANE], cnt_ref[29:30, :LANE])
    parts = []
    for summed, squares, count in ((a, c, counts[0]), (b, d, counts[1])):
        inverse = 1.0 / wide(count, u_ref.shape[1])
        center = summed * inverse
        spread = squares * inverse - center * center
        parts.append((center, spread, lax.rsqrt(spread + epsilon), inverse))
    stat_ref[0:8, :] = by_micro(parts[0][0], parts[1][0])
    stat_ref[8:16, :] = by_micro(parts[0][2], parts[1][2])
    stat_ref[16:24, :] = by_micro(parts[0][3], parts[1][3])
    stat_ref[24:25, :] = parts[0][0]
    stat_ref[25:26, :] = parts[1][0]
    stat_ref[26:27, :] = parts[0][1]
    stat_ref[27:28, :] = parts[1][1]
    stat_ref[28:29, :] = wide(counts[0], u_ref.shape[1])
    stat_ref[29:30, :] = wide(counts[1], u_ref.shape[1])
    stat_ref[30:32, :] = jnp.zeros((2, u_ref.shape[1]), F32)
    both = jnp.concatenate((par_ref[6:7, :], par_ref[6:7, :]), axis=1)

    def step(i, unused):
        masked = flat(masked_tile(u_ref, stat_ref, vec_ref, lim_ref, i))
        m_ref[rows_at(i), :] = masked
        low = masked.astype(BF16)
        ml_ref[rows_at(i), :] = low
        d_ref[rows_at(i), :] = dot(low, b_ref[layer]) * both
        return unused

    scan = Scan(d_ref, keep_ref, par_ref, zeros_state(par_ref), reverse, False)
    for i in scan.tiles():
        step(i, 0)
        scan.run(i)
    put_ends(e_ref, chunk_end(scan.ends(), kp_ref, par_ref, reverse, False))


def k_drive_first(layer, reverse, st_ref, *refs):
    k_drive(layer, reverse, st_ref, None, *refs)


def run_states(carry, d_ref, keep_ref, kp_ref, kd_ref, par_ref, s_ref, reverse):
    width = par_ref.shape[1]
    first = 0 if reverse else SUB
    start = enter(*carry, kd_ref, kp_ref, par_ref, reverse, False)
    s_ref[(s_ref.shape[0] - SUB if reverse else 0) : (s_ref.shape[0] if reverse else SUB), :] = (
        jnp.concatenate(start, axis=1)
    )

    def visit(t, states, extra):
        at = pl.ds(t * SUB + first, SUB)
        for j, (re, im) in enumerate(states):
            s_ref[at, j * LANE : (j + 1) * LANE] = re
            s_ref[at, width + j * LANE : width + (j + 1) * LANE] = im
        return extra

    return first, Scan(d_ref, keep_ref, par_ref, start, reverse, False, visit)


def sigmoid(x):
    return 0.5 + 0.5 * jnp.tanh(0.5 * x)


def gelu_parts(x):
    cdf = 0.5 * (1.0 + lax.erf(x * 0.7071067811865476))
    return x * cdf, cdf + x * jnp.exp(-0.5 * x * x) * 0.3989422804014327


def states_low(s_ref, first, i):
    return s_ref[pl.ds(pl.multiple_of(i * TILE + first, SUB), TILE), :].astype(BF16)


def take_carry(refs, parts):
    return (refs[:parts], refs[parts], refs[parts + 1], refs[-1]), refs[parts + 2 : -1]


def k_finish_first(layer, parts, *refs):
    carry, refs = take_carry(refs, parts)
    (d_ref, u_ref, m_ref, lim_ref, vec_ref, par_ref, keep_ref, kp_ref, kd_ref, c_ref, w_ref,
     s_ref, al_ref, sig_ref, q_ref, slope_ref, next_ref, st_ref) = refs
    vec_ref, par_ref = of_layer(vec_ref, layer), of_layer(par_ref, layer)
    first, scan = run_states(carry, d_ref, keep_ref, kp_ref, kd_ref, par_ref, s_ref, False)

    def step(i, sums):
        at = rows_at(i)
        valid = tile_mask(lim_ref, i)
        mixed = dot(states_low(s_ref, first, i), c_ref[layer]) + vec_ref[2:3, :] * m_ref[at, :]
        active, slope = gelu_parts(mixed)
        low = active.astype(BF16)
        sig = sigmoid(dot(low, w_ref[layer]) + vec_ref[3:4, :])
        gated = active * sig
        al_ref[at, :] = low
        sig_ref[at, :] = sig
        slope_ref[at, :] = slope
        q_ref[at, :] = gated * (1.0 - sig)
        fresh = folded(u_ref[at, :]) + jnp.where(valid, folded(gated), 0.0)
        next_ref[at, :] = flat(fresh)
        x = jnp.where(valid, fresh, 0.0)
        return (sums[0] + jnp.sum(x, axis=0), sums[1] + jnp.sum(x * x, axis=0))

    zero = jnp.zeros(lim_ref.shape, F32)
    totals = (zero, zero)
    for i in scan.ahead():
        totals = step(i, totals)
    sums, squares = totals
    a, b = per_micro(sums)
    c, d = per_micro(squares)
    pack_rows(st_ref, (a, c, b, d))


def gate_backward(layer, upstream, q, sig, slope, masked, state, c_ref, w_ref, gate_ref, mix_ref, sg_ref, i):
    at = rows_at(i)
    gate = (upstream * q).astype(BF16)
    gate_ref[at, :] = gate
    act = upstream * sig + dot_nt(gate, w_ref[layer])
    mix = (act * slope).astype(BF16)
    mix_ref[at, :] = mix
    sg = dot_nt(mix, c_ref[layer])
    sg_ref[at, :] = sg
    wide_sum = jnp.sum(folded(sg * state), axis=0)
    half = wide_sum.shape[1] // 2
    return (
        jnp.sum(folded(gate.astype(F32)), axis=0),
        jnp.sum(folded(mix.astype(F32) * masked), axis=0),
        wide_sum[:, :half] + wide_sum[:, half:],
    )


def put_sums(sums_ref, sums):
    sums_ref[...] = jnp.zeros(sums_ref.shape, F32)
    pack_rows(sums_ref, [jnp.sum(part, axis=0, keepdims=True) for part in sums])


def zero_sums(width, states):
    return (jnp.zeros((SUB, width), F32), jnp.zeros((SUB, width), F32), jnp.zeros((SUB, states), F32))


class Ends:
    def __init__(self, keep_ref, par_ref):
        self.keep_ref = keep_ref
        re, im = par_ref[0:1, :], -par_ref[1:2, :]
        for unused in range((TILE // SUB).bit_length() - 1):
            re, im = times(re, im, re, im)
        self.step = tuple(jnp.broadcast_to(part, (SUB, part.shape[1])) for part in (re, im))
        self.factor = self.total = None

    def put_before(self, i, ends):
        if self.total is None:
            self.total = ends
        else:
            re, im = times(*self.factor, *ends)
            self.total = (self.total[0] + re, self.total[1] + im)
        keep = wide(jnp.min(folded(self.keep_ref[i * TILE : (i + 1) * TILE, :]), axis=0), ends[0].shape[1])
        here = tuple(keep * part for part in self.step)
        self.factor = here if self.factor is None else times(*self.factor, *here)


def k_middle(layer, parts, *refs):
    carry, refs = take_carry(refs, parts)
    (d_ref, u_ref, m_ref, lim_ref, vec_ref, par_ref, keep_ref, kp_ref, kd_ref,
     keep_adj_ref, kp_adj_ref, c_ref, w_ref, cot32_ref,
     lines_ref, s_ref, mix_ref, sg_ref, wc_ref, sums_ref, e_ref, al_ref, gate_ref, slow_ref) = refs
    vec_ref, par_ref = of_layer(vec_ref, layer), of_layer(par_ref, layer)
    first, scan = run_states(carry, d_ref, keep_ref, kp_ref, kd_ref, par_ref, s_ref, True)

    def step(i, sums):
        at = rows_at(i)
        valid = tile_mask(lim_ref, i)
        masked = m_ref[at, :]
        state = s_ref[pl.ds(pl.multiple_of(i * TILE + first, SUB), TILE), :]
        s_low = state.astype(BF16)
        mixed = dot(s_low, c_ref[layer]) + vec_ref[2:3, :] * masked
        active, slope = gelu_parts(mixed)
        low = active.astype(BF16)
        sig = sigmoid(dot(low, w_ref[layer]) + vec_ref[3:4, :])
        gated = active * sig
        put_lines(lines_ref, i, flat(folded(u_ref[at, :]) + jnp.where(valid, folded(gated), 0.0)))
        upstream = flat(jnp.where(valid, folded(cot32_ref[at, :]), 0.0))
        al_ref[at, :] = low
        slow_ref[at, :] = s_low
        more = gate_backward(layer, upstream, gated * (1.0 - sig), sig, slope, masked, state,
                             c_ref, w_ref, gate_ref, mix_ref, sg_ref, i)
        return tuple(x + y for x, y in zip(sums, more))

    sums = zero_sums(u_ref.shape[1], par_ref.shape[1])
    ends = Ends(keep_adj_ref, par_ref)
    for i in scan.ahead():
        sums = step(i, sums)
        local = Scan(sg_ref, keep_adj_ref, par_ref, zeros_state(par_ref), False, True)
        local.run(i)
        ends.put_before(i, local.ends())
    wc_ref[: u_ref.shape[1], :] = dot_tn(al_ref[...], gate_ref[...])
    wc_ref[u_ref.shape[1] :, :] = dot_tn(slow_ref[...], mix_ref[...])
    put_sums(sums_ref, sums)
    put_ends(e_ref, chunk_end(ends.total, kp_adj_ref, par_ref, False, True))


def k_lower(layer, st_ref, z_ref, cot32_ref, u1_ref, stat1_ref, lim_ref,
            s_ref, al_ref, sig_ref, q_ref, slope_ref, m_ref, vec_ref, par_ref, c_ref, w_ref,
            keep_adj_ref, kp_adj_ref,
            grad_ref, mix_ref, sg_ref, gw_ref, gc_ref, sums_ref, e_ref, bn_ref, gate_ref, slow_ref):
    vec1_ref = of_layer(vec_ref, layer + 1)
    vec_ref, par_ref = of_layer(vec_ref, layer), of_layer(par_ref, layer)
    first = SUB
    c1, c2 = norm_sums(st_ref, stat1_ref, vec1_ref, bn_ref)

    def step(i, sums):
        at = rows_at(i)
        valid = tile_mask(lim_ref, i)
        extra = norm_backward(z_ref, u1_ref, stat1_ref, vec1_ref, c1, c2, valid, i)
        grad = folded(cot32_ref[at, :]) + extra
        grad_ref[at, :] = flat(grad)
        upstream = flat(jnp.where(valid, grad, 0.0))
        masked = m_ref[at, :]
        state = s_ref[pl.ds(pl.multiple_of(i * TILE + first, SUB), TILE), :]
        slow_ref[at, :] = state.astype(BF16)
        more = gate_backward(layer, upstream, q_ref[at, :], sig_ref[at, :], slope_ref[at, :], masked,
                             state, c_ref, w_ref, gate_ref, mix_ref, sg_ref, i)
        return tuple(x + y for x, y in zip(sums, more))

    sums = zero_sums(m_ref.shape[1], par_ref.shape[1])
    scan = Scan(sg_ref, keep_adj_ref, par_ref, zeros_state(par_ref), True, True)
    for i in scan.tiles():
        sums = step(i, sums)
        scan.run(i)
    gw_ref[...] = dot_tn(al_ref[...], gate_ref[...])
    gc_ref[...] = dot_tn(slow_ref[...], mix_ref[...])
    put_sums(sums_ref, sums)
    put_ends(e_ref, chunk_end(scan.ends(), kp_adj_ref, par_ref, True, True))


def norm_sums(st_ref, stat_ref, vec_ref, bn_ref):
    width = vec_ref.shape[1]
    a, c, b, d = unpack_rows(st_ref[...], 4, width)
    bn_ref[...] = jnp.concatenate((a + b, c + d, jnp.zeros((6, width), F32)), axis=0)
    gain = vec_ref[0:1, :]
    inverse = stat_ref[16:24, :]
    return by_micro(a * gain, b * gain) * inverse, by_micro(c * gain, d * gain) * inverse


def norm_backward(z_ref, u_ref, stat_ref, vec_ref, c1, c2, valid, i):
    normed = normed_tile(u_ref, stat_ref, i)
    z = folded(z_ref[rows_at(i), :]) * vec_ref[0:1, :][None]
    return jnp.where(valid, stat_ref[8:16, :][None] * (z - c1[None] - normed * c2[None]), 0.0)


def adjoint_scan(reverse, carry, sg_ref, s_ref, par_ref, keep_adj_ref, kp_adj_ref, kd_adj_ref, keep_ref, a_ref):
    width = par_ref.shape[1]
    tiles = width // LANE
    behind = 0 if reverse else SUB
    start = enter(*carry, kd_adj_ref, kp_adj_ref, par_ref, reverse, True)
    scale = [jnp.broadcast_to(par_ref[6:7, j * LANE : (j + 1) * LANE], (SUB, LANE)) for j in range(tiles)]

    def visit(t, adjoint, sums):
        at = pl.ds(t * SUB, SUB)
        before = pl.ds(t * SUB + behind, SUB)
        keep = keep_ref[at, :]
        fresh = []
        for j, (re, im) in enumerate(adjoint):
            a_ref[at, j * LANE : (j + 1) * LANE] = re * scale[j]
            a_ref[at, width + j * LANE : width + (j + 1) * LANE] = im * scale[j]
            pr = s_ref[before, j * LANE : (j + 1) * LANE]
            pi = s_ref[before, width + j * LANE : width + (j + 1) * LANE]
            kr, ki = keep * re, keep * im
            fresh.append((sums[j][0] + (kr * pr + ki * pi), sums[j][1] + (ki * pr - kr * pi)))
        return tuple(fresh)

    zero = jnp.zeros((SUB, LANE), F32)
    return Scan(sg_ref, keep_adj_ref, par_ref, start, reverse, True, visit, tuple((zero, zero) for j in range(tiles)))


def put_lam(lg_ref, sums):
    lg_ref[...] = jnp.zeros(lg_ref.shape, F32)
    pack_rows(lg_ref, [
        jnp.sum(jnp.concatenate([part[k] for part in sums], axis=1), axis=0, keepdims=True) for k in range(2)
    ])


def add_drives(gb_ref, low, drive):
    gb = dot_tn(low, drive)
    rows = gb.shape[0]
    gb_ref[:rows, :] += gb[:, :rows]
    gb_ref[rows:, : rows // 2] += gb[: rows // 2, rows:]
    gb_ref[rows:, rows // 2 :] += gb[rows // 2 :, rows:]


def back_to_norm(layer, i, drive, sums, b_ref, vec_ref, mix_ref, lim_ref, u_ref, stat_ref, z_ref):
    at = rows_at(i)
    back = dot_nt(drive, b_ref[layer]) + vec_ref[2:3, :] * mix_ref[at, :].astype(F32)
    z = jnp.where(tile_mask(lim_ref, i), folded(back), 0.0)
    z_ref[at, :] = flat(z)
    return (sums[0] + jnp.sum(z, axis=0), sums[1] + jnp.sum(z * normed_tile(u_ref, stat_ref, i), axis=0))


def put_norm_sums(st_ref, sums):
    a, b = per_micro(sums[0])
    c, d = per_micro(sums[1])
    pack_rows(st_ref, (a, c, b, d))


def k_adjoint(layer, reverse, parts, *refs):
    carry, refs = take_carry(refs, parts)
    (sg_ref, s_ref, mix_ref, ml_ref, u_ref, stat_ref, lim_ref, vec_ref, par_ref,
     keep_adj_ref, kp_adj_ref, kd_adj_ref, keep_ref, b_ref, z_ref, gb_ref, lg_ref, st_ref, a_ref) = refs
    vec_ref, par_ref = of_layer(vec_ref, layer), of_layer(par_ref, layer)
    scan = adjoint_scan(reverse, carry, sg_ref, s_ref, par_ref, keep_adj_ref, kp_adj_ref, kd_adj_ref, keep_ref, a_ref)
    gb_ref[...] = jnp.zeros(gb_ref.shape, F32)
    zero = jnp.zeros(lim_ref.shape, F32)
    sums = (zero, zero)
    for i in scan.ahead():
        drive = a_ref[rows_at(i), :].astype(BF16)
        add_drives(gb_ref, ml_ref[rows_at(i), :], drive)
        sums = back_to_norm(layer, i, drive, sums, b_ref, vec_ref, mix_ref, lim_ref, u_ref, stat_ref, z_ref)
    put_lam(lg_ref, scan.extra)
    put_norm_sums(st_ref, sums)


def k_adjoint_last(layer, reverse, parts, *refs):
    carry, refs = take_carry(refs, parts)
    (sg_ref, s_ref, ml_ref, par_ref, keep_adj_ref, kp_adj_ref, kd_adj_ref, keep_ref,
     drive_ref, gb_ref, lg_ref, a_ref) = refs
    par_ref = of_layer(par_ref, layer)
    scan = adjoint_scan(reverse, carry, sg_ref, s_ref, par_ref, keep_adj_ref, kp_adj_ref, kd_adj_ref, keep_ref, a_ref)
    gb_ref[...] = jnp.zeros(gb_ref.shape, F32)
    for i in scan.ahead():
        drive = a_ref[rows_at(i), :].astype(BF16)
        drive_ref[rows_at(i), :] = drive
        add_drives(gb_ref, ml_ref[rows_at(i), :], drive)
    put_lam(lg_ref, scan.extra)


def k_back(layer, drive_ref, mix_ref, u_ref, stat_ref, lim_ref, vec_ref, b_ref, *refs):
    z_ref, st_ref = refs[-2:]
    vec_ref = of_layer(vec_ref, layer)
    zero = jnp.zeros(lim_ref.shape, F32)
    sums = (zero, zero)
    for i in range(u_ref.shape[0] // TILE):
        sums = back_to_norm(layer, i, drive_ref[rows_at(i), :], sums, b_ref, vec_ref, mix_ref, lim_ref, u_ref, stat_ref, z_ref)
    put_norm_sums(st_ref, sums)
    at = 16
    for ref in refs[:-2]:
        st_ref[at : at + ref.shape[0], :] = ref[...]
        at += ref.shape[0]


def k_output(st_ref, z_ref, grad_ref, u_ref, stat_ref, vec_ref, lim_ref, par_ref, stat1_ref, bn1_ref,
             run_mean_ref, run_var_ref,
             out_ref, gain_ref, shift_ref, skip_ref, bias_ref, rate_ref, rotation_ref, mean_ref, var_ref,
             bn_ref, lines_ref):
    vec0_ref = of_layer(vec_ref, 0)
    c1, c2 = norm_sums(st_ref, stat_ref, vec0_ref, bn_ref)

    def step(i, unused):
        extra = norm_backward(z_ref, u_ref, stat_ref, vec0_ref, c1, c2, tile_mask(lim_ref, i), i)
        put_lines(lines_ref, i, grad_ref[rows_at(i), :] + flat(extra))
        return unused

    lax.fori_loop(0, u_ref.shape[0] // TILE, step, 0, unroll=True)
    spread_out(lines_ref, out_ref)
    width, states = gain_ref.shape[1], rate_ref.shape[1]
    per, per_state = width // LANE, states // LANE

    def line(at, count):
        return jnp.concatenate([st_ref[at + j : at + j + 1, :] for j in range(count)], axis=1)

    for layer, (stats_ref, norms_ref) in enumerate(((stat_ref, bn_ref), (stat1_ref, bn1_ref))):
        row = slice(layer, layer + 1)
        at = 40 - 24 * layer
        bias_ref[row, :] = line(at, per)
        skip_ref[row, :] = line(at + per, per)
        product = line(at + 2 * per, per_state)
        grad_re, grad_im = line(at + 16, per_state), line(at + 16 + per_state, per_state)
        par = of_layer(par_ref, layer)
        lam_re, lam_im, norm_in, decay = par[0:1, :], par[1:2, :], par[6:7, :], par[7:8, :]
        rotation_ref[row, :] = lam_re * grad_im - lam_im * grad_re
        rate_ref[row, :] = decay * (
            product * jnp.exp(-2.0 * decay) / (norm_in * norm_in) - (lam_re * grad_re + lam_im * grad_im)
        )
        shift_ref[row, :] = norms_ref[0:1, :]
        gain_ref[row, :] = norms_ref[1:2, :]
        mean, var = run_mean_ref[row, :], run_var_ref[row, :]
        for micro in range(2):
            mean = (1.0 - momentum) * mean + momentum * stats_ref[24 + micro : 25 + micro, :]
            var = (1.0 - momentum) * var + momentum * stats_ref[26 + micro : 27 + micro, :]
        mean_ref[row, :] = mean
        var_ref[row, :] = var


def k_split(side, x_ref, give_ref):
    half = give_ref.shape[0]
    give_ref[...] = x_ref[pl.ds(pl.multiple_of((1 - side()) * half, SUB), half), :]


def k_fold(before, side, kept_ref, got_ref, give_ref, keep_ref):
    half = give_ref.shape[0]
    base = 0 if before is None else before() * got_ref.shape[0]
    mine = side()
    for ref, at in ((give_ref, (1 - mine) * half), (keep_ref, mine * half)):
        here = kept_ref[pl.ds(pl.multiple_of(base + at, SUB), half), :]
        ref[...] = here + got_ref[pl.ds(pl.multiple_of(at, SUB), half), :]


def k_copy(src_ref, dst_ref):
    dst_ref[...] = src_ref[...]


def k_add(*refs):
    total = refs[1][...]
    for ref in refs[2:-1]:
        total = total + ref[...]
    refs[-1][...] = refs[0][...] + total


def k_join(side, own_ref, got_ref, out_ref):
    half = own_ref.shape[0]
    mine = side()
    out_ref[pl.ds(pl.multiple_of(mine * half, SUB), half), :] = own_ref[...]
    out_ref[pl.ds(pl.multiple_of((1 - mine) * half, SUB), half), :] = got_ref[...]


def copy_all(pairs, sem_ref):
    copies = [pltpu.make_async_copy(src, dst, sem_ref.at[k]) for k, (src, dst) in enumerate(pairs)]
    for copy in copies:
        copy.start()
    for copy in copies:
        copy.wait()


def cut_to(layer, first, src_ref, outs):
    pairs = []
    for begin, end, place in outs:
        low, high = max(begin, first), min(end, first + src_ref.shape[0])
        if low < high:
            pairs.extend(place(src_ref, low - first, low - begin, high - low))
    return pairs


def rows_to(layer, ref):
    return lambda src, at, row, size: [(src.at[pl.ds(at, size), :], ref.at[layer, pl.ds(row, size), :])]


def map_places(layer, *refs):
    places, first = [], 0
    for ref in refs:
        places.append((first, first + ref.shape[1], rows_to(layer, ref)))
        first += ref.shape[1]
    return places


def drive_places(layer, b_ref):
    width = b_ref.shape[1]

    def left(src, at, row, size):
        return [(src.at[pl.ds(at, size), :], b_ref.at[layer, pl.ds(row, size), pl.ds(0, width)])]

    def right(src, at, row, size):
        part = width // 2
        return [
            (src.at[pl.ds(at, size), pl.ds(k * part, part)],
             b_ref.at[layer, pl.ds(k * part + row, size), pl.ds(width, part)])
            for k in range(2)
        ]

    return [(0, width, left), (width, width + width // 2, right)]


def k_place(side, places, layer, count, own_ref, got_ref, *refs):
    token_ref, sem_ref = refs[-2:]
    outs = refs[-2 - count : -2]
    token_ref[...] = jnp.zeros(token_ref.shape, F32)
    half = own_ref.shape[0]
    for mine in range(2):
        @pl.when(side() == mine)
        def _():
            where = places(layer, *outs)
            copy_all(
                cut_to(layer, mine * half, own_ref, where) + cut_to(layer, (1 - mine) * half, got_ref, where), sem_ref
            )


def place(large, places, layer, shapes, into=None):
    count = len(shapes)
    args = [large.block, large.got] + list(into or [])
    alias = {2 + k: k for k in range(count)} if into else {}
    return list(call(
        "place", functools.partial(k_place, large.side(), places, layer, count), shapes + [shaped((SUB, LANE))], args,
        scratch=[pltpu.SemaphoreType.DMA((8,))], order=large.order, token=count, far=range(2, len(args)), alias=alias,
        out_far=count,
    ))[:count]


BOTH = ("batch", "tm")

ORDER = (
    ("AA",),
    ("B", "A", "e", "BA"),
    ("CECE",),
    ("D", "ABSDECBSA", "DCBEADCSBD", "EASCBDECDB", "SCEDALBCAE", "CDBED"),
)


def outer_bits():
    nb, nt = lax.axis_size("batch"), lax.axis_size("tm")
    return [("batch", 1 << k, nt << k) for k in range(nb.bit_length() - 1)]


def line_bits():
    return [("tm", 1 << k, 1 << k) for k in range(1, lax.axis_size("tm").bit_length() - 1)]


def swap(block, distance):
    total = lax.axis_size("batch") * lax.axis_size("tm")
    return lax.ppermute(block, BOTH, [(i, i ^ distance) for i in range(total)])


def swap_by_core(block, even, odd):
    total = lax.axis_size("batch") * lax.axis_size("tm")
    return lax.ppermute(block, BOTH, [(i, i ^ (odd if i & 1 else even)) for i in range(total)])


def sum_four(block, others, order=None):
    block, = call("add", k_add, [shaped(block.shape)], [block, others[0]], order=order, work=1)
    return call("add", k_add, [shaped(block.shape)], [block] + others[1:], order=order, work=1)[0]


def sum_over(block, bits):
    if len(bits) == 2:
        near, far = bits[0][2], bits[1][2]
        return sum_four(block, [swap(block, distance | 1) for distance in (near | far, far, near)])
    for unused, unused, distance in bits:
        block = block + swap(block, distance | 1)
    return block


def sums_of_all(block, fill):
    order = Order()
    got = swap(block, 1)
    order.token = fill()
    block, = call("add", k_add, [shaped(block.shape)], [block, got], order=order)
    return sum_over(sum_over(block, outer_bits()), line_bits())


def sums_in_order(block, order, between):
    for bits, start in zip(([("tm", 1, 0)], outer_bits(), line_bits()), between):
        if len(bits) == 2:
            near, far = bits[0][2], bits[1][2]
            got = [swap(block, distance | 1) for distance in (near | far, far, near)]
            start()
            block = sum_four(block, got, order)
        else:
            for k, bit in enumerate(bits):
                got = swap(block, bit[2] | 1)
                if k == 0:
                    start()
                block, = call("add", k_add, [shaped(block.shape)], [block, got], order=order)
    return block


def carries(e, kd, par, layer, reverse, conj, order=None):
    other = swap(e, 1)
    block, = call("combine", functools.partial(k_combine, layer, reverse, conj), [shaped(e.shape)], [e, other, kd, par],
                  order=order)
    bits = line_bits()
    if len(bits) == 2:
        near, far = bits[0][2], bits[1][2]
        last = swap(block, near | far | 1)
        others = [swap(block, distance | 1) for distance in (near, far)]
        last, = call("copy", k_copy, [shaped(block.shape)], [last], work=1)
        return [block] + others + [last, e, other]
    for unused, unused, distance in bits:
        block = jnp.concatenate((block, swap(block, distance | 1)), axis=0)
    return [block, e, other]


def bit_of(axis, bit):
    return lax.div(lax.axis_index(axis), bit) % 2


def plan(rows, line_first):
    outer, line = outer_bits(), line_bits()
    is_odd = functools.partial(bit_of, "tm", 1)
    steps = []
    for even, odd in zip(outer, outer[::-1]):
        def side(even=even, odd=odd):
            return jnp.where(is_odd() == 1, bit_of(odd[0], odd[1]), bit_of(even[0], even[1]))

        steps.append((side, functools.partial(swap_by_core, even=even[2], odd=odd[2])))
    along = [(functools.partial(bit_of, axis, bit), functools.partial(swap, distance=distance))
             for axis, bit, distance in line]
    steps = [(is_odd, lambda block: swap(block, 1))] + (along + steps if line_first else steps + along)
    most = 3 if line_first else 4
    cuts = 0
    while cuts < len(steps) and rows % (SUB << (cuts + 1)) == 0 and cuts < most:
        cuts += 1
    return steps[:cuts], [exchange for unused, exchange in steps[cuts:]]


class Large:
    def __init__(self, order, block, line_first=False):
        self.order = order
        self.rows, self.width = block.shape
        self.cuts, self.whole = plan(self.rows, line_first)
        self.block = block
        self.at = 0
        self.got = None

    def call(self, name, body, outs):
        args = [self.block] if self.got is None else [self.block, self.got]
        return call(name, body, outs, args, order=self.order)

    def send(self):
        cuts, at = self.cuts, self.at
        count = len(cuts)
        if at < count:
            side, exchange = cuts[at]
            half = shaped((self.rows >> (at + 1), self.width))
            if at == 0:
                give, = self.call("split", functools.partial(k_split, side), [half])
            else:
                before = cuts[0][0] if at == 1 else None
                give, self.block = self.call("fold", functools.partial(k_fold, before, side), [half, half])
        else:
            if at <= count + len(self.whole):
                give, = self.call("add", k_add, [shaped(self.got.shape)])
            else:
                give, = self.call("join", functools.partial(k_join, self.side()), [self.doubled()])
            self.block = give
            exchange = (self.whole + [step[1] for step in cuts[::-1]])[at - count]
        self.got = exchange(give)
        self.at += 1

    def side(self):
        return self.cuts[2 * len(self.cuts) + len(self.whole) - self.at][0]

    def doubled(self):
        return shaped((2 * self.block.shape[0], self.width))

    def left(self):
        return 2 * len(self.cuts) + len(self.whole) - self.at


class Steps:
    def __init__(self, order):
        self.order = order
        self.larges, self.other, self.into, self.shapes = {}, {}, {}, {}

    def add(self, name, block, line_first=False):
        self.larges[name] = Large(self.order, block, line_first)

    def run(self, items):
        for item in items:
            if item in self.other:
                self.other[item]()
            elif self.larges[item].left():
                self.larges[item].send()
            else:
                self.put(item)

    def put(self, item):
        large = self.larges[item]
        while large.left():
            large.send()
        if item == "A":
            w_out, c_out = place(large, map_places, 1, self.shapes["A"])
            self.into.update(E=(w_out, False), C=(c_out, False))
        elif item == "B":
            self.into["D"] = (place(large, drive_places, 1, self.shapes["B"])[0], False)
        else:
            if item not in self.into:
                self.put("B" if item == "D" else "A")
            out, done = self.into[item]
            if not done:
                shape = shaped(out.shape)
                out, = place(large, drive_places if item == "D" else map_places, 0, [shape], [out])
                self.into[item] = (out, True)

    def placed(self, item):
        self.put(item)
        return self.into[item][0]


def small_sum(order, block):
    for distance in [1] + [bit[2] | 1 for bit in outer_bits() + line_bits()]:
        got = swap(block, distance)
        yield None
        block, = call("add", k_add, [shaped(block.shape)], [block, got], order=order)
    yield block


def local(tokens, starts, lengths, cotangent, norm_gain, norm_shift, b_proj, log_rate, rotation, c_proj, skip_gain,
          w_gate, gate_bias, run_mean, run_var):
    rows, length, width = tokens.shape
    states = log_rate.shape[1]
    count = rows * length
    n = lax.axis_size("tm")
    chips = n // 2
    parts = 4 if chips == 4 else 1

    big = lambda w, dtype=F32: shaped((count, w), dtype)
    ends = shaped((SUB, 2 * states))
    kept = shaped((count + SUB, 2 * states))
    small = shaped((16, LANE))
    lines = pltpu.VMEM((width // LANE, count, LANE), F32)
    rows_low, states_low_rows = pltpu.VMEM((count, width), BF16), pltpu.VMEM((count, 2 * states), BF16)
    everyone = pltpu.VMEM((chips, SUB, 2 * states), F32)
    keeps = shaped((count + SUB, LANE))
    vector, state_vector = shaped((2, width)), shaped((2, states))

    u0, st, lim = call("enter", k_input, [big(width), shaped((24, LANE)), shaped((SUB, width), jnp.int32)],
                       [lengths, tokens], scratch=[lines], scalars=1)
    keep_shapes = [keeps, shaped((2 * SUB, LANE)), shaped((n + 1, SUB, LANE))]
    made = []

    def prepare():
        made.extend(call(
            "prepare", k_prepare, keep_shapes + [shaped((2 * SUB, states)), shaped((2 * SUB, width))],
            [starts, log_rate, rotation, norm_gain, norm_shift, skip_gain, gate_bias], scalars=1,
        ))
        return made[1]

    st = sums_of_all(st, prepare)
    keep_f, kp_f, kd_f, par, vec = made
    d0, ml0, m0, stat0, e = call(
        "drive0", functools.partial(k_drive_first, 0, False),
        [big(2 * states), big(width, BF16), big(width), shaped((32, width)), ends],
        [st, u0, lim, vec, par, b_proj, keep_f, kp_f],
    )
    s0, al0, sig0, q0, slope0, u1, st = call(
        "finish0", functools.partial(k_finish_first, 0, parts),
        [kept, big(width, BF16), big(width), big(width), big(width), big(width), small],
        carries(e, kd_f, par, 0, False, False)
        + [d0, u0, m0, lim, vec, par, keep_f, kp_f, kd_f, c_proj, w_gate],
        scratch=[everyone],
    )
    after_first = Order()
    after_first.token = st
    backward = []

    def keep():
        backward.extend(call(
            "keep", functools.partial(k_keep, True), keep_shapes, [starts], scalars=1, order=after_first, token=1,
        ))
        return backward[1]

    st = sums_of_all(st, keep)
    keep_r, kp_r, kd_r = backward
    d1, ml1, m1, stat1, e = call(
        "drive1", functools.partial(k_drive, 1, True),
        [big(2 * states), big(width, BF16), big(width), shaped((32, width)), ends],
        [st, stat0, u1, lim, vec, par, b_proj, keep_r, kp_r],
    )
    grads = [shaped((width + 2 * states, width)), small, ends]
    after_second = Order()
    after_second.token = e
    cot32, = call("cotangent", spread_in, [big(width)], [cotangent], scratch=[lines], order=after_second)
    out32, s1, mix1, sg1, wc1, sums1, e = call(
        "middle", functools.partial(k_middle, 1, parts),
        [shaped((width // LANE, count, LANE)), kept, big(width, BF16), big(2 * states)] + grads,
        carries(e, kd_r, par, 1, True, False, after_second)
        + [d1, u1, m1, lim, vec, par, keep_r, kp_r, kd_r, keep_f, kp_f, c_proj, w_gate, cot32],
        scratch=[rows_low, rows_low, states_low_rows, everyone],
    )
    order = Order()
    order.token = e
    steps = Steps(order)
    steps.add("A", wc1)
    got = carries(e, kd_f, par, 1, False, True, order)
    steps.run(ORDER[0][0])
    adjoint = [big(width), shaped((2 * states, width)), shaped((8, LANE))]
    z1, gb1, lg1, st = call(
        "adjoint1", functools.partial(k_adjoint, 1, False, parts), adjoint + [small],
        got + [sg1, s1, mix1, ml1, u1, stat1, lim, vec, par, keep_f, kp_f, kd_f, keep_r, b_proj],
        scratch=[pltpu.VMEM((count, 2 * states), F32), everyone], order=order, token=3,
    )
    steps.add("B", gb1)
    emitted = []

    def emit():
        emitted.extend(
            call("emit", k_emit, [shaped(tokens.shape, BF16), shaped((SUB, LANE))], [out32], results=1, order=order, token=1)
        )

    steps.other["e"] = emit
    st = sums_in_order(st, order, [functools.partial(steps.run, items) for items in ORDER[1][:3]])
    steps.run(ORDER[1][3])
    g0, mix0, sg0, gw0, gc0, sums0, e, bn1 = call(
        "lower", functools.partial(k_lower, 0),
        [big(width), big(width, BF16), big(2 * states), shaped((width, width)), shaped((2 * states, width)), small, ends,
         shaped((SUB, width))],
        [st, z1, cot32, u1, stat1, lim, s0, al0, sig0, q0, slope0, m0, vec, par,
         c_proj, w_gate, keep_r, kp_r],
        scratch=[rows_low, states_low_rows], order=order, token=6,
    )
    steps.add("E", gw0, True)
    steps.add("C", gc0)
    got = carries(e, kd_r, par, 0, True, True, order)
    steps.run(ORDER[2][0])
    drive0, gb0, lg0 = call(
        "adjoint0", functools.partial(k_adjoint_last, 0, True, parts), [big(2 * states, BF16)] + adjoint[1:],
        got + [sg0, s0, ml0, par, keep_r, kp_r, kd_r, keep_f],
        scratch=[pltpu.VMEM((count, 2 * states), F32), everyone], order=order, token=2,
    )
    steps.add("D", gb0)
    steps.shapes = {
        "A": [shaped((2, width, width)), shaped((2, 2 * states, width))],
        "B": [shaped((2, width, 2 * states))],
    }
    steps.run(ORDER[3][0])
    z0, st = call(
        "back", functools.partial(k_back, 0), [big(width), shaped((64, LANE))],
        [drive0, mix0, u0, stat0, lim, vec, b_proj, sums1, lg1, sums0, lg0], order=order, token=1,
    )
    small_steps = small_sum(order, st)
    last = []

    def small():
        last.extend(item for item in [next(small_steps, None)] if item is not None)

    def leave():
        while not last:
            small()
        last.extend(call(
            "leave", k_output,
            [shaped(tokens.shape), vector, vector, vector, vector, state_vector, state_vector, vector, vector,
             shaped((SUB, width))],
            [last[0], z0, g0, u0, stat0, vec, lim, par, stat1, bn1, run_mean, run_var],
            scratch=[lines], results=9, order=order, token=9,
        ))

    steps.other.update({"S": small, "L": leave})
    steps.run("".join(ORDER[3][1:]))
    (tokens_grad, grad_gain, grad_shift, grad_skip, grad_bias, grad_rate, grad_rotation, new_mean, new_var) = last[1:10]
    output, grad_w, grad_c, grad_b = emitted[0], steps.placed("E"), steps.placed("C"), steps.placed("D")
    return (output, tokens_grad, grad_gain, grad_shift, grad_b, grad_rate, grad_rotation, grad_c, grad_skip, grad_w,
            grad_bias, new_mean, new_var)


def solution(mesh):
    tokens_spec = P("batch", "tm", None)
    return jax.shard_map(
        local,
        mesh=mesh,
        in_specs=(tokens_spec, P("batch", None), P("batch"), tokens_spec) + (P(),) * 11,
        out_specs=(tokens_spec, tokens_spec) + (P(),) * 11,
        check_vma=False,
    )
```

```python
import functools
import math

import jax
import jax.numpy as jnp
from jax import lax
from jax.experimental import pallas as pl
from jax.experimental.pallas import tpu as pltpu
from jax.sharding import PartitionSpec as P

epsilon = 1e-05
momentum = 0.1
F32 = jnp.float32
BF16 = jnp.bfloat16

SUB = 8
LANE = 128
TILE = 256
WORK = 5 * 10**9


def in_vmem(count):
    return [pl.BlockSpec(memory_space=pltpu.VMEM)] * count


class Order:
    def __init__(self):
        self.token = None


def call(name, body, outs, args, scratch=(), scalars=0, results=0, order=None, token=0, far=(), alias=None, out_far=0, work=WORK):
    room = 6 * 1024 * 1024 + sum(4 * math.prod(item.shape) for item in list(scratch) + list(outs[:results]) if hasattr(item, "shape"))
    specs = [pl.BlockSpec(memory_space=pltpu.SMEM)] * scalars + in_vmem(len(args) - scalars)
    for k in far:
        specs[k] = pl.BlockSpec(memory_space=pltpu.HBM)
    count = len(args)
    args = list(args)
    run = body
    if order is not None and order.token is not None:
        args.append(order.token)
        specs.append(pl.BlockSpec(memory_space=pl.ANY))
        run = lambda *refs: body(*refs[:count], *refs[count + 1 :])
    out_specs = in_vmem(len(outs))
    for k in range(out_far):
        out_specs[k] = pl.BlockSpec(memory_space=pltpu.HBM)
    done = pl.pallas_call(
        run,
        name=name,
        out_shape=outs,
        in_specs=specs,
        out_specs=out_specs,
        scratch_shapes=list(scratch),
        input_output_aliases=alias or {},
        compiler_params=pltpu.CompilerParams(vmem_limit_bytes=room),
        cost_estimate=pl.CostEstimate(flops=work, bytes_accessed=1, transcendentals=0),
    )(*args)
    if order is not None:
        order.token = done[token]
    return done


def shaped(shape, dtype=F32):
    return jax.ShapeDtypeStruct(shape, dtype)


def tile_mask(lim_ref, i):
    steps = TILE // SUB
    t = lax.broadcasted_iota(jnp.int32, (steps,) + lim_ref.shape, 0) + i * steps
    return t < lim_ref[...][None]


def folded(values):
    return values.reshape((values.shape[0] // SUB, SUB, values.shape[1]))


def flat(values):
    return values.reshape((values.shape[0] * SUB, values.shape[2]))


def times(ar, ai, br, bi):
    return (ar * br - ai * bi, ar * bi + ai * br)


class Scan:
    def __init__(self, d_ref, keep_ref, par_ref, start, reverse, conj, visit=None, extra=()):
        self.d_ref, self.keep_ref, self.reverse = d_ref, keep_ref, reverse
        self.width = par_ref.shape[1]
        self.visit, self.extra = visit, extra
        self.lanes = [slice(j * LANE, (j + 1) * LANE) for j in range(self.width // LANE)]
        self.lam = []
        for lanes in self.lanes:
            re = jnp.broadcast_to(par_ref[0:1, lanes], (SUB, LANE))
            im = jnp.broadcast_to(par_ref[1:2, lanes], (SUB, LANE))
            self.lam.append((re, -im if conj else im))
        self.state = [(start[0][:, lanes], start[1][:, lanes]) for lanes in self.lanes]

    def tiles(self):
        count = self.d_ref.shape[0] // TILE
        return range(count - 1, -1, -1) if self.reverse else range(count)

    def ahead(self):
        order = list(self.tiles())
        self.run(order[0])
        for k, i in enumerate(order):
            if k + 1 < len(order):
                self.run(order[k + 1])
            yield i

    def run(self, i):
        steps = TILE // SUB
        for k in range(steps):
            t = i * steps + (steps - 1 - k if self.reverse else k)
            at = pl.ds(t * SUB, SUB)
            keep = self.keep_ref[at, :]
            fresh = []
            for (re, im), (lam_re, lam_im), lanes in zip(self.state, self.lam, self.lanes):
                a, b = keep * lam_re, keep * lam_im
                dr = self.d_ref[at, lanes]
                di = self.d_ref[at, lanes.start + self.width : lanes.stop + self.width]
                fresh.append((a * re - b * im + dr, a * im + b * re + di))
            self.state = fresh
            if self.visit is not None:
                self.extra = self.visit(t, fresh, self.extra)

    def ends(self):
        return tuple(jnp.concatenate([part[k] for part in self.state], axis=1) for k in range(2))


def wide(values, width):
    return jnp.concatenate([values] * (width // LANE), axis=1)


def chunk_end(ends, kp_ref, par_ref, reverse, conj):
    width = par_ref.shape[1]
    re, im = ends
    shift = SUB - 1 if reverse else 1
    pr, pi = pltpu.roll(re, shift, 0), pltpu.roll(im, shift, 0)
    keep = wide(kp_ref[:SUB, :], width)
    lr = keep * par_ref[2:3, :]
    li = keep * par_ref[3:4, :]
    li = -li if conj else li
    qr, qi = times(lr, li, pr, pi)
    odd = lax.broadcasted_iota(jnp.int32, (SUB, width), 0) % 2
    last = odd == (0 if reverse else 1)
    return jnp.where(last, qr + re, re), jnp.where(last, qi + im, im)


def chip_and_core():
    me = lax.axis_index("tm")
    return me // 2, me % 2


def enter(got_refs, e_ref, other_ref, all_ref, kd_ref, kp_ref, par_ref, reverse, conj):
    width = par_ref.shape[1]
    chips = all_ref.shape[0]
    chip, core = chip_and_core()
    sign = -1.0 if conj else 1.0
    at = 0
    for ref in got_refs:
        for k in range(ref.shape[0] // SUB):
            all_ref[at] = ref[k * SUB : (k + 1) * SUB, :]
            at += 1
    lr, li = par_ref[4:5, :], sign * par_ref[5:6, :]
    cr, ci = times(lr, li, lr, li)
    lr, li, cr, ci = (jnp.broadcast_to(x, (SUB, width)) for x in (lr, li, cr, ci))

    def step(i, x):
        j = chips - 1 - i if reverse else i
        keep = wide(kd_ref[2 * j] * kd_ref[2 * j + 1], width)
        qr, qi = times(keep * cr, keep * ci, x[0], x[1])
        use = (j > chip) if reverse else (j < chip)
        use = jnp.where(use, 1.0, 0.0)
        k = jnp.bitwise_xor(j, chip)
        nr = qr + all_ref[k, :, :width]
        ni = qi + all_ref[k, :, width:]
        return (x[0] + use * (nr - x[0]), x[1] + use * (ni - x[1]))

    zero = jnp.zeros((SUB, width), F32)
    xr, xi = lax.fori_loop(0, chips, step, (zero, zero), unroll=chips <= 4)
    first = 1 if reverse else 0
    keep = wide(kd_ref[2 * chip + first], width)
    qr, qi = times(keep * lr, keep * li, xr, xi)
    use = jnp.where(core == first, 0.0, 1.0)
    xr = xr + use * (qr + other_ref[:, :width] - xr)
    xi = xi + use * (qi + other_ref[:, width:] - xi)
    near, far = (1, SUB - 1) if reverse else (SUB - 1, 1)
    sr, si = pltpu.roll(xr, near, 0), pltpu.roll(xi, near, 0)
    keep = wide(kp_ref[:SUB, :], width)
    hr = keep * par_ref[2:3, :]
    hi = sign * keep * par_ref[3:4, :]
    tr, ti = times(hr, hi, sr, si)
    tr = pltpu.roll(tr + e_ref[:, :width], far, 0)
    ti = pltpu.roll(ti + e_ref[:, width:], far, 0)
    odd = lax.broadcasted_iota(jnp.int32, (SUB, width), 0) % 2
    second = odd == (0 if reverse else 1)
    return jnp.where(second, tr, sr), jnp.where(second, ti, si)


def put_ends(e_ref, ends):
    e_ref[...] = jnp.concatenate(ends, axis=1)


def zeros_state(par_ref):
    zero = jnp.zeros((SUB, par_ref.shape[1]), F32)
    return (zero, zero)


def per_micro(values):
    return (
        jnp.sum(values[0:4], axis=0, keepdims=True),
        jnp.sum(values[4:8], axis=0, keepdims=True),
    )


def pack_rows(out_ref, rows):
    at = 0
    for row in rows:
        for j in range(row.shape[1] // LANE):
            out_ref[at : at + 1, :] = row[:, j * LANE : (j + 1) * LANE]
            at += 1


def unpack_rows(values, count, width):
    tiles = width // LANE
    return [
        jnp.concatenate(
            [values[r * tiles + j : r * tiles + j + 1, :] for j in range(tiles)], axis=1
        )
        for r in range(count)
    ]


def by_micro(first, second):
    sub = lax.broadcasted_iota(jnp.int32, (SUB, first.shape[1]), 0)
    return jnp.where(sub < 4, jnp.broadcast_to(first, sub.shape), jnp.broadcast_to(second, sub.shape))


def dot(a, b):
    return jnp.dot(a, b, preferred_element_type=F32)


def dot_nt(a, b):
    return lax.dot_general(a, b, (((1,), (1,)), ((), ())), preferred_element_type=F32)


def dot_tn(a, b):
    return lax.dot_general(a, b, (((0,), (0,)), ((), ())), preferred_element_type=F32)


def normed_tile(u_ref, stat_ref, i):
    x = folded(u_ref[pl.ds(pl.multiple_of(i * TILE, TILE), TILE), :])
    return (x - stat_ref[0:8, :][None]) * stat_ref[8:16, :][None]


def masked_tile(u_ref, stat_ref, vec_ref, lim_ref, i):
    normed = normed_tile(u_ref, stat_ref, i)
    z = normed * vec_ref[0:1, :][None] + vec_ref[1:2, :][None]
    return jnp.where(tile_mask(lim_ref, i), z, 0.0)


def rows_at(i):
    return pl.ds(pl.multiple_of(i * TILE, TILE), TILE)


def spread_in(src_ref, dst_ref, lines_ref):
    half = src_ref.shape[1] // 2
    tiles = src_ref.shape[2] // LANE
    for s in range(SUB):
        part = src_ref[s // 2, (s % 2) * half : (s % 2 + 1) * half, :].astype(F32)
        for j in range(tiles):
            lines_ref[j, pl.ds(s, half, stride=SUB), :] = part[:, j * LANE : (j + 1) * LANE]
    for j in range(tiles):
        dst_ref[:, j * LANE : (j + 1) * LANE] = lines_ref[j]


def spread_out(lines_ref, dst_ref):
    half = dst_ref.shape[1] // 2
    tiles = dst_ref.shape[2] // LANE
    for s in range(SUB):
        for j in range(tiles):
            part = lines_ref[j, pl.ds(s, half, stride=SUB), :]
            dst_ref[s // 2, (s % 2) * half : (s % 2 + 1) * half, j * LANE : (j + 1) * LANE] = part.astype(dst_ref.dtype)


def k_emit(lines_ref, out_ref, token_ref):
    token_ref[...] = jnp.zeros(token_ref.shape, F32)
    spread_out(lines_ref, out_ref)


def put_lines(lines_ref, i, values):
    for j in range(lines_ref.shape[0]):
        lines_ref[j, rows_at(i), :] = values[:, j * LANE : (j + 1) * LANE]


def moment_sums(u_ref, lim_ref, upto):
    def step(i, sums):
        x = jnp.where(tile_mask(lim_ref, i), folded(u_ref[rows_at(i), :]), 0.0)
        return (sums[0] + jnp.sum(x, axis=0), sums[1] + jnp.sum(x * x, axis=0))

    zero = jnp.zeros(lim_ref.shape, F32)
    return lax.fori_loop(0, upto, step, (zero, zero))


def fill_lim(lengths_ref, lim_ref, half):
    sub = lax.broadcasted_iota(jnp.int32, lim_ref.shape, 0)
    length = jnp.zeros(lim_ref.shape, jnp.int32)
    for r in range(lengths_ref.shape[0]):
        length = jnp.where(sub // 2 == r, lengths_ref[r], length)
    lim_ref[...] = length - lax.axis_index("tm") * (2 * half) - (sub % 2) * half


def k_input(lengths_ref, tokens_ref, u_ref, st_ref, lim_ref, lines_ref):
    half = tokens_ref.shape[1] // 2
    fill_lim(lengths_ref, lim_ref, half)
    spread_in(tokens_ref, u_ref, lines_ref)
    sums, squares = moment_sums(u_ref, lim_ref, u_ref.shape[0] // TILE)
    a, b = per_micro(sums)
    c, d = per_micro(squares)
    st_ref[...] = jnp.zeros(st_ref.shape, F32)
    pack_rows(st_ref, (a, c, b, d))
    counts = jnp.clip(lim_ref[:, :LANE], 0, half).astype(F32)
    a, b = per_micro(counts)
    st_ref[16:17, :] = a
    st_ref[17:18, :] = b


def one_minus_exp(x):
    series = jnp.full(x.shape, 1.0 / 9.0, F32)
    for k in range(8, 0, -1):
        series = (1.0 - x * series) / k if k > 1 else 1.0 - x * series
    return jnp.where(x < 0.5, x * series, 1.0 - jnp.exp(-x))


def k_keep(reverse, starts_ref, keep_ref, kp_ref, kd_ref):
    count = keep_ref.shape[0] - SUB
    steps = count // SUB
    length = 2 * steps
    n = kd_ref.shape[0] - 1
    base = lax.axis_index("tm") * length
    for ref in (keep_ref, kp_ref, kd_ref):
        ref[...] = jnp.ones(ref.shape, F32)
    none = jnp.zeros((1, LANE), F32)

    def mark(r, place):
        local = place - base
        here = (local >= 0) & (local < length)
        second = jnp.where(local >= steps, 1, 0)
        row = (local - second * steps) * SUB + 2 * r + second
        keep_ref[pl.ds(jnp.where(here, row, count), 1), :] = none
        kp_ref[pl.ds(jnp.where(here, 2 * r + second, SUB), 1), :] = none

    def each(k, unused):
        for r in range(starts_ref.shape[0]):
            place = starts_ref[r, k] - (1 if reverse else 0)
            mark(r, place)
            device = jnp.where(place >= 0, lax.div(place, length), n)
            kd_ref[device, 2 * r : 2 * r + 2, :] = jnp.zeros((2, LANE), F32)
        return unused

    lax.fori_loop(0, starts_ref.shape[1], each, 0)
    if reverse:
        for r in range(starts_ref.shape[0]):
            mark(r, n * length - 1)


def k_prepare(starts_ref, rate_ref, rotation_ref, gain_ref, shift_ref, skip_ref, bias_ref,
              keep_ref, kp_ref, kd_ref, par_ref, vec_ref):
    k_keep(False, starts_ref, keep_ref, kp_ref, kd_ref)
    doublings = ((keep_ref.shape[0] - SUB) // SUB).bit_length() - 1
    for layer in range(2):
        decay = jnp.exp(rate_ref[layer : layer + 1, :])
        magnitude = jnp.exp(-decay)
        angle = rotation_ref[layer : layer + 1, :]
        re, im = magnitude * jnp.cos(angle), magnitude * jnp.sin(angle)
        at = layer * SUB
        norm_in = jnp.sqrt(one_minus_exp(2.0 * decay))
        par_ref[at : at + 1, :] = re
        par_ref[at + 1 : at + 2, :] = im
        for unused in range(doublings):
            re, im = times(re, im, re, im)
        par_ref[at + 2 : at + 3, :] = re
        par_ref[at + 3 : at + 4, :] = im
        re, im = times(re, im, re, im)
        par_ref[at + 4 : at + 5, :] = re
        par_ref[at + 5 : at + 6, :] = im
        par_ref[at + 6 : at + 7, :] = norm_in
        par_ref[at + 7 : at + 8, :] = decay
        vec_ref[at : at + SUB, :] = jnp.zeros((SUB, vec_ref.shape[1]), F32)
        for k, ref in enumerate((gain_ref, shift_ref, skip_ref, bias_ref)):
            vec_ref[at + k : at + k + 1, :] = ref[layer : layer + 1, :]


def of_layer(ref, layer):
    return ref.at[layer * SUB : (layer + 1) * SUB]


def k_combine(layer, reverse, conj, e_ref, other_ref, kd_ref, par_ref, out_ref):
    par_ref = of_layer(par_ref, layer)
    width = par_ref.shape[1]
    chip, core = chip_and_core()
    keep = wide(kd_ref[2 * chip + (0 if reverse else 1)], width)
    lr = keep * par_ref[4:5, :]
    li = keep * par_ref[5:6, :] * (-1.0 if conj else 1.0)
    is_first = core == (1 if reverse else 0)
    e, other = e_ref[...], other_ref[...]
    pick = jnp.where(is_first, 1.0, 0.0)
    first = other + pick * (e - other)
    last = e + pick * (other - e)
    qr, qi = times(lr, li, first[:, :width], first[:, width:])
    out_ref[...] = jnp.concatenate((qr, qi), axis=1) + last


def k_drive(layer, reverse, st_ref, cnt_ref, u_ref, lim_ref, vec_ref, par_ref, b_ref, keep_ref, kp_ref,
            d_ref, ml_ref, m_ref, stat_ref, e_ref):
    vec_ref, par_ref = of_layer(vec_ref, layer), of_layer(par_ref, layer)
    total = st_ref[...]
    a, c, b, d = unpack_rows(total, 4, u_ref.shape[1])
    if cnt_ref is None:
        counts = (total[16:17, :], total[17:18, :])
    else:
        counts = (cnt_ref[28:29, :LANE], cnt_ref[29:30, :LANE])
    parts = []
    for summed, squares, count in ((a, c, counts[0]), (b, d, counts[1])):
        inverse = 1.0 / wide(count, u_ref.shape[1])
        center = summed * inverse
        spread = squares * inverse - center * center
        parts.append((center, spread, lax.rsqrt(spread + epsilon), inverse))
    stat_ref[0:8, :] = by_micro(parts[0][0], parts[1][0])
    stat_ref[8:16, :] = by_micro(parts[0][2], parts[1][2])
    stat_ref[16:24, :] = by_micro(parts[0][3], parts[1][3])
    stat_ref[24:25, :] = parts[0][0]
    stat_ref[25:26, :] = parts[1][0]
    stat_ref[26:27, :] = parts[0][1]
    stat_ref[27:28, :] = parts[1][1]
    stat_ref[28:29, :] = wide(counts[0], u_ref.shape[1])
    stat_ref[29:30, :] = wide(counts[1], u_ref.shape[1])
    stat_ref[30:32, :] = jnp.zeros((2, u_ref.shape[1]), F32)
    both = jnp.concatenate((par_ref[6:7, :], par_ref[6:7, :]), axis=1)

    def step(i, unused):
        masked = flat(masked_tile(u_ref, stat_ref, vec_ref, lim_ref, i))
        m_ref[rows_at(i), :] = masked
        low = masked.astype(BF16)
        ml_ref[rows_at(i), :] = low
        d_ref[rows_at(i), :] = dot(low, b_ref[layer]) * both
        return unused

    scan = Scan(d_ref, keep_ref, par_ref, zeros_state(par_ref), reverse, False)
    for i in scan.tiles():
        step(i, 0)
        scan.run(i)
    put_ends(e_ref, chunk_end(scan.ends(), kp_ref, par_ref, reverse, False))


def k_drive_first(layer, reverse, st_ref, *refs):
    k_drive(layer, reverse, st_ref, None, *refs)


def run_states(carry, d_ref, keep_ref, kp_ref, kd_ref, par_ref, s_ref, reverse):
    width = par_ref.shape[1]
    first = 0 if reverse else SUB
    start = enter(*carry, kd_ref, kp_ref, par_ref, reverse, False)
    s_ref[(s_ref.shape[0] - SUB if reverse else 0) : (s_ref.shape[0] if reverse else SUB), :] = (
        jnp.concatenate(start, axis=1)
    )

    def visit(t, states, extra):
        at = pl.ds(t * SUB + first, SUB)
        for j, (re, im) in enumerate(states):
            s_ref[at, j * LANE : (j + 1) * LANE] = re
            s_ref[at, width + j * LANE : width + (j + 1) * LANE] = im
        return extra

    return first, Scan(d_ref, keep_ref, par_ref, start, reverse, False, visit)


def sigmoid(x):
    return 0.5 + 0.5 * jnp.tanh(0.5 * x)


def gelu_parts(x):
    cdf = 0.5 * (1.0 + lax.erf(x * 0.7071067811865476))
    return x * cdf, cdf + x * jnp.exp(-0.5 * x * x) * 0.3989422804014327


def states_low(s_ref, first, i):
    return s_ref[pl.ds(pl.multiple_of(i * TILE + first, SUB), TILE), :].astype(BF16)


def take_carry(refs, parts):
    return (refs[:parts], refs[parts], refs[parts + 1], refs[-1]), refs[parts + 2 : -1]


def k_finish_first(layer, parts, *refs):
    carry, refs = take_carry(refs, parts)
    (d_ref, u_ref, m_ref, lim_ref, vec_ref, par_ref, keep_ref, kp_ref, kd_ref, c_ref, w_ref,
     s_ref, al_ref, sig_ref, q_ref, slope_ref, next_ref, st_ref) = refs
    vec_ref, par_ref = of_layer(vec_ref, layer), of_layer(par_ref, layer)
    first, scan = run_states(carry, d_ref, keep_ref, kp_ref, kd_ref, par_ref, s_ref, False)

    def step(i, sums):
        at = rows_at(i)
        valid = tile_mask(lim_ref, i)
        mixed = dot(states_low(s_ref, first, i), c_ref[layer]) + vec_ref[2:3, :] * m_ref[at, :]
        active, slope = gelu_parts(mixed)
        low = active.astype(BF16)
        sig = sigmoid(dot(low, w_ref[layer]) + vec_ref[3:4, :])
        gated = active * sig
        al_ref[at, :] = low
        sig_ref[at, :] = sig
        slope_ref[at, :] = slope
        q_ref[at, :] = gated * (1.0 - sig)
        fresh = folded(u_ref[at, :]) + jnp.where(valid, folded(gated), 0.0)
        next_ref[at, :] = flat(fresh)
        x = jnp.where(valid, fresh, 0.0)
        return (sums[0] + jnp.sum(x, axis=0), sums[1] + jnp.sum(x * x, axis=0))

    zero = jnp.zeros(lim_ref.shape, F32)
    totals = (zero, zero)
    for i in scan.ahead():
        totals = step(i, totals)
    sums, squares = totals
    a, b = per_micro(sums)
    c, d = per_micro(squares)
    pack_rows(st_ref, (a, c, b, d))


def gate_backward(layer, upstream, q, sig, slope, masked, state, c_ref, w_ref, gate_ref, mix_ref, sg_ref, i):
    at = rows_at(i)
    gate = (upstream * q).astype(BF16)
    gate_ref[at, :] = gate
    act = upstream * sig + dot_nt(gate, w_ref[layer])
    mix = (act * slope).astype(BF16)
    mix_ref[at, :] = mix
    sg = dot_nt(mix, c_ref[layer])
    sg_ref[at, :] = sg
    wide_sum = jnp.sum(folded(sg * state), axis=0)
    half = wide_sum.shape[1] // 2
    return (
        jnp.sum(folded(gate.astype(F32)), axis=0),
        jnp.sum(folded(mix.astype(F32) * masked), axis=0),
        wide_sum[:, :half] + wide_sum[:, half:],
    )


def put_sums(sums_ref, sums):
    sums_ref[...] = jnp.zeros(sums_ref.shape, F32)
    pack_rows(sums_ref, [jnp.sum(part, axis=0, keepdims=True) for part in sums])


def zero_sums(width, states):
    return (jnp.zeros((SUB, width), F32), jnp.zeros((SUB, width), F32), jnp.zeros((SUB, states), F32))


class Ends:
    def __init__(self, keep_ref, par_ref):
        self.keep_ref = keep_ref
        re, im = par_ref[0:1, :], -par_ref[1:2, :]
        for unused in range((TILE // SUB).bit_length() - 1):
            re, im = times(re, im, re, im)
        self.step = tuple(jnp.broadcast_to(part, (SUB, part.shape[1])) for part in (re, im))
        self.factor = self.total = None

    def put_before(self, i, ends):
        if self.total is None:
            self.total = ends
        else:
            re, im = times(*self.factor, *ends)
            self.total = (self.total[0] + re, self.total[1] + im)
        keep = wide(jnp.min(folded(self.keep_ref[i * TILE : (i + 1) * TILE, :]), axis=0), ends[0].shape[1])
        here = tuple(keep * part for part in self.step)
        self.factor = here if self.factor is None else times(*self.factor, *here)


def k_middle(layer, parts, *refs):
    carry, refs = take_carry(refs, parts)
    (d_ref, u_ref, m_ref, lim_ref, vec_ref, par_ref, keep_ref, kp_ref, kd_ref,
     keep_adj_ref, kp_adj_ref, c_ref, w_ref, cot32_ref,
     lines_ref, s_ref, mix_ref, sg_ref, wc_ref, sums_ref, e_ref, al_ref, gate_ref, slow_ref) = refs
    vec_ref, par_ref = of_layer(vec_ref, layer), of_layer(par_ref, layer)
    first, scan = run_states(carry, d_ref, keep_ref, kp_ref, kd_ref, par_ref, s_ref, True)

    def step(i, sums):
        at = rows_at(i)
        valid = tile_mask(lim_ref, i)
        masked = m_ref[at, :]
        state = s_ref[pl.ds(pl.multiple_of(i * TILE + first, SUB), TILE), :]
        s_low = state.astype(BF16)
        mixed = dot(s_low, c_ref[layer]) + vec_ref[2:3, :] * masked
        active, slope = gelu_parts(mixed)
        low = active.astype(BF16)
        sig = sigmoid(dot(low, w_ref[layer]) + vec_ref[3:4, :])
        gated = active * sig
        put_lines(lines_ref, i, flat(folded(u_ref[at, :]) + jnp.where(valid, folded(gated), 0.0)))
        upstream = flat(jnp.where(valid, folded(cot32_ref[at, :]), 0.0))
        al_ref[at, :] = low
        slow_ref[at, :] = s_low
        more = gate_backward(layer, upstream, gated * (1.0 - sig), sig, slope, masked, state,
                             c_ref, w_ref, gate_ref, mix_ref, sg_ref, i)
        return tuple(x + y for x, y in zip(sums, more))

    sums = zero_sums(u_ref.shape[1], par_ref.shape[1])
    ends = Ends(keep_adj_ref, par_ref)
    for i in scan.ahead():
        sums = step(i, sums)
        local = Scan(sg_ref, keep_adj_ref, par_ref, zeros_state(par_ref), False, True)
        local.run(i)
        ends.put_before(i, local.ends())
    wc_ref[: u_ref.shape[1], :] = dot_tn(al_ref[...], gate_ref[...])
    wc_ref[u_ref.shape[1] :, :] = dot_tn(slow_ref[...], mix_ref[...])
    put_sums(sums_ref, sums)
    put_ends(e_ref, chunk_end(ends.total, kp_adj_ref, par_ref, False, True))


def k_lower(layer, st_ref, z_ref, cot32_ref, u1_ref, stat1_ref, lim_ref,
            s_ref, al_ref, sig_ref, q_ref, slope_ref, m_ref, vec_ref, par_ref, c_ref, w_ref,
            keep_adj_ref, kp_adj_ref,
            grad_ref, mix_ref, sg_ref, gw_ref, gc_ref, sums_ref, e_ref, bn_ref, gate_ref, slow_ref):
    vec1_ref = of_layer(vec_ref, layer + 1)
    vec_ref, par_ref = of_layer(vec_ref, layer), of_layer(par_ref, layer)
    first = SUB
    c1, c2 = norm_sums(st_ref, stat1_ref, vec1_ref, bn_ref)

    def step(i, sums):
        at = rows_at(i)
        valid = tile_mask(lim_ref, i)
        extra = norm_backward(z_ref, u1_ref, stat1_ref, vec1_ref, c1, c2, valid, i)
        grad = folded(cot32_ref[at, :]) + extra
        grad_ref[at, :] = flat(grad)
        upstream = flat(jnp.where(valid, grad, 0.0))
        masked = m_ref[at, :]
        state = s_ref[pl.ds(pl.multiple_of(i * TILE + first, SUB), TILE), :]
        slow_ref[at, :] = state.astype(BF16)
        more = gate_backward(layer, upstream, q_ref[at, :], sig_ref[at, :], slope_ref[at, :], masked,
                             state, c_ref, w_ref, gate_ref, mix_ref, sg_ref, i)
        return tuple(x + y for x, y in zip(sums, more))

    sums = zero_sums(m_ref.shape[1], par_ref.shape[1])
    scan = Scan(sg_ref, keep_adj_ref, par_ref, zeros_state(par_ref), True, True)
    for i in scan.tiles():
        sums = step(i, sums)
        scan.run(i)
    gw_ref[...] = dot_tn(al_ref[...], gate_ref[...])
    gc_ref[...] = dot_tn(slow_ref[...], mix_ref[...])
    put_sums(sums_ref, sums)
    put_ends(e_ref, chunk_end(scan.ends(), kp_adj_ref, par_ref, True, True))


def norm_sums(st_ref, stat_ref, vec_ref, bn_ref):
    width = vec_ref.shape[1]
    a, c, b, d = unpack_rows(st_ref[...], 4, width)
    bn_ref[...] = jnp.concatenate((a + b, c + d, jnp.zeros((6, width), F32)), axis=0)
    gain = vec_ref[0:1, :]
    inverse = stat_ref[16:24, :]
    return by_micro(a * gain, b * gain) * inverse, by_micro(c * gain, d * gain) * inverse


def norm_backward(z_ref, u_ref, stat_ref, vec_ref, c1, c2, valid, i):
    normed = normed_tile(u_ref, stat_ref, i)
    z = folded(z_ref[rows_at(i), :]) * vec_ref[0:1, :][None]
    return jnp.where(valid, stat_ref[8:16, :][None] * (z - c1[None] - normed * c2[None]), 0.0)


def adjoint_scan(reverse, carry, sg_ref, s_ref, par_ref, keep_adj_ref, kp_adj_ref, kd_adj_ref, keep_ref, a_ref):
    width = par_ref.shape[1]
    tiles = width // LANE
    behind = 0 if reverse else SUB
    start = enter(*carry, kd_adj_ref, kp_adj_ref, par_ref, reverse, True)
    scale = [jnp.broadcast_to(par_ref[6:7, j * LANE : (j + 1) * LANE], (SUB, LANE)) for j in range(tiles)]

    def visit(t, adjoint, sums):
        at = pl.ds(t * SUB, SUB)
        before = pl.ds(t * SUB + behind, SUB)
        keep = keep_ref[at, :]
        fresh = []
        for j, (re, im) in enumerate(adjoint):
            a_ref[at, j * LANE : (j + 1) * LANE] = re * scale[j]
            a_ref[at, width + j * LANE : width + (j + 1) * LANE] = im * scale[j]
            pr = s_ref[before, j * LANE : (j + 1) * LANE]
            pi = s_ref[before, width + j * LANE : width + (j + 1) * LANE]
            kr, ki = keep * re, keep * im
            fresh.append((sums[j][0] + (kr * pr + ki * pi), sums[j][1] + (ki * pr - kr * pi)))
        return tuple(fresh)

    zero = jnp.zeros((SUB, LANE), F32)
    return Scan(sg_ref, keep_adj_ref, par_ref, start, reverse, True, visit, tuple((zero, zero) for j in range(tiles)))


def put_lam(lg_ref, sums):
    lg_ref[...] = jnp.zeros(lg_ref.shape, F32)
    pack_rows(lg_ref, [
        jnp.sum(jnp.concatenate([part[k] for part in sums], axis=1), axis=0, keepdims=True) for k in range(2)
    ])


def add_drives(gb_ref, low, drive):
    gb = dot_tn(low, drive)
    rows = gb.shape[0]
    gb_ref[:rows, :] += gb[:, :rows]
    gb_ref[rows:, : rows // 2] += gb[: rows // 2, rows:]
    gb_ref[rows:, rows // 2 :] += gb[rows // 2 :, rows:]


def back_to_norm(layer, i, drive, sums, b_ref, vec_ref, mix_ref, lim_ref, u_ref, stat_ref, z_ref):
    at = rows_at(i)
    back = dot_nt(drive, b_ref[layer]) + vec_ref[2:3, :] * mix_ref[at, :].astype(F32)
    z = jnp.where(tile_mask(lim_ref, i), folded(back), 0.0)
    z_ref[at, :] = flat(z)
    return (sums[0] + jnp.sum(z, axis=0), sums[1] + jnp.sum(z * normed_tile(u_ref, stat_ref, i), axis=0))


def put_norm_sums(st_ref, sums):
    a, b = per_micro(sums[0])
    c, d = per_micro(sums[1])
    pack_rows(st_ref, (a, c, b, d))


def k_adjoint(layer, reverse, parts, *refs):
    carry, refs = take_carry(refs, parts)
    (sg_ref, s_ref, mix_ref, ml_ref, u_ref, stat_ref, lim_ref, vec_ref, par_ref,
     keep_adj_ref, kp_adj_ref, kd_adj_ref, keep_ref, b_ref, z_ref, gb_ref, lg_ref, st_ref, a_ref) = refs
    vec_ref, par_ref = of_layer(vec_ref, layer), of_layer(par_ref, layer)
    scan = adjoint_scan(reverse, carry, sg_ref, s_ref, par_ref, keep_adj_ref, kp_adj_ref, kd_adj_ref, keep_ref, a_ref)
    gb_ref[...] = jnp.zeros(gb_ref.shape, F32)
    zero = jnp.zeros(lim_ref.shape, F32)
    sums = (zero, zero)
    for i in scan.ahead():
        drive = a_ref[rows_at(i), :].astype(BF16)
        add_drives(gb_ref, ml_ref[rows_at(i), :], drive)
        sums = back_to_norm(layer, i, drive, sums, b_ref, vec_ref, mix_ref, lim_ref, u_ref, stat_ref, z_ref)
    put_lam(lg_ref, scan.extra)
    put_norm_sums(st_ref, sums)


def k_adjoint_last(layer, reverse, parts, *refs):
    carry, refs = take_carry(refs, parts)
    (sg_ref, s_ref, ml_ref, par_ref, keep_adj_ref, kp_adj_ref, kd_adj_ref, keep_ref,
     drive_ref, gb_ref, lg_ref, a_ref) = refs
    par_ref = of_layer(par_ref, layer)
    scan = adjoint_scan(reverse, carry, sg_ref, s_ref, par_ref, keep_adj_ref, kp_adj_ref, kd_adj_ref, keep_ref, a_ref)
    gb_ref[...] = jnp.zeros(gb_ref.shape, F32)
    for i in scan.ahead():
        drive = a_ref[rows_at(i), :].astype(BF16)
        drive_ref[rows_at(i), :] = drive
        add_drives(gb_ref, ml_ref[rows_at(i), :], drive)
    put_lam(lg_ref, scan.extra)


def k_back(layer, drive_ref, mix_ref, u_ref, stat_ref, lim_ref, vec_ref, b_ref, *refs):
    z_ref, st_ref = refs[-2:]
    vec_ref = of_layer(vec_ref, layer)
    zero = jnp.zeros(lim_ref.shape, F32)
    sums = (zero, zero)
    for i in range(u_ref.shape[0] // TILE):
        sums = back_to_norm(layer, i, drive_ref[rows_at(i), :], sums, b_ref, vec_ref, mix_ref, lim_ref, u_ref, stat_ref, z_ref)
    put_norm_sums(st_ref, sums)
    at = 16
    for ref in refs[:-2]:
        st_ref[at : at + ref.shape[0], :] = ref[...]
        at += ref.shape[0]


def k_output(st_ref, z_ref, grad_ref, u_ref, stat_ref, vec_ref, lim_ref, par_ref, stat1_ref, bn1_ref,
             run_mean_ref, run_var_ref,
             out_ref, gain_ref, shift_ref, skip_ref, bias_ref, rate_ref, rotation_ref, mean_ref, var_ref,
             bn_ref, lines_ref):
    vec0_ref = of_layer(vec_ref, 0)
    c1, c2 = norm_sums(st_ref, stat_ref, vec0_ref, bn_ref)

    def step(i, unused):
        extra = norm_backward(z_ref, u_ref, stat_ref, vec0_ref, c1, c2, tile_mask(lim_ref, i), i)
        put_lines(lines_ref, i, grad_ref[rows_at(i), :] + flat(extra))
        return unused

    lax.fori_loop(0, u_ref.shape[0] // TILE, step, 0, unroll=True)
    spread_out(lines_ref, out_ref)
    width, states = gain_ref.shape[1], rate_ref.shape[1]
    per, per_state = width // LANE, states // LANE

    def line(at, count):
        return jnp.concatenate([st_ref[at + j : at + j + 1, :] for j in range(count)], axis=1)

    for layer, (stats_ref, norms_ref) in enumerate(((stat_ref, bn_ref), (stat1_ref, bn1_ref))):
        row = slice(layer, layer + 1)
        at = 40 - 24 * layer
        bias_ref[row, :] = line(at, per)
        skip_ref[row, :] = line(at + per, per)
        product = line(at + 2 * per, per_state)
        grad_re, grad_im = line(at + 16, per_state), line(at + 16 + per_state, per_state)
        par = of_layer(par_ref, layer)
        lam_re, lam_im, norm_in, decay = par[0:1, :], par[1:2, :], par[6:7, :], par[7:8, :]
        rotation_ref[row, :] = lam_re * grad_im - lam_im * grad_re
        rate_ref[row, :] = decay * (
            product * jnp.exp(-2.0 * decay) / (norm_in * norm_in) - (lam_re * grad_re + lam_im * grad_im)
        )
        shift_ref[row, :] = norms_ref[0:1, :]
        gain_ref[row, :] = norms_ref[1:2, :]
        mean, var = run_mean_ref[row, :], run_var_ref[row, :]
        for micro in range(2):
            mean = (1.0 - momentum) * mean + momentum * stats_ref[24 + micro : 25 + micro, :]
            var = (1.0 - momentum) * var + momentum * stats_ref[26 + micro : 27 + micro, :]
        mean_ref[row, :] = mean
        var_ref[row, :] = var


def k_split(side, x_ref, give_ref):
    half = give_ref.shape[0]
    give_ref[...] = x_ref[pl.ds(pl.multiple_of((1 - side()) * half, SUB), half), :]


def k_fold(before, side, kept_ref, got_ref, give_ref, keep_ref):
    half = give_ref.shape[0]
    base = 0 if before is None else before() * got_ref.shape[0]
    mine = side()
    for ref, at in ((give_ref, (1 - mine) * half), (keep_ref, mine * half)):
        here = kept_ref[pl.ds(pl.multiple_of(base + at, SUB), half), :]
        ref[...] = here + got_ref[pl.ds(pl.multiple_of(at, SUB), half), :]


def k_copy(src_ref, dst_ref):
    dst_ref[...] = src_ref[...]


def k_add(*refs):
    total = refs[1][...]
    for ref in refs[2:-1]:
        total = total + ref[...]
    refs[-1][...] = refs[0][...] + total


def k_join(side, own_ref, got_ref, out_ref):
    half = own_ref.shape[0]
    mine = side()
    out_ref[pl.ds(pl.multiple_of(mine * half, SUB), half), :] = own_ref[...]
    out_ref[pl.ds(pl.multiple_of((1 - mine) * half, SUB), half), :] = got_ref[...]


def copy_all(pairs, sem_ref):
    copies = [pltpu.make_async_copy(src, dst, sem_ref.at[k]) for k, (src, dst) in enumerate(pairs)]
    for copy in copies:
        copy.start()
    for copy in copies:
        copy.wait()


def cut_to(layer, first, src_ref, outs):
    pairs = []
    for begin, end, place in outs:
        low, high = max(begin, first), min(end, first + src_ref.shape[0])
        if low < high:
            pairs.extend(place(src_ref, low - first, low - begin, high - low))
    return pairs


def rows_to(layer, ref):
    return lambda src, at, row, size: [(src.at[pl.ds(at, size), :], ref.at[layer, pl.ds(row, size), :])]


def map_places(layer, *refs):
    places, first = [], 0
    for ref in refs:
        places.append((first, first + ref.shape[1], rows_to(layer, ref)))
        first += ref.shape[1]
    return places


def drive_places(layer, b_ref):
    width = b_ref.shape[1]

    def left(src, at, row, size):
        return [(src.at[pl.ds(at, size), :], b_ref.at[layer, pl.ds(row, size), pl.ds(0, width)])]

    def right(src, at, row, size):
        part = width // 2
        return [
            (src.at[pl.ds(at, size), pl.ds(k * part, part)],
             b_ref.at[layer, pl.ds(k * part + row, size), pl.ds(width, part)])
            for k in range(2)
        ]

    return [(0, width, left), (width, width + width // 2, right)]


def k_place(side, layer, groups, *refs):
    token_ref, sem_ref = refs[-2:]
    outs = refs[-2 - sum(count for unused, count in groups) : -2]
    token_ref[...] = jnp.zeros(token_ref.shape, F32)
    for mine in range(2):
        @pl.when(side() == mine)
        def _():
            pairs, first = [], 0
            for k, (places, count) in enumerate(groups):
                where = places(layer, *outs[first : first + count])
                first += count
                for ref, at in zip(refs[2 * k : 2 * k + 2], (mine, 1 - mine)):
                    pairs.extend(cut_to(layer, at * ref.shape[0], ref, where))
            copy_all(pairs, sem_ref)


def place(order, layer, items, into=()):
    args = [array for large, unused, unused in items for array in (large.block, large.got)]
    shapes = [shape for unused, unused, more in items for shape in more]
    alias = {len(args) + k: k for k in range(len(into))}
    return list(call(
        "place", functools.partial(k_place, items[0][0].side(), layer, [(places, len(more)) for unused, places, more in items]),
        shapes + [shaped((SUB, LANE))], args + list(into), scratch=[pltpu.SemaphoreType.DMA((16,))], order=order,
        token=len(shapes), far=range(len(args), len(args) + len(into)), alias=alias, out_far=len(shapes),
    ))[: len(shapes)]


BOTH = ("batch", "tm")

ORDER = (
    ("AA",),
    ("B", "A", "e", "BA"),
    ("CECE",),
    ("D", "ABSDECBSAD", "CSBEADCSBD", "EASCBDECDB", "LCEDABCAEC", "DBED"),
)


def outer_bits():
    nb, nt = lax.axis_size("batch"), lax.axis_size("tm")
    return [("batch", 1 << k, nt << k) for k in range(nb.bit_length() - 1)]


def line_bits():
    return [("tm", 1 << k, 1 << k) for k in range(1, lax.axis_size("tm").bit_length() - 1)]


def swap(block, distance):
    total = lax.axis_size("batch") * lax.axis_size("tm")
    return lax.ppermute(block, BOTH, [(i, i ^ distance) for i in range(total)])


def swap_by_core(block, even, odd):
    total = lax.axis_size("batch") * lax.axis_size("tm")
    return lax.ppermute(block, BOTH, [(i, i ^ (odd if i & 1 else even)) for i in range(total)])


def sum_four(block, others, order=None):
    block, = call("add", k_add, [shaped(block.shape)], [block, others[0]], order=order, work=1)
    return call("add", k_add, [shaped(block.shape)], [block] + others[1:], order=order, work=1)[0]


def sum_over(block, bits):
    if len(bits) == 2:
        near, far = bits[0][2], bits[1][2]
        return sum_four(block, [swap(block, distance | 1) for distance in (near | far, far, near)])
    for unused, unused, distance in bits:
        block = block + swap(block, distance | 1)
    return block


def sums_of_all(block, fill):
    order = Order()
    got = swap(block, 1)
    order.token = fill()
    block, = call("add", k_add, [shaped(block.shape)], [block, got], order=order)
    return sum_over(sum_over(block, outer_bits()), line_bits())


def sums_in_order(block, order, between):
    for bits, start in zip(([("tm", 1, 0)], outer_bits(), line_bits()), between):
        if len(bits) == 2:
            near, far = bits[0][2], bits[1][2]
            got = [swap(block, distance | 1) for distance in (near | far, far, near)]
            start()
            block = sum_four(block, got, order)
        else:
            for k, bit in enumerate(bits):
                got = swap(block, bit[2] | 1)
                if k == 0:
                    start()
                block, = call("add", k_add, [shaped(block.shape)], [block, got], order=order)
    return block


def carries(e, kd, par, layer, reverse, conj, order=None):
    other = swap(e, 1)
    block, = call("combine", functools.partial(k_combine, layer, reverse, conj), [shaped(e.shape)], [e, other, kd, par],
                  order=order)
    bits = line_bits()
    if len(bits) == 2:
        near, far = bits[0][2], bits[1][2]
        last = swap(block, near | far | 1)
        others = [swap(block, distance | 1) for distance in (near, far)]
        last, = call("copy", k_copy, [shaped(block.shape)], [last], work=1)
        return [block] + others + [last, e, other]
    for unused, unused, distance in bits:
        block = jnp.concatenate((block, swap(block, distance | 1)), axis=0)
    return [block, e, other]


def bit_of(axis, bit):
    return lax.div(lax.axis_index(axis), bit) % 2


def plan(rows, line_first):
    outer, line = outer_bits(), line_bits()
    is_odd = functools.partial(bit_of, "tm", 1)
    steps = []
    for even, odd in zip(outer, outer[::-1]):
        def side(even=even, odd=odd):
            return jnp.where(is_odd() == 1, bit_of(odd[0], odd[1]), bit_of(even[0], even[1]))

        steps.append((side, functools.partial(swap_by_core, even=even[2], odd=odd[2])))
    along = [(functools.partial(bit_of, axis, bit), functools.partial(swap, distance=distance))
             for axis, bit, distance in line]
    steps = [(is_odd, lambda block: swap(block, 1))] + (along + steps if line_first else steps + along)
    most = 3 if line_first else 4
    cuts = 0
    while cuts < len(steps) and rows % (SUB << (cuts + 1)) == 0 and cuts < most:
        cuts += 1
    return steps[:cuts], [exchange for unused, exchange in steps[cuts:]]


class Large:
    def __init__(self, order, block, line_first=False):
        self.order = order
        self.rows, self.width = block.shape
        self.cuts, self.whole = plan(self.rows, line_first)
        self.block = block
        self.at = 0
        self.got = None

    def call(self, name, body, outs):
        args = [self.block] if self.got is None else [self.block, self.got]
        return call(name, body, outs, args, order=self.order)

    def send(self):
        cuts, at = self.cuts, self.at
        count = len(cuts)
        if at < count:
            side, exchange = cuts[at]
            half = shaped((self.rows >> (at + 1), self.width))
            if at == 0:
                give, = self.call("split", functools.partial(k_split, side), [half])
            else:
                before = cuts[0][0] if at == 1 else None
                give, self.block = self.call("fold", functools.partial(k_fold, before, side), [half, half])
        else:
            if at <= count + len(self.whole):
                give, = self.call("add", k_add, [shaped(self.got.shape)])
            else:
                give, = self.call("join", functools.partial(k_join, self.side()), [self.doubled()])
            self.block = give
            exchange = (self.whole + [step[1] for step in cuts[::-1]])[at - count]
        self.got = exchange(give)
        self.at += 1

    def side(self):
        return self.cuts[2 * len(self.cuts) + len(self.whole) - self.at][0]

    def doubled(self):
        return shaped((2 * self.block.shape[0], self.width))

    def left(self):
        return 2 * len(self.cuts) + len(self.whole) - self.at


class Steps:
    def __init__(self, order):
        self.order = order
        self.larges, self.other, self.out, self.shapes, self.come = {}, {}, {}, {}, set()

    def add(self, name, block, line_first=False):
        self.larges[name] = Large(self.order, block, line_first)

    def run(self, items):
        for item in items:
            if item in self.other:
                self.other[item]()
            elif self.larges[item].left():
                self.larges[item].send()
            else:
                self.put(item)

    def put(self, item):
        group = [names for names in ("AB", "CE", "D") if item in names][0]
        self.come.add(item)
        if group in self.out or not self.come.issuperset(group):
            return
        for name in group:
            while self.larges[name].left():
                self.larges[name].send()
        if group == "AB":
            self.out[group] = place(self.order, 1, [
                (self.larges["A"], map_places, self.shapes["A"]), (self.larges["B"], drive_places, self.shapes["B"]),
            ])
            return
        if "AB" not in self.out:
            self.put("A")
            self.put("B")
        w_out, c_out, b_out = self.out["AB"]
        into = [b_out] if group == "D" else [c_out, w_out]
        self.out[group] = place(self.order, 0, [
            (self.larges[name], drive_places if name == "D" else map_places, [shaped(out.shape)])
            for name, out in zip(group, into)
        ], into)

    def placed(self, item):
        for name in "CED":
            self.put(name)
        return {"C": self.out["CE"][0], "E": self.out["CE"][1], "D": self.out["D"][0]}[item]


def small_sum(order, block):
    for distance in [1] + [bit[2] | 1 for bit in outer_bits() + line_bits()]:
        got = swap(block, distance)
        yield None
        block, = call("add", k_add, [shaped(block.shape)], [block, got], order=order)
    yield block


def local(tokens, starts, lengths, cotangent, norm_gain, norm_shift, b_proj, log_rate, rotation, c_proj, skip_gain,
          w_gate, gate_bias, run_mean, run_var):
    rows, length, width = tokens.shape
    states = log_rate.shape[1]
    count = rows * length
    n = lax.axis_size("tm")
    chips = n // 2
    parts = 4 if chips == 4 else 1

    big = lambda w, dtype=F32: shaped((count, w), dtype)
    ends = shaped((SUB, 2 * states))
    kept = shaped((count + SUB, 2 * states))
    small = shaped((16, LANE))
    lines = pltpu.VMEM((width // LANE, count, LANE), F32)
    rows_low, states_low_rows = pltpu.VMEM((count, width), BF16), pltpu.VMEM((count, 2 * states), BF16)
    everyone = pltpu.VMEM((chips, SUB, 2 * states), F32)
    keeps = shaped((count + SUB, LANE))
    vector, state_vector = shaped((2, width)), shaped((2, states))

    u0, st, lim = call("enter", k_input, [big(width), shaped((24, LANE)), shaped((SUB, width), jnp.int32)],
                       [lengths, tokens], scratch=[lines], scalars=1)
    keep_shapes = [keeps, shaped((2 * SUB, LANE)), shaped((n + 1, SUB, LANE))]
    made = []

    def prepare():
        made.extend(call(
            "prepare", k_prepare, keep_shapes + [shaped((2 * SUB, states)), shaped((2 * SUB, width))],
            [starts, log_rate, rotation, norm_gain, norm_shift, skip_gain, gate_bias], scalars=1,
        ))
        return made[1]

    st = sums_of_all(st, prepare)
    keep_f, kp_f, kd_f, par, vec = made
    d0, ml0, m0, stat0, e = call(
        "drive0", functools.partial(k_drive_first, 0, False),
        [big(2 * states), big(width, BF16), big(width), shaped((32, width)), ends],
        [st, u0, lim, vec, par, b_proj, keep_f, kp_f],
    )
    s0, al0, sig0, q0, slope0, u1, st = call(
        "finish0", functools.partial(k_finish_first, 0, parts),
        [kept, big(width, BF16), big(width), big(width), big(width), big(width), small],
        carries(e, kd_f, par, 0, False, False)
        + [d0, u0, m0, lim, vec, par, keep_f, kp_f, kd_f, c_proj, w_gate],
        scratch=[everyone],
    )
    after_first = Order()
    after_first.token = st
    backward = []

    def keep():
        backward.extend(call(
            "keep", functools.partial(k_keep, True), keep_shapes, [starts], scalars=1, order=after_first, token=1,
        ))
        return backward[1]

    st = sums_of_all(st, keep)
    keep_r, kp_r, kd_r = backward
    d1, ml1, m1, stat1, e = call(
        "drive1", functools.partial(k_drive, 1, True),
        [big(2 * states), big(width, BF16), big(width), shaped((32, width)), ends],
        [st, stat0, u1, lim, vec, par, b_proj, keep_r, kp_r],
    )
    grads = [shaped((width + 2 * states, width)), small, ends]
    after_second = Order()
    after_second.token = e
    cot32, = call("cotangent", spread_in, [big(width)], [cotangent], scratch=[lines], order=after_second)
    out32, s1, mix1, sg1, wc1, sums1, e = call(
        "middle", functools.partial(k_middle, 1, parts),
        [shaped((width // LANE, count, LANE)), kept, big(width, BF16), big(2 * states)] + grads,
        carries(e, kd_r, par, 1, True, False, after_second)
        + [d1, u1, m1, lim, vec, par, keep_r, kp_r, kd_r, keep_f, kp_f, c_proj, w_gate, cot32],
        scratch=[rows_low, rows_low, states_low_rows, everyone],
    )
    order = Order()
    order.token = e
    steps = Steps(order)
    steps.add("A", wc1)
    got = carries(e, kd_f, par, 1, False, True, order)
    steps.run(ORDER[0][0])
    adjoint = [big(width), shaped((2 * states, width)), shaped((8, LANE))]
    z1, gb1, lg1, st = call(
        "adjoint1", functools.partial(k_adjoint, 1, False, parts), adjoint + [small],
        got + [sg1, s1, mix1, ml1, u1, stat1, lim, vec, par, keep_f, kp_f, kd_f, keep_r, b_proj],
        scratch=[pltpu.VMEM((count, 2 * states), F32), everyone], order=order, token=3,
    )
    steps.add("B", gb1)
    emitted = []

    def emit():
        emitted.extend(
            call("emit", k_emit, [shaped(tokens.shape, BF16), shaped((SUB, LANE))], [out32], results=1, order=order, token=1)
        )

    steps.other["e"] = emit
    st = sums_in_order(st, order, [functools.partial(steps.run, items) for items in ORDER[1][:3]])
    steps.run(ORDER[1][3])
    g0, mix0, sg0, gw0, gc0, sums0, e, bn1 = call(
        "lower", functools.partial(k_lower, 0),
        [big(width), big(width, BF16), big(2 * states), shaped((width, width)), shaped((2 * states, width)), small, ends,
         shaped((SUB, width))],
        [st, z1, cot32, u1, stat1, lim, s0, al0, sig0, q0, slope0, m0, vec, par,
         c_proj, w_gate, keep_r, kp_r],
        scratch=[rows_low, states_low_rows], order=order, token=6,
    )
    steps.add("E", gw0, True)
    steps.add("C", gc0)
    got = carries(e, kd_r, par, 0, True, True, order)
    steps.run(ORDER[2][0])
    drive0, gb0, lg0 = call(
        "adjoint0", functools.partial(k_adjoint_last, 0, True, parts), [big(2 * states, BF16)] + adjoint[1:],
        got + [sg0, s0, ml0, par, keep_r, kp_r, kd_r, keep_f],
        scratch=[pltpu.VMEM((count, 2 * states), F32), everyone], order=order, token=2,
    )
    steps.add("D", gb0)
    steps.shapes = {
        "A": [shaped((2, width, width)), shaped((2, 2 * states, width))],
        "B": [shaped((2, width, 2 * states))],
    }
    steps.run(ORDER[3][0])
    z0, st = call(
        "back", functools.partial(k_back, 0), [big(width), shaped((64, LANE))],
        [drive0, mix0, u0, stat0, lim, vec, b_proj, sums1, lg1, sums0, lg0], order=order, token=1,
    )
    small_steps = small_sum(order, st)
    last = []

    def small():
        last.extend(item for item in [next(small_steps, None)] if item is not None)

    def leave():
        while not last:
            small()
        last.extend(call(
            "leave", k_output,
            [shaped(tokens.shape), vector, vector, vector, vector, state_vector, state_vector, vector, vector,
             shaped((SUB, width))],
            [last[0], z0, g0, u0, stat0, vec, lim, par, stat1, bn1, run_mean, run_var],
            scratch=[lines], results=9, order=order, token=9,
        ))

    steps.other.update({"S": small, "L": leave})
    steps.run("".join(ORDER[3][1:]))
    (tokens_grad, grad_gain, grad_shift, grad_skip, grad_bias, grad_rate, grad_rotation, new_mean, new_var) = last[1:10]
    output, grad_w, grad_c, grad_b = emitted[0], steps.placed("E"), steps.placed("C"), steps.placed("D")
    return (output, tokens_grad, grad_gain, grad_shift, grad_b, grad_rate, grad_rotation, grad_c, grad_skip, grad_w,
            grad_bias, new_mean, new_var)


def solution(mesh):
    tokens_spec = P("batch", "tm", None)
    return jax.shard_map(
        local,
        mesh=mesh,
        in_specs=(tokens_spec, P("batch", None), P("batch"), tokens_spec) + (P(),) * 11,
        out_specs=(tokens_spec, tokens_spec) + (P(),) * 11,
        check_vma=False,
    )
```

```python
import functools
import math

import jax
import jax.numpy as jnp
from jax import lax
from jax.experimental import pallas as pl
from jax.experimental.pallas import tpu as pltpu
from jax.sharding import PartitionSpec as P

epsilon = 1e-05
momentum = 0.1
F32 = jnp.float32
BF16 = jnp.bfloat16

SUB = 8
LANE = 128
TILE = 256
WORK = 5 * 10**9


def in_vmem(count):
    return [pl.BlockSpec(memory_space=pltpu.VMEM)] * count


class Order:
    def __init__(self):
        self.token = None


def call(name, body, outs, args, scratch=(), scalars=0, results=0, order=None, token=0, far=(), alias=None, out_far=0, work=WORK):
    room = 6 * 1024 * 1024 + sum(4 * math.prod(item.shape) for item in list(scratch) + list(outs[:results]) if hasattr(item, "shape"))
    specs = [pl.BlockSpec(memory_space=pltpu.SMEM)] * scalars + in_vmem(len(args) - scalars)
    for k in far:
        specs[k] = pl.BlockSpec(memory_space=pltpu.HBM)
    count = len(args)
    args = list(args)
    run = body
    if order is not None and order.token is not None:
        args.append(order.token)
        specs.append(pl.BlockSpec(memory_space=pl.ANY))
        run = lambda *refs: body(*refs[:count], *refs[count + 1 :])
    out_specs = in_vmem(len(outs))
    for k in range(out_far):
        out_specs[k] = pl.BlockSpec(memory_space=pltpu.HBM)
    done = pl.pallas_call(
        run,
        name=name,
        out_shape=outs,
        in_specs=specs,
        out_specs=out_specs,
        scratch_shapes=list(scratch),
        input_output_aliases=alias or {},
        compiler_params=pltpu.CompilerParams(vmem_limit_bytes=room),
        cost_estimate=pl.CostEstimate(flops=work, bytes_accessed=1, transcendentals=0),
    )(*args)
    if order is not None:
        order.token = done[token]
    return done


def shaped(shape, dtype=F32):
    return jax.ShapeDtypeStruct(shape, dtype)


def tile_mask(lim_ref, i):
    steps = TILE // SUB
    t = lax.broadcasted_iota(jnp.int32, (steps,) + lim_ref.shape, 0) + i * steps
    return t < lim_ref[...][None]


def folded(values):
    return values.reshape((values.shape[0] // SUB, SUB, values.shape[1]))


def flat(values):
    return values.reshape((values.shape[0] * SUB, values.shape[2]))


def times(ar, ai, br, bi):
    return (ar * br - ai * bi, ar * bi + ai * br)


class Scan:
    def __init__(self, d_ref, keep_ref, par_ref, start, reverse, conj, visit=None, extra=()):
        self.d_ref, self.keep_ref, self.reverse = d_ref, keep_ref, reverse
        self.width = par_ref.shape[1]
        self.visit, self.extra = visit, extra
        self.lanes = [slice(j * LANE, (j + 1) * LANE) for j in range(self.width // LANE)]
        self.lam = []
        for lanes in self.lanes:
            re = jnp.broadcast_to(par_ref[0:1, lanes], (SUB, LANE))
            im = jnp.broadcast_to(par_ref[1:2, lanes], (SUB, LANE))
            self.lam.append((re, -im if conj else im))
        self.state = [(start[0][:, lanes], start[1][:, lanes]) for lanes in self.lanes]

    def tiles(self):
        count = self.d_ref.shape[0] // TILE
        return range(count - 1, -1, -1) if self.reverse else range(count)

    def ahead(self):
        order = list(self.tiles())
        self.run(order[0])
        for k, i in enumerate(order):
            if k + 1 < len(order):
                self.run(order[k + 1])
            yield i

    def run(self, i):
        steps = TILE // SUB
        for k in range(steps):
            t = i * steps + (steps - 1 - k if self.reverse else k)
            at = pl.ds(t * SUB, SUB)
            keep = self.keep_ref[at, :]
            fresh = []
            for (re, im), (lam_re, lam_im), lanes in zip(self.state, self.lam, self.lanes):
                a, b = keep * lam_re, keep * lam_im
                dr = self.d_ref[at, lanes]
                di = self.d_ref[at, lanes.start + self.width : lanes.stop + self.width]
                fresh.append((a * re - b * im + dr, a * im + b * re + di))
            self.state = fresh
            if self.visit is not None:
                self.extra = self.visit(t, fresh, self.extra)

    def ends(self):
        return tuple(jnp.concatenate([part[k] for part in self.state], axis=1) for k in range(2))


def wide(values, width):
    return jnp.concatenate([values] * (width // LANE), axis=1)


def chunk_end(ends, kp_ref, par_ref, reverse, conj):
    width = par_ref.shape[1]
    re, im = ends
    shift = SUB - 1 if reverse else 1
    pr, pi = pltpu.roll(re, shift, 0), pltpu.roll(im, shift, 0)
    keep = wide(kp_ref[:SUB, :], width)
    lr = keep * par_ref[2:3, :]
    li = keep * par_ref[3:4, :]
    li = -li if conj else li
    qr, qi = times(lr, li, pr, pi)
    odd = lax.broadcasted_iota(jnp.int32, (SUB, width), 0) % 2
    last = odd == (0 if reverse else 1)
    return jnp.where(last, qr + re, re), jnp.where(last, qi + im, im)


def chip_and_core():
    me = lax.axis_index("tm")
    return me // 2, me % 2


def enter(got_refs, e_ref, other_ref, all_ref, kd_ref, kp_ref, par_ref, reverse, conj):
    width = par_ref.shape[1]
    chips = all_ref.shape[0]
    chip, core = chip_and_core()
    sign = -1.0 if conj else 1.0
    at = 0
    for ref in got_refs:
        for k in range(ref.shape[0] // SUB):
            all_ref[at] = ref[k * SUB : (k + 1) * SUB, :]
            at += 1
    lr, li = par_ref[4:5, :], sign * par_ref[5:6, :]
    cr, ci = times(lr, li, lr, li)
    lr, li, cr, ci = (jnp.broadcast_to(x, (SUB, width)) for x in (lr, li, cr, ci))

    def step(i, x):
        j = chips - 1 - i if reverse else i
        keep = wide(kd_ref[2 * j] * kd_ref[2 * j + 1], width)
        qr, qi = times(keep * cr, keep * ci, x[0], x[1])
        use = (j > chip) if reverse else (j < chip)
        use = jnp.where(use, 1.0, 0.0)
        k = jnp.bitwise_xor(j, chip)
        nr = qr + all_ref[k, :, :width]
        ni = qi + all_ref[k, :, width:]
        return (x[0] + use * (nr - x[0]), x[1] + use * (ni - x[1]))

    zero = jnp.zeros((SUB, width), F32)
    xr, xi = lax.fori_loop(0, chips, step, (zero, zero), unroll=chips <= 4)
    first = 1 if reverse else 0
    keep = wide(kd_ref[2 * chip + first], width)
    qr, qi = times(keep * lr, keep * li, xr, xi)
    use = jnp.where(core == first, 0.0, 1.0)
    xr = xr + use * (qr + other_ref[:, :width] - xr)
    xi = xi + use * (qi + other_ref[:, width:] - xi)
    near, far = (1, SUB - 1) if reverse else (SUB - 1, 1)
    sr, si = pltpu.roll(xr, near, 0), pltpu.roll(xi, near, 0)
    keep = wide(kp_ref[:SUB, :], width)
    hr = keep * par_ref[2:3, :]
    hi = sign * keep * par_ref[3:4, :]
    tr, ti = times(hr, hi, sr, si)
    tr = pltpu.roll(tr + e_ref[:, :width], far, 0)
    ti = pltpu.roll(ti + e_ref[:, width:], far, 0)
    odd = lax.broadcasted_iota(jnp.int32, (SUB, width), 0) % 2
    second = odd == (0 if reverse else 1)
    return jnp.where(second, tr, sr), jnp.where(second, ti, si)


def put_ends(e_ref, ends):
    e_ref[...] = jnp.concatenate(ends, axis=1)


def zeros_state(par_ref):
    zero = jnp.zeros((SUB, par_ref.shape[1]), F32)
    return (zero, zero)


def per_micro(values):
    return (
        jnp.sum(values[0:4], axis=0, keepdims=True),
        jnp.sum(values[4:8], axis=0, keepdims=True),
    )


def pack_rows(out_ref, rows):
    at = 0
    for row in rows:
        for j in range(row.shape[1] // LANE):
            out_ref[at : at + 1, :] = row[:, j * LANE : (j + 1) * LANE]
            at += 1


def unpack_rows(values, count, width):
    tiles = width // LANE
    return [
        jnp.concatenate(
            [values[r * tiles + j : r * tiles + j + 1, :] for j in range(tiles)], axis=1
        )
        for r in range(count)
    ]


def by_micro(first, second):
    sub = lax.broadcasted_iota(jnp.int32, (SUB, first.shape[1]), 0)
    return jnp.where(sub < 4, jnp.broadcast_to(first, sub.shape), jnp.broadcast_to(second, sub.shape))


def dot(a, b):
    return jnp.dot(a, b, preferred_element_type=F32)


def dot_nt(a, b):
    return lax.dot_general(a, b, (((1,), (1,)), ((), ())), preferred_element_type=F32)


def dot_tn(a, b):
    return lax.dot_general(a, b, (((0,), (0,)), ((), ())), preferred_element_type=F32)


def normed_tile(u_ref, stat_ref, i):
    x = folded(u_ref[pl.ds(pl.multiple_of(i * TILE, TILE), TILE), :])
    return (x - stat_ref[0:8, :][None]) * stat_ref[8:16, :][None]


def masked_tile(u_ref, stat_ref, vec_ref, lim_ref, i):
    normed = normed_tile(u_ref, stat_ref, i)
    z = normed * vec_ref[0:1, :][None] + vec_ref[1:2, :][None]
    return jnp.where(tile_mask(lim_ref, i), z, 0.0)


def rows_at(i):
    return pl.ds(pl.multiple_of(i * TILE, TILE), TILE)


def spread_in(src_ref, dst_ref, lines_ref):
    half = src_ref.shape[1] // 2
    tiles = src_ref.shape[2] // LANE
    for s in range(SUB):
        part = src_ref[s // 2, (s % 2) * half : (s % 2 + 1) * half, :].astype(F32)
        for j in range(tiles):
            lines_ref[j, pl.ds(s, half, stride=SUB), :] = part[:, j * LANE : (j + 1) * LANE]
    for j in range(tiles):
        dst_ref[:, j * LANE : (j + 1) * LANE] = lines_ref[j]


def spread_out(lines_ref, dst_ref):
    half = dst_ref.shape[1] // 2
    tiles = dst_ref.shape[2] // LANE
    for s in range(SUB):
        for j in range(tiles):
            part = lines_ref[j, pl.ds(s, half, stride=SUB), :]
            dst_ref[s // 2, (s % 2) * half : (s % 2 + 1) * half, j * LANE : (j + 1) * LANE] = part.astype(dst_ref.dtype)


def k_emit(lines_ref, out_ref, token_ref):
    token_ref[...] = jnp.zeros(token_ref.shape, F32)
    spread_out(lines_ref, out_ref)


def put_lines(lines_ref, i, values):
    for j in range(lines_ref.shape[0]):
        lines_ref[j, rows_at(i), :] = values[:, j * LANE : (j + 1) * LANE]


def moment_sums(u_ref, lim_ref, upto):
    def step(i, sums):
        x = jnp.where(tile_mask(lim_ref, i), folded(u_ref[rows_at(i), :]), 0.0)
        return (sums[0] + jnp.sum(x, axis=0), sums[1] + jnp.sum(x * x, axis=0))

    zero = jnp.zeros(lim_ref.shape, F32)
    return lax.fori_loop(0, upto, step, (zero, zero))


def fill_lim(lengths_ref, lim_ref, half):
    sub = lax.broadcasted_iota(jnp.int32, lim_ref.shape, 0)
    length = jnp.zeros(lim_ref.shape, jnp.int32)
    for r in range(lengths_ref.shape[0]):
        length = jnp.where(sub // 2 == r, lengths_ref[r], length)
    lim_ref[...] = length - lax.axis_index("tm") * (2 * half) - (sub % 2) * half


def k_input(lengths_ref, tokens_ref, u_ref, st_ref, lim_ref, lines_ref):
    half = tokens_ref.shape[1] // 2
    fill_lim(lengths_ref, lim_ref, half)
    spread_in(tokens_ref, u_ref, lines_ref)
    sums, squares = moment_sums(u_ref, lim_ref, u_ref.shape[0] // TILE)
    a, b = per_micro(sums)
    c, d = per_micro(squares)
    st_ref[...] = jnp.zeros(st_ref.shape, F32)
    pack_rows(st_ref, (a, c, b, d))
    counts = jnp.clip(lim_ref[:, :LANE], 0, half).astype(F32)
    a, b = per_micro(counts)
    st_ref[16:17, :] = a
    st_ref[17:18, :] = b


def one_minus_exp(x):
    series = jnp.full(x.shape, 1.0 / 9.0, F32)
    for k in range(8, 0, -1):
        series = (1.0 - x * series) / k if k > 1 else 1.0 - x * series
    return jnp.where(x < 0.5, x * series, 1.0 - jnp.exp(-x))


def k_keep(reverse, starts_ref, keep_ref, kp_ref, kd_ref):
    count = keep_ref.shape[0] - SUB
    steps = count // SUB
    length = 2 * steps
    n = kd_ref.shape[0] - 1
    base = lax.axis_index("tm") * length
    for ref in (keep_ref, kp_ref, kd_ref):
        ref[...] = jnp.ones(ref.shape, F32)
    none = jnp.zeros((1, LANE), F32)

    def mark(r, place):
        local = place - base
        here = (local >= 0) & (local < length)
        second = jnp.where(local >= steps, 1, 0)
        row = (local - second * steps) * SUB + 2 * r + second
        keep_ref[pl.ds(jnp.where(here, row, count), 1), :] = none
        kp_ref[pl.ds(jnp.where(here, 2 * r + second, SUB), 1), :] = none

    def each(k, unused):
        for r in range(starts_ref.shape[0]):
            place = starts_ref[r, k] - (1 if reverse else 0)
            mark(r, place)
            device = jnp.where(place >= 0, lax.div(place, length), n)
            kd_ref[device, 2 * r : 2 * r + 2, :] = jnp.zeros((2, LANE), F32)
        return unused

    lax.fori_loop(0, starts_ref.shape[1], each, 0)
    if reverse:
        for r in range(starts_ref.shape[0]):
            mark(r, n * length - 1)


def k_prepare(starts_ref, rate_ref, rotation_ref, gain_ref, shift_ref, skip_ref, bias_ref,
              keep_ref, kp_ref, kd_ref, par_ref, vec_ref):
    k_keep(False, starts_ref, keep_ref, kp_ref, kd_ref)
    doublings = ((keep_ref.shape[0] - SUB) // SUB).bit_length() - 1
    for layer in range(2):
        decay = jnp.exp(rate_ref[layer : layer + 1, :])
        magnitude = jnp.exp(-decay)
        angle = rotation_ref[layer : layer + 1, :]
        re, im = magnitude * jnp.cos(angle), magnitude * jnp.sin(angle)
        at = layer * SUB
        norm_in = jnp.sqrt(one_minus_exp(2.0 * decay))
        par_ref[at : at + 1, :] = re
        par_ref[at + 1 : at + 2, :] = im
        for unused in range(doublings):
            re, im = times(re, im, re, im)
        par_ref[at + 2 : at + 3, :] = re
        par_ref[at + 3 : at + 4, :] = im
        re, im = times(re, im, re, im)
        par_ref[at + 4 : at + 5, :] = re
        par_ref[at + 5 : at + 6, :] = im
        par_ref[at + 6 : at + 7, :] = norm_in
        par_ref[at + 7 : at + 8, :] = decay
        vec_ref[at : at + SUB, :] = jnp.zeros((SUB, vec_ref.shape[1]), F32)
        for k, ref in enumerate((gain_ref, shift_ref, skip_ref, bias_ref)):
            vec_ref[at + k : at + k + 1, :] = ref[layer : layer + 1, :]


def of_layer(ref, layer):
    return ref.at[layer * SUB : (layer + 1) * SUB]


def k_combine(layer, reverse, conj, e_ref, other_ref, kd_ref, par_ref, out_ref):
    par_ref = of_layer(par_ref, layer)
    width = par_ref.shape[1]
    chip, core = chip_and_core()
    keep = wide(kd_ref[2 * chip + (0 if reverse else 1)], width)
    lr = keep * par_ref[4:5, :]
    li = keep * par_ref[5:6, :] * (-1.0 if conj else 1.0)
    is_first = core == (1 if reverse else 0)
    e, other = e_ref[...], other_ref[...]
    pick = jnp.where(is_first, 1.0, 0.0)
    first = other + pick * (e - other)
    last = e + pick * (other - e)
    qr, qi = times(lr, li, first[:, :width], first[:, width:])
    out_ref[...] = jnp.concatenate((qr, qi), axis=1) + last


def k_drive(layer, reverse, st_ref, cnt_ref, u_ref, lim_ref, vec_ref, par_ref, b_ref, keep_ref, kp_ref,
            d_ref, ml_ref, m_ref, stat_ref, e_ref):
    vec_ref, par_ref = of_layer(vec_ref, layer), of_layer(par_ref, layer)
    total = st_ref[...]
    a, c, b, d = unpack_rows(total, 4, u_ref.shape[1])
    if cnt_ref is None:
        counts = (total[16:17, :], total[17:18, :])
    else:
        counts = (cnt_ref[28:29, :LANE], cnt_ref[29:30, :LANE])
    parts = []
    for summed, squares, count in ((a, c, counts[0]), (b, d, counts[1])):
        inverse = 1.0 / wide(count, u_ref.shape[1])
        center = summed * inverse
        spread = squares * inverse - center * center
        parts.append((center, spread, lax.rsqrt(spread + epsilon), inverse))
    stat_ref[0:8, :] = by_micro(parts[0][0], parts[1][0])
    stat_ref[8:16, :] = by_micro(parts[0][2], parts[1][2])
    stat_ref[16:24, :] = by_micro(parts[0][3], parts[1][3])
    stat_ref[24:25, :] = parts[0][0]
    stat_ref[25:26, :] = parts[1][0]
    stat_ref[26:27, :] = parts[0][1]
    stat_ref[27:28, :] = parts[1][1]
    stat_ref[28:29, :] = wide(counts[0], u_ref.shape[1])
    stat_ref[29:30, :] = wide(counts[1], u_ref.shape[1])
    stat_ref[30:32, :] = jnp.zeros((2, u_ref.shape[1]), F32)
    both = jnp.concatenate((par_ref[6:7, :], par_ref[6:7, :]), axis=1)

    def step(i, unused):
        masked = flat(masked_tile(u_ref, stat_ref, vec_ref, lim_ref, i))
        m_ref[rows_at(i), :] = masked
        low = masked.astype(BF16)
        ml_ref[rows_at(i), :] = low
        d_ref[rows_at(i), :] = dot(low, b_ref[layer]) * both
        return unused

    scan = Scan(d_ref, keep_ref, par_ref, zeros_state(par_ref), reverse, False)
    for i in scan.tiles():
        step(i, 0)
        scan.run(i)
    put_ends(e_ref, chunk_end(scan.ends(), kp_ref, par_ref, reverse, False))


def k_drive_first(layer, reverse, st_ref, *refs):
    k_drive(layer, reverse, st_ref, None, *refs)


def run_states(carry, d_ref, keep_ref, kp_ref, kd_ref, par_ref, s_ref, reverse):
    width = par_ref.shape[1]
    first = 0 if reverse else SUB
    start = enter(*carry, kd_ref, kp_ref, par_ref, reverse, False)
    s_ref[(s_ref.shape[0] - SUB if reverse else 0) : (s_ref.shape[0] if reverse else SUB), :] = (
        jnp.concatenate(start, axis=1)
    )

    def visit(t, states, extra):
        at = pl.ds(t * SUB + first, SUB)
        for j, (re, im) in enumerate(states):
            s_ref[at, j * LANE : (j + 1) * LANE] = re
            s_ref[at, width + j * LANE : width + (j + 1) * LANE] = im
        return extra

    return first, Scan(d_ref, keep_ref, par_ref, start, reverse, False, visit)


def sigmoid(x):
    return 0.5 + 0.5 * jnp.tanh(0.5 * x)


def gelu_parts(x):
    cdf = 0.5 * (1.0 + lax.erf(x * 0.7071067811865476))
    return x * cdf, cdf + x * jnp.exp(-0.5 * x * x) * 0.3989422804014327


def states_low(s_ref, first, i):
    return s_ref[pl.ds(pl.multiple_of(i * TILE + first, SUB), TILE), :].astype(BF16)


def take_carry(refs, parts):
    return (refs[:parts], refs[parts], refs[parts + 1], refs[-1]), refs[parts + 2 : -1]


def k_finish_first(layer, parts, *refs):
    carry, refs = take_carry(refs, parts)
    (d_ref, u_ref, m_ref, lim_ref, vec_ref, par_ref, keep_ref, kp_ref, kd_ref, c_ref, w_ref,
     s_ref, al_ref, sig_ref, q_ref, slope_ref, next_ref, st_ref) = refs
    vec_ref, par_ref = of_layer(vec_ref, layer), of_layer(par_ref, layer)
    first, scan = run_states(carry, d_ref, keep_ref, kp_ref, kd_ref, par_ref, s_ref, False)

    def step(i, sums):
        at = rows_at(i)
        valid = tile_mask(lim_ref, i)
        mixed = dot(states_low(s_ref, first, i), c_ref[layer]) + vec_ref[2:3, :] * m_ref[at, :]
        active, slope = gelu_parts(mixed)
        low = active.astype(BF16)
        sig = sigmoid(dot(low, w_ref[layer]) + vec_ref[3:4, :])
        gated = active * sig
        al_ref[at, :] = low
        sig_ref[at, :] = sig
        slope_ref[at, :] = slope
        q_ref[at, :] = gated * (1.0 - sig)
        fresh = folded(u_ref[at, :]) + jnp.where(valid, folded(gated), 0.0)
        next_ref[at, :] = flat(fresh)
        x = jnp.where(valid, fresh, 0.0)
        return (sums[0] + jnp.sum(x, axis=0), sums[1] + jnp.sum(x * x, axis=0))

    zero = jnp.zeros(lim_ref.shape, F32)
    totals = (zero, zero)
    for i in scan.ahead():
        totals = step(i, totals)
    sums, squares = totals
    a, b = per_micro(sums)
    c, d = per_micro(squares)
    pack_rows(st_ref, (a, c, b, d))


def gate_backward(layer, upstream, q, sig, slope, masked, state, c_ref, w_ref, gate_ref, mix_ref, sg_ref, i):
    at = rows_at(i)
    gate = (upstream * q).astype(BF16)
    gate_ref[at, :] = gate
    act = upstream * sig + dot_nt(gate, w_ref[layer])
    mix = (act * slope).astype(BF16)
    mix_ref[at, :] = mix
    sg = dot_nt(mix, c_ref[layer])
    sg_ref[at, :] = sg
    wide_sum = jnp.sum(folded(sg * state), axis=0)
    half = wide_sum.shape[1] // 2
    return (
        jnp.sum(folded(gate.astype(F32)), axis=0),
        jnp.sum(folded(mix.astype(F32) * masked), axis=0),
        wide_sum[:, :half] + wide_sum[:, half:],
    )


def put_sums(sums_ref, sums):
    sums_ref[...] = jnp.zeros(sums_ref.shape, F32)
    pack_rows(sums_ref, [jnp.sum(part, axis=0, keepdims=True) for part in sums])


def zero_sums(width, states):
    return (jnp.zeros((SUB, width), F32), jnp.zeros((SUB, width), F32), jnp.zeros((SUB, states), F32))


class Ends:
    def __init__(self, keep_ref, par_ref):
        self.keep_ref = keep_ref
        re, im = par_ref[0:1, :], -par_ref[1:2, :]
        for unused in range((TILE // SUB).bit_length() - 1):
            re, im = times(re, im, re, im)
        self.step = tuple(jnp.broadcast_to(part, (SUB, part.shape[1])) for part in (re, im))
        self.factor = self.total = None

    def put_before(self, i, ends):
        if self.total is None:
            self.total = ends
        else:
            re, im = times(*self.factor, *ends)
            self.total = (self.total[0] + re, self.total[1] + im)
        keep = wide(jnp.min(folded(self.keep_ref[i * TILE : (i + 1) * TILE, :]), axis=0), ends[0].shape[1])
        here = tuple(keep * part for part in self.step)
        self.factor = here if self.factor is None else times(*self.factor, *here)


def k_middle(layer, parts, *refs):
    carry, refs = take_carry(refs, parts)
    (d_ref, u_ref, m_ref, lim_ref, vec_ref, par_ref, keep_ref, kp_ref, kd_ref,
     keep_adj_ref, kp_adj_ref, c_ref, w_ref, cot32_ref,
     lines_ref, s_ref, mix_ref, sg_ref, wc_ref, sums_ref, e_ref, al_ref, gate_ref, slow_ref) = refs
    vec_ref, par_ref = of_layer(vec_ref, layer), of_layer(par_ref, layer)
    first, scan = run_states(carry, d_ref, keep_ref, kp_ref, kd_ref, par_ref, s_ref, True)

    def step(i, sums):
        at = rows_at(i)
        valid = tile_mask(lim_ref, i)
        masked = m_ref[at, :]
        state = s_ref[pl.ds(pl.multiple_of(i * TILE + first, SUB), TILE), :]
        s_low = state.astype(BF16)
        mixed = dot(s_low, c_ref[layer]) + vec_ref[2:3, :] * masked
        active, slope = gelu_parts(mixed)
        low = active.astype(BF16)
        sig = sigmoid(dot(low, w_ref[layer]) + vec_ref[3:4, :])
        gated = active * sig
        put_lines(lines_ref, i, flat(folded(u_ref[at, :]) + jnp.where(valid, folded(gated), 0.0)))
        upstream = flat(jnp.where(valid, folded(cot32_ref[at, :]), 0.0))
        al_ref[at, :] = low
        slow_ref[at, :] = s_low
        more = gate_backward(layer, upstream, gated * (1.0 - sig), sig, slope, masked, state,
                             c_ref, w_ref, gate_ref, mix_ref, sg_ref, i)
        return tuple(x + y for x, y in zip(sums, more))

    sums = zero_sums(u_ref.shape[1], par_ref.shape[1])
    ends = Ends(keep_adj_ref, par_ref)
    for i in scan.ahead():
        sums = step(i, sums)
        local = Scan(sg_ref, keep_adj_ref, par_ref, zeros_state(par_ref), False, True)
        local.run(i)
        ends.put_before(i, local.ends())
    wc_ref[: u_ref.shape[1], :] = dot_tn(al_ref[...], gate_ref[...])
    wc_ref[u_ref.shape[1] :, :] = dot_tn(slow_ref[...], mix_ref[...])
    put_sums(sums_ref, sums)
    put_ends(e_ref, chunk_end(ends.total, kp_adj_ref, par_ref, False, True))


def k_lower(layer, st_ref, z_ref, cot32_ref, u1_ref, stat1_ref, lim_ref,
            s_ref, al_ref, sig_ref, q_ref, slope_ref, m_ref, vec_ref, par_ref, c_ref, w_ref,
            keep_adj_ref, kp_adj_ref,
            grad_ref, mix_ref, sg_ref, gw_ref, gc_ref, sums_ref, e_ref, bn_ref, gate_ref, slow_ref):
    vec1_ref = of_layer(vec_ref, layer + 1)
    vec_ref, par_ref = of_layer(vec_ref, layer), of_layer(par_ref, layer)
    first = SUB
    c1, c2 = norm_sums(st_ref, stat1_ref, vec1_ref, bn_ref)

    def step(i, sums):
        at = rows_at(i)
        valid = tile_mask(lim_ref, i)
        extra = norm_backward(z_ref, u1_ref, stat1_ref, vec1_ref, c1, c2, valid, i)
        grad = folded(cot32_ref[at, :]) + extra
        grad_ref[at, :] = flat(grad)
        upstream = flat(jnp.where(valid, grad, 0.0))
        masked = m_ref[at, :]
        state = s_ref[pl.ds(pl.multiple_of(i * TILE + first, SUB), TILE), :]
        slow_ref[at, :] = state.astype(BF16)
        more = gate_backward(layer, upstream, q_ref[at, :], sig_ref[at, :], slope_ref[at, :], masked,
                             state, c_ref, w_ref, gate_ref, mix_ref, sg_ref, i)
        return tuple(x + y for x, y in zip(sums, more))

    sums = zero_sums(m_ref.shape[1], par_ref.shape[1])
    scan = Scan(sg_ref, keep_adj_ref, par_ref, zeros_state(par_ref), True, True)
    for i in scan.tiles():
        sums = step(i, sums)
        scan.run(i)
    gw_ref[...] = dot_tn(al_ref[...], gate_ref[...])
    gc_ref[...] = dot_tn(slow_ref[...], mix_ref[...])
    put_sums(sums_ref, sums)
    put_ends(e_ref, chunk_end(scan.ends(), kp_adj_ref, par_ref, True, True))


def norm_sums(st_ref, stat_ref, vec_ref, bn_ref):
    width = vec_ref.shape[1]
    a, c, b, d = unpack_rows(st_ref[...], 4, width)
    bn_ref[...] = jnp.concatenate((a + b, c + d, jnp.zeros((6, width), F32)), axis=0)
    gain = vec_ref[0:1, :]
    inverse = stat_ref[16:24, :]
    return by_micro(a * gain, b * gain) * inverse, by_micro(c * gain, d * gain) * inverse


def norm_backward(z_ref, u_ref, stat_ref, vec_ref, c1, c2, valid, i):
    normed = normed_tile(u_ref, stat_ref, i)
    z = folded(z_ref[rows_at(i), :]) * vec_ref[0:1, :][None]
    return jnp.where(valid, stat_ref[8:16, :][None] * (z - c1[None] - normed * c2[None]), 0.0)


def adjoint_scan(reverse, carry, sg_ref, s_ref, par_ref, keep_adj_ref, kp_adj_ref, kd_adj_ref, keep_ref, a_ref):
    width = par_ref.shape[1]
    tiles = width // LANE
    behind = 0 if reverse else SUB
    start = enter(*carry, kd_adj_ref, kp_adj_ref, par_ref, reverse, True)
    scale = [jnp.broadcast_to(par_ref[6:7, j * LANE : (j + 1) * LANE], (SUB, LANE)) for j in range(tiles)]

    def visit(t, adjoint, sums):
        at = pl.ds(t * SUB, SUB)
        before = pl.ds(t * SUB + behind, SUB)
        keep = keep_ref[at, :]
        fresh = []
        for j, (re, im) in enumerate(adjoint):
            a_ref[at, j * LANE : (j + 1) * LANE] = re * scale[j]
            a_ref[at, width + j * LANE : width + (j + 1) * LANE] = im * scale[j]
            pr = s_ref[before, j * LANE : (j + 1) * LANE]
            pi = s_ref[before, width + j * LANE : width + (j + 1) * LANE]
            kr, ki = keep * re, keep * im
            fresh.append((sums[j][0] + (kr * pr + ki * pi), sums[j][1] + (ki * pr - kr * pi)))
        return tuple(fresh)

    zero = jnp.zeros((SUB, LANE), F32)
    return Scan(sg_ref, keep_adj_ref, par_ref, start, reverse, True, visit, tuple((zero, zero) for j in range(tiles)))


def put_lam(lg_ref, sums):
    lg_ref[...] = jnp.zeros(lg_ref.shape, F32)
    pack_rows(lg_ref, [
        jnp.sum(jnp.concatenate([part[k] for part in sums], axis=1), axis=0, keepdims=True) for k in range(2)
    ])


def add_drives(gb_ref, low, drive):
    gb = dot_tn(low, drive)
    rows = gb.shape[0]
    gb_ref[:rows, :] += gb[:, :rows]
    gb_ref[rows:, : rows // 2] += gb[: rows // 2, rows:]
    gb_ref[rows:, rows // 2 :] += gb[rows // 2 :, rows:]


def back_to_norm(layer, i, drive, sums, b_ref, vec_ref, mix_ref, lim_ref, u_ref, stat_ref, z_ref):
    at = rows_at(i)
    back = dot_nt(drive, b_ref[layer]) + vec_ref[2:3, :] * mix_ref[at, :].astype(F32)
    z = jnp.where(tile_mask(lim_ref, i), folded(back), 0.0)
    z_ref[at, :] = flat(z)
    return (sums[0] + jnp.sum(z, axis=0), sums[1] + jnp.sum(z * normed_tile(u_ref, stat_ref, i), axis=0))


def put_norm_sums(st_ref, sums):
    a, b = per_micro(sums[0])
    c, d = per_micro(sums[1])
    pack_rows(st_ref, (a, c, b, d))


def k_adjoint(layer, reverse, parts, *refs):
    carry, refs = take_carry(refs, parts)
    (sg_ref, s_ref, mix_ref, ml_ref, u_ref, stat_ref, lim_ref, vec_ref, par_ref,
     keep_adj_ref, kp_adj_ref, kd_adj_ref, keep_ref, b_ref, z_ref, gb_ref, lg_ref, st_ref, a_ref) = refs
    vec_ref, par_ref = of_layer(vec_ref, layer), of_layer(par_ref, layer)
    scan = adjoint_scan(reverse, carry, sg_ref, s_ref, par_ref, keep_adj_ref, kp_adj_ref, kd_adj_ref, keep_ref, a_ref)
    gb_ref[...] = jnp.zeros(gb_ref.shape, F32)
    zero = jnp.zeros(lim_ref.shape, F32)
    sums = (zero, zero)
    for i in scan.ahead():
        drive = a_ref[rows_at(i), :].astype(BF16)
        add_drives(gb_ref, ml_ref[rows_at(i), :], drive)
        sums = back_to_norm(layer, i, drive, sums, b_ref, vec_ref, mix_ref, lim_ref, u_ref, stat_ref, z_ref)
    put_lam(lg_ref, scan.extra)
    put_norm_sums(st_ref, sums)


def k_adjoint_last(layer, reverse, parts, *refs):
    carry, refs = take_carry(refs, parts)
    (sg_ref, s_ref, ml_ref, par_ref, keep_adj_ref, kp_adj_ref, kd_adj_ref, keep_ref,
     drive_ref, gb_ref, lg_ref, a_ref) = refs
    par_ref = of_layer(par_ref, layer)
    scan = adjoint_scan(reverse, carry, sg_ref, s_ref, par_ref, keep_adj_ref, kp_adj_ref, kd_adj_ref, keep_ref, a_ref)
    gb_ref[...] = jnp.zeros(gb_ref.shape, F32)
    for i in scan.ahead():
        drive = a_ref[rows_at(i), :].astype(BF16)
        drive_ref[rows_at(i), :] = drive
        add_drives(gb_ref, ml_ref[rows_at(i), :], drive)
    put_lam(lg_ref, scan.extra)


def k_back(layer, drive_ref, mix_ref, u_ref, stat_ref, lim_ref, vec_ref, b_ref, *refs):
    z_ref, st_ref = refs[-2:]
    vec_ref = of_layer(vec_ref, layer)
    zero = jnp.zeros(lim_ref.shape, F32)
    sums = (zero, zero)
    for i in range(u_ref.shape[0] // TILE):
        sums = back_to_norm(layer, i, drive_ref[rows_at(i), :], sums, b_ref, vec_ref, mix_ref, lim_ref, u_ref, stat_ref, z_ref)
    put_norm_sums(st_ref, sums)
    at = 16
    for ref in refs[:-2]:
        st_ref[at : at + ref.shape[0], :] = ref[...]
        at += ref.shape[0]


def k_output(st_ref, z_ref, grad_ref, u_ref, stat_ref, vec_ref, lim_ref, par_ref, stat1_ref, bn1_ref,
             run_mean_ref, run_var_ref,
             out_ref, gain_ref, shift_ref, skip_ref, bias_ref, rate_ref, rotation_ref, mean_ref, var_ref,
             bn_ref, lines_ref):
    vec0_ref = of_layer(vec_ref, 0)
    c1, c2 = norm_sums(st_ref, stat_ref, vec0_ref, bn_ref)

    def step(i, unused):
        extra = norm_backward(z_ref, u_ref, stat_ref, vec0_ref, c1, c2, tile_mask(lim_ref, i), i)
        put_lines(lines_ref, i, grad_ref[rows_at(i), :] + flat(extra))
        return unused

    lax.fori_loop(0, u_ref.shape[0] // TILE, step, 0, unroll=True)
    spread_out(lines_ref, out_ref)
    width, states = gain_ref.shape[1], rate_ref.shape[1]
    per, per_state = width // LANE, states // LANE

    def line(at, count):
        return jnp.concatenate([st_ref[at + j : at + j + 1, :] for j in range(count)], axis=1)

    for layer, (stats_ref, norms_ref) in enumerate(((stat_ref, bn_ref), (stat1_ref, bn1_ref))):
        row = slice(layer, layer + 1)
        at = 40 - 24 * layer
        bias_ref[row, :] = line(at, per)
        skip_ref[row, :] = line(at + per, per)
        product = line(at + 2 * per, per_state)
        grad_re, grad_im = line(at + 16, per_state), line(at + 16 + per_state, per_state)
        par = of_layer(par_ref, layer)
        lam_re, lam_im, norm_in, decay = par[0:1, :], par[1:2, :], par[6:7, :], par[7:8, :]
        rotation_ref[row, :] = lam_re * grad_im - lam_im * grad_re
        rate_ref[row, :] = decay * (
            product * jnp.exp(-2.0 * decay) / (norm_in * norm_in) - (lam_re * grad_re + lam_im * grad_im)
        )
        shift_ref[row, :] = norms_ref[0:1, :]
        gain_ref[row, :] = norms_ref[1:2, :]
        mean, var = run_mean_ref[row, :], run_var_ref[row, :]
        for micro in range(2):
            mean = (1.0 - momentum) * mean + momentum * stats_ref[24 + micro : 25 + micro, :]
            var = (1.0 - momentum) * var + momentum * stats_ref[26 + micro : 27 + micro, :]
        mean_ref[row, :] = mean
        var_ref[row, :] = var


def k_split(side, x_ref, give_ref):
    half = give_ref.shape[0]
    give_ref[...] = x_ref[pl.ds(pl.multiple_of((1 - side()) * half, SUB), half), :]


def k_fold(before, side, kept_ref, got_ref, give_ref, keep_ref):
    half = give_ref.shape[0]
    base = 0 if before is None else before() * got_ref.shape[0]
    mine = side()
    for ref, at in ((give_ref, (1 - mine) * half), (keep_ref, mine * half)):
        here = kept_ref[pl.ds(pl.multiple_of(base + at, SUB), half), :]
        ref[...] = here + got_ref[pl.ds(pl.multiple_of(at, SUB), half), :]


def k_copy(src_ref, dst_ref):
    dst_ref[...] = src_ref[...]


def k_add(*refs):
    total = refs[1][...]
    for ref in refs[2:-1]:
        total = total + ref[...]
    refs[-1][...] = refs[0][...] + total


def k_join(side, own_ref, got_ref, out_ref):
    half = own_ref.shape[0]
    mine = side()
    out_ref[pl.ds(pl.multiple_of(mine * half, SUB), half), :] = own_ref[...]
    out_ref[pl.ds(pl.multiple_of((1 - mine) * half, SUB), half), :] = got_ref[...]


def copy_all(pairs, sem_ref):
    copies = [pltpu.make_async_copy(src, dst, sem_ref.at[k]) for k, (src, dst) in enumerate(pairs)]
    for copy in copies:
        copy.start()
    for copy in copies:
        copy.wait()


def cut_to(layer, first, src_ref, outs):
    pairs = []
    for begin, end, place in outs:
        low, high = max(begin, first), min(end, first + src_ref.shape[0])
        if low < high:
            pairs.extend(place(src_ref, low - first, low - begin, high - low))
    return pairs


def rows_to(layer, ref):
    return lambda src, at, row, size: [(src.at[pl.ds(at, size), :], ref.at[layer, pl.ds(row, size), :])]


def map_places(layer, *refs):
    places, first = [], 0
    for ref in refs:
        places.append((first, first + ref.shape[1], rows_to(layer, ref)))
        first += ref.shape[1]
    return places


def drive_places(layer, b_ref):
    width = b_ref.shape[1]

    def left(src, at, row, size):
        return [(src.at[pl.ds(at, size), :], b_ref.at[layer, pl.ds(row, size), pl.ds(0, width)])]

    def right(src, at, row, size):
        part = width // 2
        return [
            (src.at[pl.ds(at, size), pl.ds(k * part, part)],
             b_ref.at[layer, pl.ds(k * part + row, size), pl.ds(width, part)])
            for k in range(2)
        ]

    return [(0, width, left), (width, width + width // 2, right)]


def k_place(side, layer, groups, *refs):
    token_ref, sem_ref = refs[-2:]
    outs = refs[-2 - sum(count for unused, count in groups) : -2]
    token_ref[...] = jnp.zeros(token_ref.shape, F32)
    for mine in range(2):
        @pl.when(side() == mine)
        def _():
            pairs, first = [], 0
            for k, (places, count) in enumerate(groups):
                where = places(layer, *outs[first : first + count])
                first += count
                for ref, at in zip(refs[2 * k : 2 * k + 2], (mine, 1 - mine)):
                    pairs.extend(cut_to(layer, at * ref.shape[0], ref, where))
            copy_all(pairs, sem_ref)


def place(order, layer, items, into=()):
    args = [array for large, unused, unused in items for array in (large.block, large.got)]
    shapes = [shape for unused, unused, more in items for shape in more]
    alias = {len(args) + k: k for k in range(len(into))}
    return list(call(
        "place", functools.partial(k_place, items[0][0].side(), layer, [(places, len(more)) for unused, places, more in items]),
        shapes + [shaped((SUB, LANE))], args + list(into), scratch=[pltpu.SemaphoreType.DMA((16,))], order=order,
        token=len(shapes), far=range(len(args), len(args) + len(into)), alias=alias, out_far=len(shapes),
    ))[: len(shapes)]


BOTH = ("batch", "tm")

ORDER = (
    ("AA",),
    ("B", "A", "e", "BA"),
    ("CECE",),
    ("DAB", "SDECBSADCS", "BEADCSBDEA", "SCBDECDBLC", "EDABCAECDB", "ED"),
)


def outer_bits():
    nb, nt = lax.axis_size("batch"), lax.axis_size("tm")
    return [("batch", 1 << k, nt << k) for k in range(nb.bit_length() - 1)]


def line_bits():
    return [("tm", 1 << k, 1 << k) for k in range(1, lax.axis_size("tm").bit_length() - 1)]


def swap(block, distance):
    total = lax.axis_size("batch") * lax.axis_size("tm")
    return lax.ppermute(block, BOTH, [(i, i ^ distance) for i in range(total)])


def swap_by_core(block, even, odd):
    total = lax.axis_size("batch") * lax.axis_size("tm")
    return lax.ppermute(block, BOTH, [(i, i ^ (odd if i & 1 else even)) for i in range(total)])


def sum_four(block, others, order=None):
    block, = call("add", k_add, [shaped(block.shape)], [block, others[0]], order=order, work=1)
    return call("add", k_add, [shaped(block.shape)], [block] + others[1:], order=order, work=1)[0]


def sum_over(block, bits):
    if len(bits) == 2:
        near, far = bits[0][2], bits[1][2]
        return sum_four(block, [swap(block, distance | 1) for distance in (near | far, far, near)])
    for unused, unused, distance in bits:
        block = block + swap(block, distance | 1)
    return block


def sums_of_all(block, fill):
    order = Order()
    got = swap(block, 1)
    order.token = fill()
    block, = call("add", k_add, [shaped(block.shape)], [block, got], order=order)
    return sum_over(sum_over(block, outer_bits()), line_bits())


def sums_in_order(block, order, between):
    for bits, start in zip(([("tm", 1, 0)], outer_bits(), line_bits()), between):
        if len(bits) == 2:
            near, far = bits[0][2], bits[1][2]
            got = [swap(block, distance | 1) for distance in (near | far, far, near)]
            start()
            block = sum_four(block, got, order)
        else:
            for k, bit in enumerate(bits):
                got = swap(block, bit[2] | 1)
                if k == 0:
                    start()
                block, = call("add", k_add, [shaped(block.shape)], [block, got], order=order)
    return block


def carries(e, kd, par, layer, reverse, conj, order=None):
    other = swap(e, 1)
    block, = call("combine", functools.partial(k_combine, layer, reverse, conj), [shaped(e.shape)], [e, other, kd, par],
                  order=order)
    bits = line_bits()
    if len(bits) == 2:
        near, far = bits[0][2], bits[1][2]
        last = swap(block, near | far | 1)
        others = [swap(block, distance | 1) for distance in (near, far)]
        last, = call("copy", k_copy, [shaped(block.shape)], [last], work=1)
        return [block] + others + [last, e, other]
    for unused, unused, distance in bits:
        block = jnp.concatenate((block, swap(block, distance | 1)), axis=0)
    return [block, e, other]


def bit_of(axis, bit):
    return lax.div(lax.axis_index(axis), bit) % 2


def plan(rows, line_first):
    outer, line = outer_bits(), line_bits()
    is_odd = functools.partial(bit_of, "tm", 1)
    steps = []
    for even, odd in zip(outer, outer[::-1]):
        def side(even=even, odd=odd):
            return jnp.where(is_odd() == 1, bit_of(odd[0], odd[1]), bit_of(even[0], even[1]))

        steps.append((side, functools.partial(swap_by_core, even=even[2], odd=odd[2])))
    along = [(functools.partial(bit_of, axis, bit), functools.partial(swap, distance=distance))
             for axis, bit, distance in line]
    steps = [(is_odd, lambda block: swap(block, 1))] + (along + steps if line_first else steps + along)
    most = 3 if line_first else 4
    cuts = 0
    while cuts < len(steps) and rows % (SUB << (cuts + 1)) == 0 and cuts < most:
        cuts += 1
    return steps[:cuts], [exchange for unused, exchange in steps[cuts:]]


class Large:
    def __init__(self, order, block, line_first=False):
        self.order = order
        self.rows, self.width = block.shape
        self.cuts, self.whole = plan(self.rows, line_first)
        self.block = block
        self.at = 0
        self.got = None

    def call(self, name, body, outs):
        args = [self.block] if self.got is None else [self.block, self.got]
        return call(name, body, outs, args, order=self.order)

    def send(self):
        cuts, at = self.cuts, self.at
        count = len(cuts)
        if at < count:
            side, exchange = cuts[at]
            half = shaped((self.rows >> (at + 1), self.width))
            if at == 0:
                give, = self.call("split", functools.partial(k_split, side), [half])
            else:
                before = cuts[0][0] if at == 1 else None
                give, self.block = self.call("fold", functools.partial(k_fold, before, side), [half, half])
        else:
            if at <= count + len(self.whole):
                give, = self.call("add", k_add, [shaped(self.got.shape)])
            else:
                give, = self.call("join", functools.partial(k_join, self.side()), [self.doubled()])
            self.block = give
            exchange = (self.whole + [step[1] for step in cuts[::-1]])[at - count]
        self.got = exchange(give)
        self.at += 1

    def side(self):
        return self.cuts[2 * len(self.cuts) + len(self.whole) - self.at][0]

    def doubled(self):
        return shaped((2 * self.block.shape[0], self.width))

    def left(self):
        return 2 * len(self.cuts) + len(self.whole) - self.at


class Steps:
    def __init__(self, order):
        self.order = order
        self.larges, self.other, self.out, self.shapes, self.come = {}, {}, {}, {}, set()

    def add(self, name, block, line_first=False):
        self.larges[name] = Large(self.order, block, line_first)

    def run(self, items):
        for item in items:
            if item in self.other:
                self.other[item]()
            elif self.larges[item].left():
                self.larges[item].send()
            else:
                self.put(item)

    def put(self, item):
        group = [names for names in ("AB", "CE", "D") if item in names][0]
        self.come.add(item)
        if group in self.out or not self.come.issuperset(group):
            return
        for name in group:
            while self.larges[name].left():
                self.larges[name].send()
        if group == "AB":
            self.out[group] = place(self.order, 1, [
                (self.larges["A"], map_places, self.shapes["A"]), (self.larges["B"], drive_places, self.shapes["B"]),
            ])
            return
        if "AB" not in self.out:
            self.put("A")
            self.put("B")
        w_out, c_out, b_out = self.out["AB"]
        into = [b_out] if group == "D" else [c_out, w_out]
        self.out[group] = place(self.order, 0, [
            (self.larges[name], drive_places if name == "D" else map_places, [shaped(out.shape)])
            for name, out in zip(group, into)
        ], into)

    def placed(self, item):
        for name in "CED":
            self.put(name)
        return {"C": self.out["CE"][0], "E": self.out["CE"][1], "D": self.out["D"][0]}[item]


def small_sum(order, block):
    for distance in [1] + [bit[2] | 1 for bit in outer_bits() + line_bits()]:
        got = swap(block, distance)
        yield None
        block, = call("add", k_add, [shaped(block.shape)], [block, got], order=order)
    yield block


def local(tokens, starts, lengths, cotangent, norm_gain, norm_shift, b_proj, log_rate, rotation, c_proj, skip_gain,
          w_gate, gate_bias, run_mean, run_var):
    rows, length, width = tokens.shape
    states = log_rate.shape[1]
    count = rows * length
    n = lax.axis_size("tm")
    chips = n // 2
    parts = 4 if chips == 4 else 1

    big = lambda w, dtype=F32: shaped((count, w), dtype)
    ends = shaped((SUB, 2 * states))
    kept = shaped((count + SUB, 2 * states))
    small = shaped((16, LANE))
    lines = pltpu.VMEM((width // LANE, count, LANE), F32)
    rows_low, states_low_rows = pltpu.VMEM((count, width), BF16), pltpu.VMEM((count, 2 * states), BF16)
    everyone = pltpu.VMEM((chips, SUB, 2 * states), F32)
    keeps = shaped((count + SUB, LANE))
    vector, state_vector = shaped((2, width)), shaped((2, states))

    u0, st, lim = call("enter", k_input, [big(width), shaped((24, LANE)), shaped((SUB, width), jnp.int32)],
                       [lengths, tokens], scratch=[lines], scalars=1)
    keep_shapes = [keeps, shaped((2 * SUB, LANE)), shaped((n + 1, SUB, LANE))]
    made = []

    def prepare():
        made.extend(call(
            "prepare", k_prepare, keep_shapes + [shaped((2 * SUB, states)), shaped((2 * SUB, width))],
            [starts, log_rate, rotation, norm_gain, norm_shift, skip_gain, gate_bias], scalars=1,
        ))
        return made[1]

    st = sums_of_all(st, prepare)
    keep_f, kp_f, kd_f, par, vec = made
    d0, ml0, m0, stat0, e = call(
        "drive0", functools.partial(k_drive_first, 0, False),
        [big(2 * states), big(width, BF16), big(width), shaped((32, width)), ends],
        [st, u0, lim, vec, par, b_proj, keep_f, kp_f],
    )
    s0, al0, sig0, q0, slope0, u1, st = call(
        "finish0", functools.partial(k_finish_first, 0, parts),
        [kept, big(width, BF16), big(width), big(width), big(width), big(width), small],
        carries(e, kd_f, par, 0, False, False)
        + [d0, u0, m0, lim, vec, par, keep_f, kp_f, kd_f, c_proj, w_gate],
        scratch=[everyone],
    )
    after_first = Order()
    after_first.token = st
    backward = []

    def keep():
        backward.extend(call(
            "keep", functools.partial(k_keep, True), keep_shapes, [starts], scalars=1, order=after_first, token=1,
        ))
        return backward[1]

    st = sums_of_all(st, keep)
    keep_r, kp_r, kd_r = backward
    d1, ml1, m1, stat1, e = call(
        "drive1", functools.partial(k_drive, 1, True),
        [big(2 * states), big(width, BF16), big(width), shaped((32, width)), ends],
        [st, stat0, u1, lim, vec, par, b_proj, keep_r, kp_r],
    )
    grads = [shaped((width + 2 * states, width)), small, ends]
    after_second = Order()
    after_second.token = e
    cot32, = call("cotangent", spread_in, [big(width)], [cotangent], scratch=[lines], order=after_second)
    out32, s1, mix1, sg1, wc1, sums1, e = call(
        "middle", functools.partial(k_middle, 1, parts),
        [shaped((width // LANE, count, LANE)), kept, big(width, BF16), big(2 * states)] + grads,
        carries(e, kd_r, par, 1, True, False, after_second)
        + [d1, u1, m1, lim, vec, par, keep_r, kp_r, kd_r, keep_f, kp_f, c_proj, w_gate, cot32],
        scratch=[rows_low, rows_low, states_low_rows, everyone],
    )
    order = Order()
    order.token = e
    steps = Steps(order)
    steps.add("A", wc1)
    got = carries(e, kd_f, par, 1, False, True, order)
    steps.run(ORDER[0][0])
    adjoint = [big(width), shaped((2 * states, width)), shaped((8, LANE))]
    z1, gb1, lg1, st = call(
        "adjoint1", functools.partial(k_adjoint, 1, False, parts), adjoint + [small],
        got + [sg1, s1, mix1, ml1, u1, stat1, lim, vec, par, keep_f, kp_f, kd_f, keep_r, b_proj],
        scratch=[pltpu.VMEM((count, 2 * states), F32), everyone], order=order, token=3,
    )
    steps.add("B", gb1)
    emitted = []

    def emit():
        emitted.extend(
            call("emit", k_emit, [shaped(tokens.shape, BF16), shaped((SUB, LANE))], [out32], results=1, order=order, token=1)
        )

    steps.other["e"] = emit
    st = sums_in_order(st, order, [functools.partial(steps.run, items) for items in ORDER[1][:3]])
    steps.run(ORDER[1][3])
    g0, mix0, sg0, gw0, gc0, sums0, e, bn1 = call(
        "lower", functools.partial(k_lower, 0),
        [big(width), big(width, BF16), big(2 * states), shaped((width, width)), shaped((2 * states, width)), small, ends,
         shaped((SUB, width))],
        [st, z1, cot32, u1, stat1, lim, s0, al0, sig0, q0, slope0, m0, vec, par,
         c_proj, w_gate, keep_r, kp_r],
        scratch=[rows_low, states_low_rows], order=order, token=6,
    )
    steps.add("E", gw0, True)
    steps.add("C", gc0)
    got = carries(e, kd_r, par, 0, True, True, order)
    steps.run(ORDER[2][0])
    drive0, gb0, lg0 = call(
        "adjoint0", functools.partial(k_adjoint_last, 0, True, parts), [big(2 * states, BF16)] + adjoint[1:],
        got + [sg0, s0, ml0, par, keep_r, kp_r, kd_r, keep_f],
        scratch=[pltpu.VMEM((count, 2 * states), F32), everyone], order=order, token=2,
    )
    steps.add("D", gb0)
    steps.shapes = {
        "A": [shaped((2, width, width)), shaped((2, 2 * states, width))],
        "B": [shaped((2, width, 2 * states))],
    }
    steps.run(ORDER[3][0])
    z0, st = call(
        "back", functools.partial(k_back, 0), [big(width), shaped((64, LANE))],
        [drive0, mix0, u0, stat0, lim, vec, b_proj, sums1, lg1, sums0, lg0], order=order, token=1,
    )
    small_steps = small_sum(order, st)
    last = []

    def small():
        last.extend(item for item in [next(small_steps, None)] if item is not None)

    def leave():
        while not last:
            small()
        last.extend(call(
            "leave", k_output,
            [shaped(tokens.shape), vector, vector, vector, vector, state_vector, state_vector, vector, vector,
             shaped((SUB, width))],
            [last[0], z0, g0, u0, stat0, vec, lim, par, stat1, bn1, run_mean, run_var],
            scratch=[lines], results=9, order=order, token=9,
        ))

    steps.other.update({"S": small, "L": leave})
    steps.run("".join(ORDER[3][1:]))
    (tokens_grad, grad_gain, grad_shift, grad_skip, grad_bias, grad_rate, grad_rotation, new_mean, new_var) = last[1:10]
    output, grad_w, grad_c, grad_b = emitted[0], steps.placed("E"), steps.placed("C"), steps.placed("D")
    return (output, tokens_grad, grad_gain, grad_shift, grad_b, grad_rate, grad_rotation, grad_c, grad_skip, grad_w,
            grad_bias, new_mean, new_var)


def solution(mesh):
    tokens_spec = P("batch", "tm", None)
    return jax.shard_map(
        local,
        mesh=mesh,
        in_specs=(tokens_spec, P("batch", None), P("batch"), tokens_spec) + (P(),) * 11,
        out_specs=(tokens_spec, tokens_spec) + (P(),) * 11,
        check_vma=False,
    )
```
